128 devices in a mesh: seq: 64 (over x_lo, z, y, core), samp: 2 (over x_hi).
Axes of the slice: x: 4 (x_hi: 2, x_lo: 2; x = x_hi * 2 + x_lo), y: 4, z: 4, core: 2. Of those that a mesh axis runs over, the one named last changes fastest.
Arguments:
- trunk: bfloat16 [2, 16384, 768], P('samp', 'seq'), may hold values from -6 to 6
- conv_weight: bfloat16 [3, 3, 768, 768], replicated, may hold values from -0.125 to 0.125
- head_weight: bfloat16 [768, 2688], replicated, may hold values from -0.21875 to 0.21875
- targets: int32 [2, 16384, 2688], P('samp', 'seq'), may hold values from 0 to 8
- error_mask: int32 [2, 16384], P('samp', 'seq'), may hold values 0 or 1
- upweight: int32 [2, 16384], P('samp', 'seq'), may hold values from 1 to 16, as said below
Outputs:
- loss: float32 [], replicated
- grad_conv: float32 [3, 2304, 768], P(None, 'seq', 'samp')
- grad_head: float32 [768, 2688], P('seq', 'samp')
- trunk_input_gradient: bfloat16 [2, 16384, 768], P('samp', 'seq')
The draws below stay inside these ranges and needn't reach their ends.
Inputs may be any that keep to these rules, and one draw needn't show every extreme that they name: upweight is 1 at the first bin of each window and 16 at the last; at bin p it is at most 1 + (15 p) // 16383.
All inputs are finite; a program needn't handle non-finite values. No bound on the sum of `error_mask` on one device may be relied on, other than what follows from the above.
Results may differ from the reference program's by a relative error of at most 0.015.
Values may be sent and summed in bfloat16 or wider, within the bound.
No kernel may reach another device: no remote copies, remote signals or barrier semaphores. Data moves between devices by JAX's collectives and lax.ppermute only.
A program may use at most 192 MiB of HBM per device.

```python
import jax
import jax.numpy as jnp
from jax import lax

C = 768
OUTPUT_TRACKS = 2688
LAYERS = 3
BASE_DILATION = 64
LENGTH = 16384
BATCH = 2


def draw_upweight(key, part):
    places = jnp.arange(LENGTH, dtype=jnp.int32)
    ceiling = 2 + 15 * places // max(LENGTH - 1, 1)
    drawn = jax.random.randint(key, (BATCH, LENGTH), 1, ceiling[None, :])
    drawn = jnp.where(places[None, :] == LENGTH - 1, 16, drawn)
    return drawn.astype(jnp.int32)


def touch_ends(entries, key, smallest, high):
    place = [jax.random.randint(jax.random.fold_in(key, axis), (), 0, length) for axis, length in enumerate(entries.shape)]
    longest = entries.shape.index(max(entries.shape))
    next_to = place[:longest] + [(place[longest] + 1) % entries.shape[longest]] + place[longest + 1:]
    return entries.at[tuple(place)].set(smallest).at[tuple(next_to)].set(high)


def block_levels(key, shape, shards, least, largest):
    def one(dim, blocks):
        steps = jax.random.uniform(jax.random.fold_in(jax.random.fold_in(key, 6), dim), (blocks,), jnp.float32, least / len(shards), largest / len(shards))
        return jnp.repeat(jnp.exp(steps), shape[dim] // blocks).reshape((-1,) + (1,) * (len(shape) - dim - 1))

    gain = one(*shards[0])
    for cut in shards[1:]:
        gain = gain * one(*cut)
    return gain


def bell_draw(rng, shape, deviation, limit, cuts=(), kind=jnp.bfloat16):
    gain = block_levels(rng, shape, cuts, -0.22, 0.18) if cuts else 1.0
    result = jax.random.normal(rng, shape, jnp.float32) * deviation * gain
    return jnp.minimum(jnp.maximum(result, -limit), limit).astype(kind)


def setup_inputs(seed: int = 0) -> dict:
    streams_of = jax.random.split(jax.random.key(seed), 7)
    trunk = bell_draw(streams_of[0], (BATCH, LENGTH, C), 1.0, 6.0, ((0, 2), (1, 64)))
    conv_weight = bell_draw(streams_of[1], (LAYERS, 3, C, C), (3 * C) ** -0.5, 0.125)
    head_weight = bell_draw(streams_of[2], (C, OUTPUT_TRACKS), C ** -0.5, 0.21875)
    targets = touch_ends(jax.random.randint(streams_of[3], (BATCH, LENGTH, OUTPUT_TRACKS), 0, 9), jax.random.fold_in(streams_of[3], 1), 0, 8).astype(jnp.int32)
    error_mask = touch_ends((jax.random.randint(streams_of[4], (BATCH, LENGTH), 0, 2) < 1).astype(jnp.int32), jax.random.fold_in(streams_of[4], 1), 0, 1)
    upweight = draw_upweight(jax.random.fold_in(streams_of[6], 71), 0)
    return {"trunk": trunk, "conv_weight": conv_weight, "head_weight": head_weight, "targets": targets, "error_mask": error_mask, "upweight": upweight}


def smooth(values):
    return jax.nn.gelu(values, approximate=True)

def shifted(values, offset):
    length_all = values.shape[1]
    margin = abs(offset)
    padded = jnp.pad(values, ((0, 0), (margin, margin), (0, 0)))
    return padded[:, margin + offset:margin + offset + length_all]

def reference(trunk, conv_weight, head_weight, targets, error_mask, upweight):
    bin_weight = jnp.where(error_mask == 1, upweight, 1).astype(jnp.float32)
    weight_sum = jnp.sum(bin_weight)
    factor = BATCH * LENGTH / weight_sum
    stream = trunk
    stored = []
    activations = []
    for layer_number in range(LAYERS):
        dilation_spread = BASE_DILATION * 2 ** layer_number
        activated = smooth(stream.astype(jnp.float32)).astype(jnp.bfloat16)
        conv_out = jnp.zeros((BATCH * LENGTH, C), jnp.float32)
        for tap_num in range(3):
            moved = shifted(activated, (tap_num - 1) * dilation_spread).reshape(-1, C)
            conv_out = conv_out + jnp.dot(moved, conv_weight[layer_number, tap_num], preferred_element_type=jnp.float32)
        stored.append(stream)
        activations.append(activated)
        stream = (stream.astype(jnp.float32) + conv_out.reshape(stream.shape)).astype(jnp.bfloat16)

    def head_part(inputs):
        window_rows, window_counts, window_weight = inputs
        logits = jnp.dot(window_rows, head_weight, preferred_element_type=jnp.float32)
        predicted = jax.nn.softplus(logits)
        slope = jax.nn.sigmoid(logits)
        counts = window_counts.astype(jnp.float32)
        partial_loss = jnp.sum(window_weight[:, None] * (predicted - counts * jnp.log(predicted)))
        logit_grad = (factor * window_weight[:, None] * (1.0 - counts / predicted) * slope).astype(jnp.bfloat16)
        head_grad = jnp.dot(window_rows.T, logit_grad, preferred_element_type=jnp.float32)
        back_grad = jnp.dot(logit_grad, head_weight.T, preferred_element_type=jnp.float32)
        return (partial_loss, back_grad, head_grad)
    loss_parts, stream_grad, head_grads = lax.map(head_part, (stream, targets, bin_weight))
    loss = jnp.sum(loss_parts) / (OUTPUT_TRACKS * weight_sum)
    grad_head = lax.optimization_barrier(jnp.sum(head_grads, axis=0))
    kernel_grads = [None] * LAYERS
    for layer_number in reversed(range(LAYERS)):
        dilation_spread = BASE_DILATION * 2 ** layer_number
        grad_bf = stream_grad.astype(jnp.bfloat16)
        grad_flat = grad_bf.reshape(-1, C)
        pieces = []
        act_grad = jnp.zeros((BATCH * LENGTH, C), jnp.float32)
        for tap_num in range(3):
            offset = (tap_num - 1) * dilation_spread
            moved = shifted(activations[layer_number], offset).reshape(-1, C)
            pieces.append(jnp.dot(moved.T, grad_flat, preferred_element_type=jnp.float32))
            back_moved = shifted(grad_bf, -offset).reshape(-1, C)
            act_grad = act_grad + jnp.dot(back_moved, conv_weight[layer_number, tap_num].T, preferred_element_type=jnp.float32)
        kernel_grads[layer_number] = jnp.concatenate(pieces, axis=0)
        residual_float32 = stored[layer_number].astype(jnp.float32)
        pullback = jax.vjp(smooth, residual_float32)[1]
        stream_grad = stream_grad + pullback(act_grad.reshape(residual_float32.shape))[0]
    grad_conv = jnp.stack(kernel_grads, axis=0)
    return (loss, grad_conv, grad_head, stream_grad.astype(jnp.bfloat16))
```

```python
import jax
import jax.numpy as jnp
from jax import lax
from jax.sharding import PartitionSpec as P

OUTPUT_TRACKS = 2688
LAYERS = 3
BASE_DILATION = 64
AXES = ("seq", "samp")
BF = jnp.bfloat16
F32 = jnp.float32


def perm_of(target):
    pairs = []
    for xl in range(2):
        for z in range(4):
            for y in range(4):
                for c in range(2):
                    for xh in range(2):
                        goal = target(xl, z, y, c, xh)
                        pairs.append((lin(xl, z, y, c, xh), lin(*goal)))
    return pairs


def lin(xl, z, y, c, xh):
    return (((xl * 4 + z) * 4 + y) * 2 + c) * 2 + xh


CORE = perm_of(lambda xl, z, y, c, xh: (xl, z, y, 1 - c, xh))


def along_y(k):
    return perm_of(lambda xl, z, y, c, xh: (xl, z, (y + k) % 4, c, xh))


def along_z(k):
    return perm_of(lambda xl, z, y, c, xh: (xl, (z + k) % 4, y, c, xh))


def last_hop(dx, m):
    return perm_of(lambda xl, z, y, c, xh: (xl ^ dx, z, y, xh ^ m, c))


def send(v, pairs):
    return lax.ppermute(v, AXES, pairs)


def extended(shard, width):
    devices, length = (lax.axis_size("seq"), shard.shape[0])
    up = [(i, (i + 1) % devices) for i in range(devices - 1)]
    down = [(j, i) for i, j in up]
    before = lax.ppermute(shard[length - width :], "seq", up)
    after = lax.ppermute(shard[:width], "seq", down)
    return jnp.concatenate([before, shard, after], axis=0)


def smooth(values):
    return jax.nn.gelu(values, approximate=True)


def ring_sum(blocks, place, route):
    total = lax.dynamic_index_in_dim(blocks, place, 1, keepdims=False).astype(F32)
    for k in (1, 3, 2):
        mine = lax.dynamic_index_in_dim(blocks, (place + k) % 4, 1, keepdims=False)
        total = total + send(mine, route(k)).astype(F32)
    return total.astype(BF)


def reduce_rows(part, z_first, y, z):
    rows = part.shape[0] // 32
    lanes = part.shape[1]
    if z_first:
        part = ring_sum(
            part.reshape(2, 4, 4 * rows, lanes), z, along_z
        )
        part = ring_sum(part.reshape(2, 4, rows, lanes), y, along_y)
    else:
        part = ring_sum(part.reshape(8, 4, rows, lanes), y, along_y)
        part = ring_sum(part.reshape(2, 4, rows, lanes), z, along_z)
    return part


def last_sum(blocks, xl, c, xh):
    total = None
    for dx in range(2):
        for m in range(2):
            mine = lax.dynamic_index_in_dim(blocks, xl ^ dx, 0, keepdims=False)
            mine = lax.dynamic_index_in_dim(mine, xh ^ m, 0, keepdims=False)
            got = send(mine, last_hop(dx, m)).astype(F32)
            total = got if total is None else total + got
    return total


def per_device(trunk, conv_weight, head_weight, targets, error_mask, upweight):
    _, positions, channels = trunk.shape
    seq = lax.axis_index("seq")
    xh = lax.axis_index("samp")
    c = seq % 2
    y = (seq // 2) % 4
    z = (seq // 8) % 4
    xl = seq // 32
    bins_all = positions * lax.axis_size("seq") * lax.axis_size("samp")
    bin_weight = jnp.where(error_mask == 1, upweight, 1).astype(F32).reshape(positions, 1)
    weight_part = jnp.sum(bin_weight)
    stream = trunk[0]
    stored = []
    padded_acts = []
    for layer in range(LAYERS):
        d = BASE_DILATION * 2**layer
        activated = smooth(stream.astype(F32)).astype(BF)
        padded = extended(activated, d)
        conv_out = jnp.zeros((positions, channels), F32)
        for tap in range(3):
            conv_out = conv_out + jnp.dot(
                padded[tap * d : tap * d + positions],
                conv_weight[layer, tap],
                preferred_element_type=F32,
            )
        stored.append(stream)
        padded_acts.append(padded)
        stream = (stream.astype(F32) + conv_out).astype(BF)
    logits = jnp.dot(stream, head_weight, preferred_element_type=F32)
    predicted = jax.nn.softplus(logits)
    slope = jax.nn.sigmoid(logits)
    counts = targets[0].astype(F32)
    partial_loss = jnp.sum(bin_weight * (predicted - counts * jnp.log(predicted)))
    logit_grad = (bin_weight * (1.0 - counts / predicted) * slope).astype(BF)
    head_grad = jnp.dot(stream.T, logit_grad, preferred_element_type=F32)
    def core_sum(grad, width, starts):
        grad = grad.astype(BF)
        mine = jnp.where(c == 0, grad[:, :width], grad[:, starts : starts + width])
        other = jnp.where(c == 1, grad[:, :width], grad[:, starts : starts + width])
        return (mine.astype(F32) + send(other, CORE).astype(F32)).astype(BF)

    head_half = core_sum(head_grad, 1408, 1280)
    scal = jnp.stack([weight_part, partial_loss])
    scal = scal + send(scal, CORE)

    def scalar_ring(s, route):
        return s + send(s, route(1)) + send(s, route(2)) + send(s, route(3))

    scal = scalar_ring(scal, along_y)
    scal = scalar_ring(scal, along_z)
    scal = scal + send(scal, perm_of(lambda a, b, e, f, g: (1 - a, b, e, f, g)))
    scal = scal + send(scal, perm_of(lambda a, b, e, f, g: (a, b, e, f, 1 - g)))
    head_sum = reduce_rows(head_half, False, y, z)
    stream_grad = jnp.dot(logit_grad, head_weight.T, preferred_element_type=F32)
    conv_sums = [None] * LAYERS
    for layer in reversed(range(LAYERS)):
        d = BASE_DILATION * 2**layer
        grad_bf = stream_grad.astype(BF)
        padded_grad = extended(grad_bf, d)
        padded = padded_acts[layer]
        pieces = []
        act_grad = jnp.zeros((positions, channels), F32)
        for tap in range(3):
            pieces.append(
                jnp.dot(
                    padded[tap * d : tap * d + positions].T, grad_bf, preferred_element_type=F32
                )
            )
            act_grad = act_grad + jnp.dot(
                padded_grad[(2 - tap) * d : (2 - tap) * d + positions],
                conv_weight[layer, tap].T,
                preferred_element_type=F32,
            )
        conv_half = core_sum(jnp.concatenate(pieces, axis=0), 384, 384)
        conv_sums[layer] = reduce_rows(conv_half, layer != 1, y, z)
        residual = stored[layer].astype(F32)
        pullback = jax.vjp(smooth, residual)[1]
        stream_grad = stream_grad + pullback(act_grad)[0]
    head_total = last_sum(head_sum.reshape(2, 2, 12, 1408), xl, c, xh)
    conv_total = last_sum(
        jnp.stack(conv_sums).reshape(3, 2, 2, 36, 384).transpose(1, 2, 0, 3, 4), xl, c, xh
    )
    head_total = jnp.where(xh == 0, head_total[:, :1344], head_total[:, 64:])
    factor = bins_all / scal[0]
    loss = scal[1] / (OUTPUT_TRACKS * scal[0])
    return (
        loss,
        conv_total * factor,
        head_total * factor,
        (stream_grad * factor).astype(BF)[None],
    )


def solution(mesh):
    return jax.shard_map(
        per_device,
        mesh=mesh,
        in_specs=(
            P("samp", "seq", None),
            P(),
            P(),
            P("samp", "seq", None),
            P("samp", "seq"),
            P("samp", "seq"),
        ),
        out_specs=(P(), P(None, "seq", "samp"), P("seq", "samp"), P("samp", "seq", None)),
        check_vma=False,
    )
```

```python
import jax
import jax.numpy as jnp
from jax import lax
from jax.sharding import PartitionSpec as P

OUTPUT_TRACKS = 2688
LAYERS = 3
BASE_DILATION = 64
AXES = ("seq", "samp")
BF = jnp.bfloat16
F32 = jnp.float32


def perm_of(target):
    pairs = []
    for xl in range(2):
        for z in range(4):
            for y in range(4):
                for c in range(2):
                    for xh in range(2):
                        goal = target(xl, z, y, c, xh)
                        pairs.append((lin(xl, z, y, c, xh), lin(*goal)))
    return pairs


def lin(xl, z, y, c, xh):
    return (((xl * 4 + z) * 4 + y) * 2 + c) * 2 + xh


CORE = perm_of(lambda xl, z, y, c, xh: (xl, z, y, 1 - c, xh))
ALONG_Y = [perm_of(lambda xl, z, y, c, xh, k=k: (xl, z, y ^ k, c, xh)) for k in range(4)]
ALONG_Z = [perm_of(lambda xl, z, y, c, xh, k=k: (xl, z ^ k, y, c, xh)) for k in range(4)]


def last_hop(dx, m):
    return perm_of(lambda xl, z, y, c, xh: (xl ^ dx, z, y, xh ^ m, c))


def send(v, pairs):
    return lax.ppermute(v, AXES, pairs)


def extended(shard, width):
    devices, length = (lax.axis_size("seq"), shard.shape[0])
    up = [(i, (i + 1) % devices) for i in range(devices - 1)]
    down = [(j, i) for i, j in up]
    before = lax.ppermute(shard[length - width :], "seq", up)
    after = lax.ppermute(shard[:width], "seq", down)
    return jnp.concatenate([before, shard, after], axis=0)


def smooth(values):
    return jax.nn.gelu(values, approximate=True)


def pick(blocks, place):
    return lax.dynamic_index_in_dim(blocks, place, 1, keepdims=False)


def add_bf(a, b):
    return (a.astype(F32) + b.astype(F32)).astype(BF)


def ring_direct(blocks, place, route):
    total = pick(blocks, place).astype(F32)
    got = [send(pick(blocks, place ^ k), route[k]) for k in (1, 3, 2)]
    for g in got:
        total = total + g.astype(F32)
    return total.astype(BF)


def ring_halve(blocks, place, route, wrap_first):
    n, _, rows, lanes = blocks.shape
    hi = place // 2
    if wrap_first:
        pairs = blocks.reshape(n, 2, 2, rows, lanes)
        keep, away = pick(pairs, hi), pick(pairs, 1 - hi)
        keep = add_bf(keep, send(away, route[3]))
        lo = place % 2
        return add_bf(pick(keep, lo), send(pick(keep, 1 - lo), route[1]))
    outer = jnp.stack([blocks[:, 0], blocks[:, 3]], axis=1)
    inner = blocks[:, 1:3]
    is_outer = (place == 0) | (place == 3)
    keep = jnp.where(is_outer, outer, inner)
    away = jnp.where(is_outer, inner, outer)
    keep = add_bf(keep, send(away, route[1]))
    return add_bf(pick(keep, hi), send(pick(keep, 1 - hi), route[3]))


def reduce_rows(part, z_first, how, y, z):
    rows = part.shape[0] // 32
    lanes = part.shape[1]
    if how == "direct":
        ring = ring_direct
    else:
        ring = lambda b, p, r: ring_halve(b, p, r, how == "wrap")
    if z_first:
        part = ring(part.reshape(2, 4, 4 * rows, lanes), z, ALONG_Z)
        part = ring(part.reshape(2, 4, rows, lanes), y, ALONG_Y)
    else:
        part = ring(part.reshape(8, 4, rows, lanes), y, ALONG_Y)
        part = ring(part.reshape(2, 4, rows, lanes), z, ALONG_Z)
    return part


def last_sum(blocks, xl, c, xh):
    total = None
    for dx in range(2):
        for m in range(2):
            mine = lax.dynamic_index_in_dim(blocks, xl ^ dx, 0, keepdims=False)
            mine = lax.dynamic_index_in_dim(mine, xh ^ m, 0, keepdims=False)
            got = send(mine, last_hop(dx, m)).astype(F32)
            total = got if total is None else total + got
    return total


def per_device(trunk, conv_weight, head_weight, targets, error_mask, upweight):
    _, positions, channels = trunk.shape
    seq = lax.axis_index("seq")
    xh = lax.axis_index("samp")
    c = seq % 2
    y = (seq // 2) % 4
    z = (seq // 8) % 4
    xl = seq // 32
    bins_all = positions * lax.axis_size("seq") * lax.axis_size("samp")
    bin_weight = jnp.where(error_mask == 1, upweight, 1).astype(F32).reshape(positions, 1)
    weight_part = jnp.sum(bin_weight)
    stream = trunk[0]
    stored = []
    padded_acts = []
    for layer in range(LAYERS):
        d = BASE_DILATION * 2**layer
        activated = smooth(stream.astype(F32)).astype(BF)
        padded = extended(activated, d)
        conv_out = jnp.zeros((positions, channels), F32)
        for tap in range(3):
            conv_out = conv_out + jnp.dot(
                padded[tap * d : tap * d + positions],
                conv_weight[layer, tap],
                preferred_element_type=F32,
            )
        stored.append(stream)
        padded_acts.append(padded)
        stream = (stream.astype(F32) + conv_out).astype(BF)
    logits = jnp.dot(stream, head_weight, preferred_element_type=F32)
    predicted = jax.nn.softplus(logits)
    slope = jax.nn.sigmoid(logits)
    counts = targets[0].astype(F32)
    partial_loss = jnp.sum(bin_weight * (predicted - counts * jnp.log(predicted)))
    logit_grad = (bin_weight * (1.0 - counts / predicted) * slope).astype(BF)
    lanes = lax.broadcasted_iota(jnp.int32, (1, 1408), 1)
    spare = lanes - 1344 * (1 - c)

    def with_scalars(v, scalars):
        for n, s in enumerate(scalars):
            inside = (spare >= 32 * n) & (spare < 32 * n + 32)
            v = jnp.where(inside, s * (1.0 + (spare - 32 * n).astype(F32) / 32), v)
        return v

    def halves(v, width):
        low, high = v[:, :width], v[:, v.shape[1] - width :]
        return jnp.where(c == 0, low, high), jnp.where(c == 0, high, low)

    def pair_dot(a, b, far_a, far_b):
        return jnp.dot(a.T, b, preferred_element_type=F32) + jnp.dot(
            far_a.T, far_b, preferred_element_type=F32
        )

    near, far = halves(logit_grad, 1408)
    scal = jnp.stack([weight_part, partial_loss])
    scal = scal + send(scal, CORE)
    head_half = pair_dot(stream, near, send(stream, CORE), send(far, CORE))
    head_half = with_scalars(head_half, (scal[0], scal[1])).astype(BF)
    head_sum = reduce_rows(head_half, False, "near", y, z)
    stream_grad = jnp.dot(logit_grad, head_weight.T, preferred_element_type=F32)
    conv_sums = [None] * LAYERS
    for layer in reversed(range(LAYERS)):
        d = BASE_DILATION * 2**layer
        grad_bf = stream_grad.astype(BF)
        padded_grad = extended(grad_bf, d)
        padded = padded_acts[layer]
        far_padded = send(padded, CORE)
        near, far = halves(grad_bf, 384)
        far = send(far, CORE)
        pieces = []
        act_grad = jnp.zeros((positions, channels), F32)
        for tap in range(3):
            rows = slice(tap * d, tap * d + positions)
            pieces.append(pair_dot(padded[rows], near, far_padded[rows], far).astype(BF))
            act_grad = act_grad + jnp.dot(
                padded_grad[(2 - tap) * d : (2 - tap) * d + positions],
                conv_weight[layer, tap].T,
                preferred_element_type=F32,
            )
        conv_sums[layer] = reduce_rows(
            jnp.concatenate(pieces, axis=0), layer != 1, ("direct", "wrap", "near")[layer], y, z
        )
        residual = stored[layer].astype(F32)
        pullback = jax.vjp(smooth, residual)[1]
        stream_grad = stream_grad + pullback(act_grad)[0]
    head_rows = jnp.pad(head_sum.reshape(2, 2, 12, 1408), ((0, 0), (0, 0), (0, 0), (0, 128)))
    message = jnp.concatenate(
        [jnp.pad(v.reshape(2, 2, 36, 384), ((0, 0), (0, 0), (0, 4), (0, 0))) for v in conv_sums]
        + [head_rows[..., 384 * k : 384 * k + 384] for k in range(4)],
        axis=2,
    )
    total = last_sum(message, xl, c, xh)
    conv_total = jnp.stack([total[40 * k : 40 * k + 36] for k in range(LAYERS)])
    head_total = jnp.concatenate([total[120 + 12 * k : 132 + 12 * k] for k in range(4)], axis=1)
    low = head_total[:, :1344]
    high = head_total[:, 64:1408]
    row = head_total[0]
    found = jnp.where(xh == 0, row[1344:1408], row[:64])
    weight_sum = jnp.sum(found[:32]) / 47.5
    loss_sum = jnp.sum(found[32:]) / 47.5
    factor = bins_all / weight_sum
    loss = loss_sum / (OUTPUT_TRACKS * weight_sum)
    return (
        loss,
        conv_total * factor,
        jnp.where(xh == 0, low, high) * factor,
        (stream_grad * factor).astype(BF)[None],
    )


def solution(mesh):
    return jax.shard_map(
        per_device,
        mesh=mesh,
        in_specs=(
            P("samp", "seq", None),
            P(),
            P(),
            P("samp", "seq", None),
            P("samp", "seq"),
            P("samp", "seq"),
        ),
        out_specs=(P(), P(None, "seq", "samp"), P("seq", "samp"), P("samp", "seq", None)),
        check_vma=False,
    )
```

```python
import jax
import jax.numpy as jnp
from jax import lax
from jax.sharding import PartitionSpec as P

OUTPUT_TRACKS = 2688
LAYERS = 3
BASE_DILATION = 64
AXES = ("seq", "samp")
BF = jnp.bfloat16
F32 = jnp.float32


def perm_of(target):
    pairs = []
    for xl in range(2):
        for z in range(4):
            for y in range(4):
                for c in range(2):
                    for xh in range(2):
                        goal = target(xl, z, y, c, xh)
                        pairs.append((lin(xl, z, y, c, xh), lin(*goal)))
    return pairs


def lin(xl, z, y, c, xh):
    return (((xl * 4 + z) * 4 + y) * 2 + c) * 2 + xh


CORE = perm_of(lambda xl, z, y, c, xh: (xl, z, y, 1 - c, xh))
NEXT_CHIP = [(a * 2 + xh, (a + 1) * 2 + xh) for a in range(1, 63, 2) for xh in range(2)]
NEXT_CHIP = NEXT_CHIP + [(b, a) for a, b in NEXT_CHIP]
ALONG_Y = [perm_of(lambda xl, z, y, c, xh, k=k: (xl, z, y ^ k, c, xh)) for k in range(4)]
ALONG_Z = [perm_of(lambda xl, z, y, c, xh, k=k: (xl, z ^ k, y, c, xh)) for k in range(4)]


def last_hop(dx, m):
    return perm_of(lambda xl, z, y, c, xh: (xl ^ dx, z, y, xh ^ m, c))


def send(v, pairs):
    return lax.ppermute(v, AXES, pairs)


def edges(shard, width, c):
    first, last = shard[:width], shard[shard.shape[0] - width :]
    if width == shard.shape[0]:
        inner = outer = shard
    else:
        inner = jnp.where(c == 0, last, first)
        outer = jnp.where(c == 0, first, last)
    outer = send(outer, NEXT_CHIP)
    inner = send(inner, CORE)
    return jnp.where(c == 0, outer, inner), jnp.where(c == 0, inner, outer)


def extended(shard, width, c):
    before, after = edges(shard, width, c)
    return jnp.concatenate([before, shard, after], axis=0)


def after_all(value, *others):
    return lax.optimization_barrier((value,) + others)[0]


def smooth(values):
    return jax.nn.gelu(values, approximate=True)


def pick(blocks, place):
    return lax.dynamic_index_in_dim(blocks, place, 1, keepdims=False)


def add_bf(a, b):
    return (a.astype(F32) + b.astype(F32)).astype(BF)


def ring_direct(blocks, place, route):
    total = pick(blocks, place).astype(F32)
    got = [send(pick(blocks, place ^ k), route[k]) for k in (1, 3, 2)]
    for g in got:
        total = total + g.astype(F32)
    return total.astype(BF)


def ring_halve(blocks, place, route, wrap_first):
    n, _, rows, lanes = blocks.shape
    hi = place // 2
    if wrap_first:
        pairs = blocks.reshape(n, 2, 2, rows, lanes)
        keep, away = pick(pairs, hi), pick(pairs, 1 - hi)
        keep = add_bf(keep, send(away, route[3]))
        lo = place % 2
        return add_bf(pick(keep, lo), send(pick(keep, 1 - lo), route[1]))
    outer = jnp.stack([blocks[:, 0], blocks[:, 3]], axis=1)
    inner = blocks[:, 1:3]
    is_outer = (place == 0) | (place == 3)
    keep = jnp.where(is_outer, outer, inner)
    away = jnp.where(is_outer, inner, outer)
    keep = add_bf(keep, send(away, route[1]))
    return add_bf(pick(keep, hi), send(pick(keep, 1 - hi), route[3]))


def reduce_rows(part, z_first, how, y, z):
    rows = part.shape[0] // 32
    lanes = part.shape[1]
    if how == "direct":
        ring = ring_direct
    else:
        ring = lambda b, p, r: ring_halve(b, p, r, how == "wrap")
    if z_first:
        part = ring(part.reshape(2, 4, 4 * rows, lanes), z, ALONG_Z)
        part = ring(part.reshape(2, 4, rows, lanes), y, ALONG_Y)
    else:
        part = ring(part.reshape(8, 4, rows, lanes), y, ALONG_Y)
        part = ring(part.reshape(2, 4, rows, lanes), z, ALONG_Z)
    return part


def last_sum(blocks, xl, c, xh):
    total = None
    for dx in range(2):
        for m in range(2):
            mine = lax.dynamic_index_in_dim(blocks, xl ^ dx, 0, keepdims=False)
            mine = lax.dynamic_index_in_dim(mine, xh ^ m, 0, keepdims=False)
            got = send(mine, last_hop(dx, m)).astype(F32)
            total = got if total is None else total + got
    return total


def per_device(trunk, conv_weight, head_weight, targets, error_mask, upweight):
    _, positions, channels = trunk.shape
    seq = lax.axis_index("seq")
    xh = lax.axis_index("samp")
    c = seq % 2
    y = (seq // 2) % 4
    z = (seq // 8) % 4
    xl = seq // 32
    bins_all = positions * lax.axis_size("seq") * lax.axis_size("samp")
    bin_weight = jnp.where(error_mask == 1, upweight, 1).astype(F32).reshape(positions, 1)
    weight_part = jnp.sum(bin_weight)
    stream = trunk[0]
    stored = []
    padded_acts = []
    for layer in range(LAYERS):
        d = BASE_DILATION * 2**layer
        activated = smooth(stream.astype(F32)).astype(BF)
        padded = extended(activated, d, c)
        conv_out = jnp.zeros((positions, channels), F32)
        for tap in range(3):
            conv_out = conv_out + jnp.dot(
                padded[tap * d : tap * d + positions],
                conv_weight[layer, tap],
                preferred_element_type=F32,
            )
        stored.append(stream)
        padded_acts.append(padded)
        stream = (stream.astype(F32) + conv_out).astype(BF)
    logits = jnp.dot(stream, head_weight, preferred_element_type=F32)
    predicted = jax.nn.softplus(logits)
    slope = jax.nn.sigmoid(logits)
    counts = targets[0].astype(F32)
    partial_loss = jnp.sum(bin_weight * (predicted - counts * jnp.log(predicted)))
    logit_grad = (bin_weight * (1.0 - counts / predicted) * slope).astype(BF)
    lanes = lax.broadcasted_iota(jnp.int32, (1, 1408), 1)
    spare = lanes - 1344 * (1 - c)

    def with_scalars(v, scalars):
        for n, s in enumerate(scalars):
            inside = (spare >= 32 * n) & (spare < 32 * n + 32)
            v = jnp.where(inside, s * (1.0 + (spare - 32 * n).astype(F32) / 32), v)
        return v

    def halves(v, width):
        low, high = v[:, :width], v[:, v.shape[1] - width :]
        return jnp.where(c == 0, low, high), jnp.where(c == 0, high, low)

    def pair_dot(a, b, far_a, far_b):
        return jnp.dot(a.T, b, preferred_element_type=F32) + jnp.dot(
            far_a.T, far_b, preferred_element_type=F32
        )

    near, far = halves(logit_grad, 1408)
    scal = jnp.stack([weight_part, partial_loss])
    scal = scal + send(scal, CORE)
    head_half = pair_dot(stream, near, send(stream, CORE), send(far, CORE))
    head_half = with_scalars(head_half, (scal[0], scal[1])).astype(BF)
    head_sum = reduce_rows(head_half, False, "near", y, z)
    stream_grad = jnp.dot(logit_grad, head_weight.T, preferred_element_type=F32)
    conv_sums = [None] * LAYERS
    ready = [head_half]
    for layer in reversed(range(LAYERS)):
        d = BASE_DILATION * 2**layer
        grad_bf = stream_grad.astype(BF)
        before, after = edges(grad_bf, d, c)
        padded = padded_acts[layer]
        far_padded = send(padded, CORE)
        near, far = halves(grad_bf, 384)
        far = send(far, CORE)
        pieces = []
        for tap in range(3):
            rows = slice(tap * d, tap * d + positions)
            pieces.append(pair_dot(padded[rows], near, far_padded[rows], far).astype(BF))
        conv_half = jnp.concatenate(pieces, axis=0)
        conv_sums[layer] = reduce_rows(
            conv_half, layer != 1, ("direct", "wrap", "near")[layer], y, z
        )
        ready.append(conv_half)
        before = after_all(before, *ready)
        padded_grad = jnp.concatenate([before, grad_bf, after], axis=0)
        act_grad = jnp.zeros((positions, channels), F32)
        for tap in range(3):
            act_grad = act_grad + jnp.dot(
                padded_grad[(2 - tap) * d : (2 - tap) * d + positions],
                conv_weight[layer, tap].T,
                preferred_element_type=F32,
            )
        residual = stored[layer].astype(F32)
        pullback = jax.vjp(smooth, residual)[1]
        stream_grad = stream_grad + pullback(act_grad)[0]
    head_rows = jnp.pad(head_sum.reshape(2, 2, 12, 1408), ((0, 0), (0, 0), (0, 0), (0, 128)))
    message = jnp.concatenate(
        [jnp.pad(v.reshape(2, 2, 36, 384), ((0, 0), (0, 0), (0, 4), (0, 0))) for v in conv_sums]
        + [head_rows[..., 384 * k : 384 * k + 384] for k in range(4)],
        axis=2,
    )
    total = last_sum(message, xl, c, xh)
    conv_total = jnp.stack([total[40 * k : 40 * k + 36] for k in range(LAYERS)])
    head_total = jnp.concatenate([total[120 + 12 * k : 132 + 12 * k] for k in range(4)], axis=1)
    low = head_total[:, :1344]
    high = head_total[:, 64:1408]
    row = head_total[0]
    found = jnp.where(xh == 0, row[1344:1408], row[:64])
    weight_sum = jnp.sum(found[:32]) / 47.5
    loss_sum = jnp.sum(found[32:]) / 47.5
    factor = bins_all / weight_sum
    loss = loss_sum / (OUTPUT_TRACKS * weight_sum)
    return (
        loss,
        conv_total * factor,
        jnp.where(xh == 0, low, high) * factor,
        (stream_grad * factor).astype(BF)[None],
    )


def solution(mesh):
    return jax.shard_map(
        per_device,
        mesh=mesh,
        in_specs=(
            P("samp", "seq", None),
            P(),
            P(),
            P("samp", "seq", None),
            P("samp", "seq"),
            P("samp", "seq"),
        ),
        out_specs=(P(), P(None, "seq", "samp"), P("seq", "samp"), P("samp", "seq", None)),
        check_vma=False,
    )
```

```python
import jax
import jax.numpy as jnp
from jax import lax
from jax.sharding import Mesh
from jax.sharding import PartitionSpec as P

OUTPUT_TRACKS = 2688
LAYERS = 3
BASE_DILATION = 64
AXES = ("xl", "z", "y", "c", "xh")
BF = jnp.bfloat16
F32 = jnp.float32


def perm_of(target):
    pairs = []
    for xl in range(2):
        for z in range(4):
            for y in range(4):
                for c in range(2):
                    for xh in range(2):
                        goal = target(xl, z, y, c, xh)
                        pairs.append((lin(xl, z, y, c, xh), lin(*goal)))
    return pairs


def lin(xl, z, y, c, xh):
    return (((xl * 4 + z) * 4 + y) * 2 + c) * 2 + xh


CORE = perm_of(lambda xl, z, y, c, xh: (xl, z, y, 1 - c, xh))
NEXT_CHIP = [(a * 2 + xh, (a + 1) * 2 + xh) for a in range(1, 63, 2) for xh in range(2)]
NEXT_CHIP = NEXT_CHIP + [(b, a) for a, b in NEXT_CHIP]
ALONG_X = perm_of(lambda xl, z, y, c, xh: (1 - xl, z, y, c, xh))


def last_hop(dx, m):
    return perm_of(lambda xl, z, y, c, xh: (xl ^ dx, z, y, xh ^ m, c))


def send(v, pairs):
    return lax.ppermute(v, AXES, pairs)


def edges(shard, width, c):
    first, last = shard[:width], shard[shard.shape[0] - width :]
    if width == shard.shape[0]:
        inner = outer = shard
    else:
        inner = jnp.where(c == 0, last, first)
        outer = jnp.where(c == 0, first, last)
    outer = send(outer, NEXT_CHIP)
    inner = send(inner, CORE)
    return jnp.where(c == 0, outer, inner), jnp.where(c == 0, inner, outer)


def extended(shard, width, c):
    before, after = edges(shard, width, c)
    return jnp.concatenate([before, shard, after], axis=0)


def after_all(value, *others):
    return lax.optimization_barrier((value,) + others)[0]


def smooth(values):
    return jax.nn.gelu(values, approximate=True)


def pick(blocks, place):
    return lax.dynamic_index_in_dim(blocks, place, 0, keepdims=False)


def swap_xl(part, xl):
    halves = part.reshape(2, part.shape[0] // 2, part.shape[1])
    got = send(pick(halves, 1 - xl), ALONG_X)
    return (pick(halves, xl).astype(F32) + got.astype(F32)).astype(BF)


def plane_sum(blocks):
    got = lax.all_to_all(blocks, ("z", "y"), 0, 0, tiled=True)
    return jnp.sum(got.astype(F32), axis=0).astype(BF)


def last_sum(block, extra, xl, xh, at):
    near = jnp.concatenate([block[:, :at], pick(extra, xl), block[:, at:]], axis=1)
    rest = pick(extra, 1 - xl)
    total = sum(send(pick(near, xh ^ m), last_hop(0, m)).astype(F32) for m in range(2))
    more = sum(send(pick(rest, xh ^ m), last_hop(1, m)).astype(F32) for m in range(2))
    return jnp.concatenate(
        [total[:at], total[at : at + more.shape[0]] + more, total[at + more.shape[0] :]], axis=0
    )


def per_device(trunk, conv_weight, head_weight, targets, error_mask, upweight):
    _, positions, channels = trunk.shape
    xl, z, y, c, xh = (lax.axis_index(axis) for axis in AXES)
    bins_all = positions * lax.axis_size(AXES)
    bin_weight = jnp.where(error_mask == 1, upweight, 1).astype(F32).reshape(positions, 1)
    weight_part = jnp.sum(bin_weight)
    first, last = (xl + z + y + c == 0), (xl == 1) & (z == 3) & (y == 3) & (c == 1)

    def inside(v, width):
        row = lax.broadcasted_iota(jnp.int32, (v.shape[0], 1), 0)
        out = (first & (row < width)) | (last & (row >= v.shape[0] - width))
        return jnp.where(out, jnp.zeros_like(v), v)

    def conv(rows, weights, d, count):
        total = jnp.dot(rows[d : d + count], weights[1], preferred_element_type=F32)
        total = total + jnp.dot(rows[:count], weights[0], preferred_element_type=F32)
        return total + jnp.dot(
            rows[2 * d : 2 * d + count], weights[2], preferred_element_type=F32
        )

    def conv_back(rows, weights, d, count):
        total = jnp.dot(rows[d : d + count], weights[1].T, preferred_element_type=F32)
        total = total + jnp.dot(
            rows[2 * d : 2 * d + count], weights[0].T, preferred_element_type=F32
        )
        return total + jnp.dot(rows[:count], weights[2].T, preferred_element_type=F32)

    def activate(v):
        return smooth(v.astype(F32)).astype(BF)

    def through(v, grad):
        return jax.vjp(smooth, v.astype(F32))[1](grad)[0]

    wide0 = extended(trunk[0], 192, c)
    act0 = activate(wide0)
    wide1 = (wide0[64:576].astype(F32) + conv(act0, conv_weight[0], 64, 512)).astype(BF)
    wide1 = inside(wide1, 128)
    act1 = activate(wide1)
    stream2 = (wide1[128:384].astype(F32) + conv(act1, conv_weight[1], 128, 256)).astype(BF)
    act2 = extended(activate(stream2), 256, c)
    stream = (stream2.astype(F32) + conv(act2, conv_weight[2], 256, 256)).astype(BF)
    padded_acts = [act0[128:512], act1, act2]
    logits = jnp.dot(stream, head_weight, preferred_element_type=F32)
    predicted = jax.nn.softplus(logits)
    slope = jax.nn.sigmoid(logits)
    counts = targets[0].astype(F32)
    partial_loss = jnp.sum(bin_weight * (predicted - counts * jnp.log(predicted)))
    logit_grad = (bin_weight * (1.0 - counts / predicted) * slope).astype(BF)
    lanes = lax.broadcasted_iota(jnp.int32, (1, 1408), 1)
    spare = lanes - 1344 * (1 - c)

    def with_scalars(v, scalars):
        for n, s in enumerate(scalars):
            inside = (spare >= 32 * n) & (spare < 32 * n + 32)
            v = jnp.where(inside, s * (1.0 + (spare - 32 * n).astype(F32) / 32), v)
        return v

    def halves(v, width):
        low, high = v[:, :width], v[:, v.shape[1] - width :]
        return jnp.where(c == 0, low, high), jnp.where(c == 0, high, low)

    def pair_dot(a, b, far_a, far_b):
        return jnp.dot(a.T, b, preferred_element_type=F32) + jnp.dot(
            far_a.T, far_b, preferred_element_type=F32
        )

    near, far = halves(logit_grad, 1408)
    scal = jnp.stack([weight_part, partial_loss])
    scal = scal + send(scal, CORE)
    head_half = pair_dot(stream, near, send(stream, CORE), send(far, CORE))
    head_half = with_scalars(head_half, (scal[0], scal[1])).astype(BF)
    head_sum = swap_xl(head_half, xl)
    g_top = jnp.dot(logit_grad, head_weight.T, preferred_element_type=F32)

    def conv_grad(layer, grad_bf):
        d = BASE_DILATION * 2**layer
        padded = padded_acts[layer]
        far_padded = send(padded, CORE)
        near, far = halves(grad_bf, 384)
        far = send(far, CORE)
        return jnp.concatenate(
            [
                pair_dot(padded[rows], near, far_padded[rows], far).astype(BF)
                for rows in (slice(tap * d, tap * d + positions) for tap in range(3))
            ],
            axis=0,
        )

    gb2 = g_top.astype(BF)
    before, after = edges(gb2, 256, c)
    half2 = conv_grad(2, gb2)
    sum2 = swap_xl(half2, xl)
    before = after_all(before, head_half, half2)
    wide = jnp.concatenate([before, gb2, after], axis=0)
    g2 = g_top + through(stream2, conv_back(wide, conv_weight[2], 256, 256))
    gb1 = g2.astype(BF)
    before, after = edges(gb1, 192, c)
    half1 = conv_grad(1, gb1)
    sum1 = swap_xl(half1, xl)
    head_plane = plane_sum(head_sum.reshape(16, 24, 1408))
    plane2 = plane_sum(sum2.reshape(16, 72, 384))
    before = after_all(before, half1, head_sum, sum2)
    wide = jnp.concatenate([before, gb1, after], axis=0)
    g_in = jnp.concatenate([before[128:].astype(F32), g2, after[:64].astype(F32)], axis=0)
    g1 = g_in + through(wide1[64:448], conv_back(wide, conv_weight[1], 128, 384))
    gb0 = inside(g1.astype(BF), 64)
    half0 = conv_grad(0, gb0[64:320])
    plane0 = plane_sum(half0.reshape(2, 16, 72, 384).transpose(1, 0, 2, 3))
    plane1 = plane_sum(sum1.reshape(16, 72, 384))
    gb0 = after_all(gb0, half0)
    g0 = g1[64:320] + through(trunk[0], conv_back(gb0, conv_weight[0], 64, 256))

    def by_core(v, rows):
        v = v.reshape(v.shape[:-2] + (2, rows, 384))
        return jnp.pad(v, ((0, 0),) * (v.ndim - 2) + ((0, 4), (0, 0)))

    head_rows = jnp.pad(head_plane.reshape(2, 12, 1408), ((0, 0), (0, 0), (0, 128)))
    message = jnp.concatenate(
        [by_core(plane1, 36), by_core(plane2, 36)]
        + [head_rows[..., 384 * k : 384 * k + 384] for k in range(4)],
        axis=1,
    )
    total = last_sum(message, by_core(plane0, 36), xl, xh, 0)
    conv_total = jnp.stack([total[40 * k : 40 * k + 36] for k in range(LAYERS)])
    head_total = jnp.concatenate([total[120 + 12 * k : 132 + 12 * k] for k in range(4)], axis=1)
    low = head_total[:, :1344]
    high = head_total[:, 64:1408]
    row = head_total[0]
    found = jnp.where(xh == 0, row[1344:1408], row[:64])
    weight_sum = jnp.sum(found[:32]) / 47.5
    loss_sum = jnp.sum(found[32:]) / 47.5
    factor = bins_all / weight_sum
    loss = loss_sum / (OUTPUT_TRACKS * weight_sum)
    return (
        loss,
        conv_total * factor,
        jnp.where(xh == 0, low, high) * factor,
        (g0 * factor).astype(BF)[None],
    )


def solution(mesh):
    parts = Mesh(mesh.devices.reshape(2, 4, 4, 2, 2), ("xl", "z", "y", "c", "xh"))
    seq = ("xl", "z", "y", "c")
    return jax.shard_map(
        per_device,
        mesh=parts,
        in_specs=(
            P("xh", seq, None),
            P(),
            P(),
            P("xh", seq, None),
            P("xh", seq),
            P("xh", seq),
        ),
        out_specs=(P(), P(None, seq, "xh"), P(seq, "xh"), P("xh", seq, None)),
        check_vma=False,
    )
```

```python
import jax
import jax.numpy as jnp
from jax import lax
from jax.sharding import Mesh
from jax.sharding import PartitionSpec as P

OUTPUT_TRACKS = 2688
LAYERS = 3
BASE_DILATION = 64
AXES = ("xl", "z", "y", "c", "xh")
BF = jnp.bfloat16
F32 = jnp.float32


def perm_of(target):
    pairs = []
    for xl in range(2):
        for z in range(4):
            for y in range(4):
                for c in range(2):
                    for xh in range(2):
                        goal = target(xl, z, y, c, xh)
                        pairs.append((lin(xl, z, y, c, xh), lin(*goal)))
    return pairs


def lin(xl, z, y, c, xh):
    return (((xl * 4 + z) * 4 + y) * 2 + c) * 2 + xh


CORE = perm_of(lambda xl, z, y, c, xh: (xl, z, y, 1 - c, xh))
NEXT_CHIP = [(a * 2 + xh, (a + 1) * 2 + xh) for a in range(1, 63, 2) for xh in range(2)]
NEXT_CHIP = NEXT_CHIP + [(b, a) for a, b in NEXT_CHIP]
ALONG_X = perm_of(lambda xl, z, y, c, xh: (1 - xl, z, y, c, xh))
ALONG_Y = [perm_of(lambda xl, z, y, c, xh, k=k: (xl, z, y ^ k, c, xh)) for k in range(4)]
ALONG_Z = [perm_of(lambda xl, z, y, c, xh, k=k: (xl, z ^ k, y, c, xh)) for k in range(4)]


def last_hop(dx, m):
    return perm_of(lambda xl, z, y, c, xh: (xl ^ dx, z, y, xh ^ m, c))


def send(v, pairs):
    return lax.ppermute(v, AXES, pairs)


def edges(shard, width, c):
    first, last = shard[:width], shard[shard.shape[0] - width :]
    if width == shard.shape[0]:
        inner = outer = shard
    else:
        inner = jnp.where(c == 0, last, first)
        outer = jnp.where(c == 0, first, last)
    outer = send(outer, NEXT_CHIP)
    inner = send(inner, CORE)
    return jnp.where(c == 0, outer, inner), jnp.where(c == 0, inner, outer)


def extended(shard, width, c):
    before, after = edges(shard, width, c)
    return jnp.concatenate([before, shard, after], axis=0)


def smooth(values):
    return jax.nn.gelu(values, approximate=True)


def pick(blocks, place, axis=0):
    return lax.dynamic_index_in_dim(blocks, place, axis, keepdims=False)


def give(part, bit, route, outer=1):
    rows, lanes = part.shape
    halves = part.reshape(outer, 2, rows // (2 * outer), lanes)
    return send(pick(halves, 1 - bit, 1), route)


def take(part, got, bit):
    rows, lanes = part.shape
    outer = got.shape[0]
    halves = part.reshape(outer, 2, rows // (2 * outer), lanes)
    total = pick(halves, bit, 1).astype(F32) + got.astype(F32)
    return total.astype(BF).reshape(rows // 2, lanes)


def halve(part, bit, route, outer=1):
    return take(part, give(part, bit, route, outer), bit)


def plane_sum(blocks):
    got = lax.all_to_all(blocks, ("z", "y"), 0, 0, tiled=True)
    return jnp.sum(got.astype(F32), axis=0).astype(BF)


def last_sum(near, rest):
    total = sum(send(near, last_hop(0, m)).astype(F32) for m in range(2))
    more = sum(send(rest, last_hop(1, m)).astype(F32) for m in range(2))
    count = rest.shape[0]
    return total[:count] + more, total[count:]


def per_device(trunk, conv_weight, head_weight, targets, error_mask, upweight):
    _, positions, channels = trunk.shape
    xl, z, y, c, xh = (lax.axis_index(axis) for axis in AXES)
    bins_all = positions * lax.axis_size(AXES)
    bin_weight = jnp.where(error_mask == 1, upweight, 1).astype(F32).reshape(positions, 1)
    weight_part = jnp.sum(bin_weight)
    first, last = (xl + z + y + c == 0), (xl == 1) & (z == 3) & (y == 3) & (c == 1)

    def inside(v, width):
        row = lax.broadcasted_iota(jnp.int32, (v.shape[0], 1), 0)
        out = (first & (row < width)) | (last & (row >= v.shape[0] - width))
        return jnp.where(out, jnp.zeros_like(v), v)

    def conv(rows, weights, d, count):
        total = jnp.dot(rows[d : d + count], weights[1], preferred_element_type=F32)
        total = total + jnp.dot(rows[:count], weights[0], preferred_element_type=F32)
        return total + jnp.dot(
            rows[2 * d : 2 * d + count], weights[2], preferred_element_type=F32
        )

    def conv_back(rows, weights, d, count):
        total = jnp.dot(rows[d : d + count], weights[1].T, preferred_element_type=F32)
        total = total + jnp.dot(
            rows[2 * d : 2 * d + count], weights[0].T, preferred_element_type=F32
        )
        return total + jnp.dot(rows[:count], weights[2].T, preferred_element_type=F32)

    def activate(v):
        return smooth(v.astype(F32)).astype(BF)

    def through(v, grad):
        return jax.vjp(smooth, v.astype(F32))[1](grad)[0]

    wide0 = extended(trunk[0], 192, c)
    act0 = activate(wide0)
    wide1 = (wide0[64:576].astype(F32) + conv(act0, conv_weight[0], 64, 512)).astype(BF)
    wide1 = inside(wide1, 128)
    act1 = activate(wide1)
    stream2 = (wide1[128:384].astype(F32) + conv(act1, conv_weight[1], 128, 256)).astype(BF)
    act2 = activate(stream2)
    before, after = edges(act2, 256, c)
    far_acts = [send(act0[128:512], CORE), send(act1, CORE)]
    before, far_acts[0], far_acts[1] = lax.optimization_barrier((before, *far_acts))
    act2 = jnp.concatenate([before, act2, after], axis=0)
    far_acts.append(send(act2, CORE))
    stream = (stream2.astype(F32) + conv(act2, conv_weight[2], 256, 256)).astype(BF)
    padded_acts = [act0[128:512], act1, act2]
    logits = jnp.dot(stream, head_weight, preferred_element_type=F32)
    predicted = jax.nn.softplus(logits)
    slope = jax.nn.sigmoid(logits)
    counts = targets[0].astype(F32)
    partial_loss = jnp.sum(bin_weight * (predicted - counts * jnp.log(predicted)))
    logit_grad = (bin_weight * (1.0 - counts / predicted) * slope).astype(BF)
    logit_grad, far_acts[2] = lax.optimization_barrier((logit_grad, far_acts[2]))
    lanes = lax.broadcasted_iota(jnp.int32, (1, 1408), 1)
    spare = lanes - 1344 * (1 - c)

    def with_scalars(v, scalars):
        for n, s in enumerate(scalars):
            inside = (spare >= 32 * n) & (spare < 32 * n + 32)
            v = jnp.where(inside, s * (1.0 + (spare - 32 * n).astype(F32) / 32), v)
        return v

    def halves(v, width):
        low, high = v[:, :width], v[:, v.shape[1] - width :]
        return jnp.where(c == 0, low, high), jnp.where(c == 0, high, low)

    def pair_dot(a, b, far_a, far_b):
        return jnp.dot(a.T, b, preferred_element_type=F32) + jnp.dot(
            far_a.T, far_b, preferred_element_type=F32
        )

    near, far = halves(logit_grad, 1408)
    scal = jnp.stack([weight_part, partial_loss])
    scal = scal + send(scal, CORE)
    head_half = pair_dot(stream, near, send(stream, CORE), send(far, CORE))
    head_half = with_scalars(head_half, (scal[0], scal[1])).astype(BF)
    head_got = give(head_half, xl, ALONG_X)
    g_top = jnp.dot(logit_grad, head_weight.T, preferred_element_type=F32)

    def conv_grad(layer, grad_bf):
        d = BASE_DILATION * 2**layer
        padded = padded_acts[layer]
        far_padded = far_acts[layer]
        near, far = halves(grad_bf, 384)
        far = send(far, CORE)
        return jnp.concatenate(
            [
                pair_dot(padded[rows], near, far_padded[rows], far).astype(BF)
                for rows in (slice(tap * d, tap * d + positions) for tap in range(3))
            ],
            axis=0,
        )

    gb2 = g_top.astype(BF)
    before, after = edges(gb2, 256, c)
    half2 = conv_grad(2, gb2)
    got2 = give(half2, z // 2, ALONG_Z[3], 2)
    before, head_half, half2 = lax.optimization_barrier((before, head_half, half2))
    wide = jnp.concatenate([before, gb2, after], axis=0)
    g2 = g_top + through(stream2, conv_back(wide, conv_weight[2], 256, 256))
    gb1 = g2.astype(BF)
    before, after = edges(gb1, 192, c)
    half1 = conv_grad(1, gb1)
    head_x = take(head_half, head_got, xl)
    part2_z = take(half2, got2, z // 2)
    half1, head_x, part2_z = lax.optimization_barrier((half1, head_x, part2_z))
    got1 = give(half1, xl, ALONG_X)
    head_got = give(head_x, z // 2, ALONG_Z[3])
    got2 = give(part2_z, z % 2, ALONG_Z[1], 2)
    before, half1, head_x, part2_z = lax.optimization_barrier((before, half1, head_x, part2_z))
    wide = jnp.concatenate([before, gb1, after], axis=0)
    g_in = jnp.concatenate([before[128:].astype(F32), g2, after[:64].astype(F32)], axis=0)
    g1 = g_in + through(wide1[64:448], conv_back(wide, conv_weight[1], 128, 384))
    gb0 = inside(g1.astype(BF), 64)
    head_z = take(head_x, head_got, z // 2)
    part2_zz = take(part2_z, got2, z % 2)
    head_got = give(head_z, z % 2, ALONG_Z[1])
    got2 = give(part2_zz, xl, ALONG_X)
    gb0, head_z, part2_zz = lax.optimization_barrier((gb0, head_z, part2_zz))
    half0 = conv_grad(0, gb0[64:320])
    plane0 = plane_sum(half0.reshape(2, 16, 72, 384).transpose(1, 0, 2, 3))
    head_zz = take(head_z, head_got, z % 2)
    part2 = take(part2_zz, got2, xl)
    part1_x = take(half1, got1, xl)
    part1_z = halve(part1_x, z // 2, ALONG_Z[3])
    part1 = halve(part1_z, z % 2, ALONG_Z[1])
    g0 = g1[64:320] + through(trunk[0], conv_back(gb0, conv_weight[0], 64, 256))
    g0 = lax.optimization_barrier(g0)
    head_rows = jnp.pad(head_zz, ((0, 0), (0, 128))).reshape(4, 24, 1536)
    early = jnp.concatenate(
        [part1.reshape(4, 72, 384), part2.reshape(4, 72, 384)]
        + [head_rows[..., 384 * k : 384 * k + 384] for k in range(4)],
        axis=1,
    ).reshape(960, 384)
    early = halve(early, y // 2, ALONG_Y[3])
    early = halve(early, y % 2, ALONG_Y[1])
    near = jnp.concatenate([pick(plane0, xl), early], axis=0)
    part0, early = last_sum(near, pick(plane0, 1 - xl))

    def own(v):
        half = v.shape[0] // 2
        return jnp.where(c == 0, v[:half], v[half:])

    conv_total = jnp.stack([own(part0), own(early[:72]), own(early[72:144])])
    head_total = jnp.concatenate(
        [own(early[144 + 24 * k : 168 + 24 * k]) for k in range(4)], axis=1
    )
    low = head_total[:, :1344]
    high = head_total[:, 64:1408]
    row = head_total[0]
    found = jnp.where(xh == 0, row[1344:1408], row[:64])
    weight_sum = jnp.sum(found[:32]) / 47.5
    loss_sum = jnp.sum(found[32:]) / 47.5
    factor = bins_all / weight_sum
    loss = loss_sum / (OUTPUT_TRACKS * weight_sum)
    return (
        loss,
        conv_total * factor,
        jnp.where(xh == 0, low, high) * factor,
        (g0 * factor).astype(BF)[None],
    )


def solution(mesh):
    parts = Mesh(mesh.devices.reshape(2, 4, 4, 2, 2), ("xl", "z", "y", "c", "xh"))
    seq = ("xl", "z", "y", "c")
    return jax.shard_map(
        per_device,
        mesh=parts,
        in_specs=(
            P("xh", seq, None),
            P(),
            P(),
            P("xh", seq, None),
            P("xh", seq),
            P("xh", seq),
        ),
        out_specs=(P(), P(None, seq, "xh"), P(seq, "xh"), P("xh", seq, None)),
        check_vma=False,
    )
```

```python
import jax
import jax.numpy as jnp
from jax import lax
from jax.sharding import Mesh
from jax.sharding import PartitionSpec as P

OUTPUT_TRACKS = 2688
LAYERS = 3
BASE_DILATION = 64
AXES = ("xl", "z", "y", "c", "xh")
BF = jnp.bfloat16
F32 = jnp.float32


def perm_of(target):
    pairs = []
    for xl in range(2):
        for z in range(4):
            for y in range(4):
                for c in range(2):
                    for xh in range(2):
                        goal = target(xl, z, y, c, xh)
                        pairs.append((lin(xl, z, y, c, xh), lin(*goal)))
    return pairs


def lin(xl, z, y, c, xh):
    return (((xl * 4 + z) * 4 + y) * 2 + c) * 2 + xh


CORE = perm_of(lambda xl, z, y, c, xh: (xl, z, y, 1 - c, xh))
NEXT_CHIP = [(a * 2 + xh, (a + 1) * 2 + xh) for a in range(1, 63, 2) for xh in range(2)]
NEXT_CHIP = NEXT_CHIP + [(b, a) for a, b in NEXT_CHIP]

def last_hop(m):
    return perm_of(lambda xl, z, y, c, xh: (xl, z, y, xh ^ m, c))


def send(v, pairs):
    return lax.ppermute(v, AXES, pairs)


def edges(shard, width, c):
    first, last = shard[:width], shard[shard.shape[0] - width :]
    if width == shard.shape[0]:
        inner = outer = shard
    else:
        inner = jnp.where(c == 0, last, first)
        outer = jnp.where(c == 0, first, last)
    outer = send(outer, NEXT_CHIP)
    inner = send(inner, CORE)
    return jnp.where(c == 0, outer, inner), jnp.where(c == 0, inner, outer)


def extended(shard, width, c):
    before, after = edges(shard, width, c)
    return jnp.concatenate([before, shard, after], axis=0)


def smooth(values):
    return jax.nn.gelu(values, approximate=True)


def over_chips(blocks):
    got = lax.all_to_all(blocks, ("xl", "z", "y"), 0, 0, tiled=True)
    return jnp.sum(got.astype(F32), axis=0).astype(BF)


def over_halves(v):
    return sum(send(v, last_hop(m)).astype(F32) for m in range(2))


def per_device(trunk, conv_weight, head_weight, targets, error_mask, upweight):
    _, positions, channels = trunk.shape
    xl, z, y, c, xh = (lax.axis_index(axis) for axis in AXES)
    bins_all = positions * lax.axis_size(AXES)
    bin_weight = jnp.where(error_mask == 1, upweight, 1).astype(F32).reshape(positions, 1)
    weight_part = jnp.sum(bin_weight)
    first, last = (xl + z + y + c == 0), (xl == 1) & (z == 3) & (y == 3) & (c == 1)

    def inside(v, width):
        row = lax.broadcasted_iota(jnp.int32, (v.shape[0], 1), 0)
        out = (first & (row < width)) | (last & (row >= v.shape[0] - width))
        return jnp.where(out, jnp.zeros_like(v), v)

    def conv(rows, weights, d, count):
        total = jnp.dot(rows[d : d + count], weights[1], preferred_element_type=F32)
        total = total + jnp.dot(rows[:count], weights[0], preferred_element_type=F32)
        return total + jnp.dot(
            rows[2 * d : 2 * d + count], weights[2], preferred_element_type=F32
        )

    def conv_back(rows, weights, d, count):
        total = jnp.dot(rows[d : d + count], weights[1].T, preferred_element_type=F32)
        total = total + jnp.dot(
            rows[2 * d : 2 * d + count], weights[0].T, preferred_element_type=F32
        )
        return total + jnp.dot(rows[:count], weights[2].T, preferred_element_type=F32)

    def activate(v):
        return smooth(v.astype(F32)).astype(BF)

    def through(v, grad):
        return jax.vjp(smooth, v.astype(F32))[1](grad)[0]

    wide0 = extended(trunk[0], 192, c)
    act0 = activate(wide0)
    wide1 = (wide0[64:576].astype(F32) + conv(act0, conv_weight[0], 64, 512)).astype(BF)
    wide1 = inside(wide1, 128)
    act1 = activate(wide1)
    stream2 = (wide1[128:384].astype(F32) + conv(act1, conv_weight[1], 128, 256)).astype(BF)
    act2 = activate(stream2)
    before, after = edges(act2, 256, c)
    far_acts = [send(act0[128:512], CORE), send(act1, CORE)]
    before, far_acts[0], far_acts[1] = lax.optimization_barrier((before, *far_acts))
    act2 = jnp.concatenate([before, act2, after], axis=0)
    far_acts.append(send(act2, CORE))
    stream = (stream2.astype(F32) + conv(act2, conv_weight[2], 256, 256)).astype(BF)
    padded_acts = [act0[128:512], act1, act2]
    logits = jnp.dot(stream, head_weight, preferred_element_type=F32)
    predicted = jax.nn.softplus(logits)
    slope = jax.nn.sigmoid(logits)
    counts = targets[0].astype(F32)
    partial_loss = jnp.sum(bin_weight * (predicted - counts * jnp.log(predicted)))
    logit_grad = (bin_weight * (1.0 - counts / predicted) * slope).astype(BF)
    logit_grad, far_acts[2] = lax.optimization_barrier((logit_grad, far_acts[2]))
    lanes = lax.broadcasted_iota(jnp.int32, (1, 1408), 1)
    spare = lanes - 1344 * (1 - c)

    def with_scalars(v, scalars):
        for n, s in enumerate(scalars):
            inside = (spare >= 32 * n) & (spare < 32 * n + 32)
            v = jnp.where(inside, s * (1.0 + (spare - 32 * n).astype(F32) / 32), v)
        return v

    def halves(v, width):
        low, high = v[:, :width], v[:, v.shape[1] - width :]
        return jnp.where(c == 0, low, high), jnp.where(c == 0, high, low)

    def pair_dot(a, b, far_a, far_b):
        return jnp.dot(a.T, b, preferred_element_type=F32) + jnp.dot(
            far_a.T, far_b, preferred_element_type=F32
        )

    near, far = halves(logit_grad, 1408)
    scal = jnp.stack([weight_part, partial_loss])
    scal = scal + send(scal, CORE)
    head_half = pair_dot(stream, near, send(stream, CORE), send(far, CORE))
    head_half = with_scalars(head_half, (scal[0], scal[1])).astype(BF)
    g_top = jnp.dot(logit_grad, head_weight.T, preferred_element_type=F32)

    def conv_grad(layer, grad_bf):
        d = BASE_DILATION * 2**layer
        padded = padded_acts[layer]
        far_padded = far_acts[layer]
        near, far = halves(grad_bf, 384)
        far = send(far, CORE)
        return jnp.concatenate(
            [
                pair_dot(padded[rows], near, far_padded[rows], far).astype(BF)
                for rows in (slice(tap * d, tap * d + positions) for tap in range(3))
            ],
            axis=0,
        )

    gb2 = g_top.astype(BF)
    before, after = edges(gb2, 256, c)
    half2 = conv_grad(2, gb2)
    head_rows = jnp.pad(head_half, ((0, 0), (0, 128))).reshape(32, 24, 1536)
    early = jnp.concatenate(
        [half2.reshape(32, 72, 384)]
        + [head_rows[..., 384 * k : 384 * k + 384] for k in range(4)],
        axis=1,
    )
    before, early = lax.optimization_barrier((before, early))
    early = over_chips(early)
    wide = jnp.concatenate([before, gb2, after], axis=0)
    g2 = g_top + through(stream2, conv_back(wide, conv_weight[2], 256, 256))
    gb1 = g2.astype(BF)
    before, after = edges(gb1, 192, c)
    half1 = conv_grad(1, gb1)
    before, half1 = lax.optimization_barrier((before, half1))
    wide = jnp.concatenate([before, gb1, after], axis=0)
    g_in = jnp.concatenate([before[128:].astype(F32), g2, after[:64].astype(F32)], axis=0)
    g1 = g_in + through(wide1[64:448], conv_back(wide, conv_weight[1], 128, 384))
    gb0 = inside(g1.astype(BF), 64)
    half0 = conv_grad(0, gb0[64:320])
    late = jnp.concatenate([half0.reshape(32, 72, 384), half1.reshape(32, 72, 384)], axis=1)
    gb0, late, early = lax.optimization_barrier((gb0, late, early))
    late = over_chips(late)
    g0 = g1[64:320] + through(trunk[0], conv_back(gb0, conv_weight[0], 64, 256))
    g0 = lax.optimization_barrier(g0)
    early = over_halves(early)
    late = over_halves(late)

    def own(v):
        half = v.shape[0] // 2
        return jnp.where(c == 0, v[:half], v[half:])

    conv_total = jnp.stack([own(late[:72]), own(late[72:]), own(early[:72])])
    head_total = jnp.concatenate(
        [own(early[72 + 24 * k : 96 + 24 * k]) for k in range(4)], axis=1
    )
    low = head_total[:, :1344]
    high = head_total[:, 64:1408]
    row = head_total[0]
    found = jnp.where(xh == 0, row[1344:1408], row[:64])
    weight_sum = jnp.sum(found[:32]) / 47.5
    loss_sum = jnp.sum(found[32:]) / 47.5
    factor = bins_all / weight_sum
    loss = loss_sum / (OUTPUT_TRACKS * weight_sum)
    return (
        loss,
        conv_total * factor,
        jnp.where(xh == 0, low, high) * factor,
        (g0 * factor).astype(BF)[None],
    )


def solution(mesh):
    parts = Mesh(mesh.devices.reshape(2, 4, 4, 2, 2), ("xl", "z", "y", "c", "xh"))
    seq = ("xl", "z", "y", "c")
    return jax.shard_map(
        per_device,
        mesh=parts,
        in_specs=(
            P("xh", seq, None),
            P(),
            P(),
            P("xh", seq, None),
            P("xh", seq),
            P("xh", seq),
        ),
        out_specs=(P(), P(None, seq, "xh"), P(seq, "xh"), P("xh", seq, None)),
        check_vma=False,
    )
```

```python
import jax
import jax.numpy as jnp
from jax import lax
from jax.sharding import Mesh
from jax.sharding import PartitionSpec as P

OUTPUT_TRACKS = 2688
LAYERS = 3
BASE_DILATION = 64
AXES = ("xl", "z", "y", "c", "xh")
BF = jnp.bfloat16
F32 = jnp.float32


def perm_of(target):
    pairs = []
    for xl in range(2):
        for z in range(4):
            for y in range(4):
                for c in range(2):
                    for xh in range(2):
                        goal = target(xl, z, y, c, xh)
                        pairs.append((lin(xl, z, y, c, xh), lin(*goal)))
    return pairs


def lin(xl, z, y, c, xh):
    return (((xl * 4 + z) * 4 + y) * 2 + c) * 2 + xh


CORE = perm_of(lambda xl, z, y, c, xh: (xl, z, y, 1 - c, xh))
NEXT_CHIP = [(a * 2 + xh, (a + 1) * 2 + xh) for a in range(1, 63, 2) for xh in range(2)]
NEXT_CHIP = NEXT_CHIP + [(b, a) for a, b in NEXT_CHIP]

ALONG_X = perm_of(lambda xl, z, y, c, xh: (1 - xl, z, y, c, xh))


def last_hop(dx, m):
    return perm_of(lambda xl, z, y, c, xh: (xl ^ dx, z, y, xh ^ m, c))


def send(v, pairs):
    return lax.ppermute(v, AXES, pairs)


def edges(shard, width, c):
    first, last = shard[:width], shard[shard.shape[0] - width :]
    if width == shard.shape[0]:
        inner = outer = shard
    else:
        inner = jnp.where(c == 0, last, first)
        outer = jnp.where(c == 0, first, last)
    outer = send(outer, NEXT_CHIP)
    inner = send(inner, CORE)
    return jnp.where(c == 0, outer, inner), jnp.where(c == 0, inner, outer)


def extended(shard, width, c):
    before, after = edges(shard, width, c)
    return jnp.concatenate([before, shard, after], axis=0)


def smooth(values):
    return jax.nn.gelu(values, approximate=True)


def pick(blocks, place):
    return lax.dynamic_index_in_dim(blocks, place, 0, keepdims=False)


def over_plane(blocks):
    got = lax.all_to_all(blocks, ("z", "y"), 0, 0, tiled=True)
    return jnp.sum(got.astype(F32), axis=0).astype(BF)


def last_sum(near, rest):
    total = sum(send(near, last_hop(0, m)).astype(F32) for m in range(2))
    more = sum(send(rest, last_hop(1, m)).astype(F32) for m in range(2))
    count = rest.shape[0]
    return jnp.concatenate([total[:count] + more, total[count:]], axis=0)


def per_device(trunk, conv_weight, head_weight, targets, error_mask, upweight):
    _, positions, channels = trunk.shape
    xl, z, y, c, xh = (lax.axis_index(axis) for axis in AXES)
    bins_all = positions * lax.axis_size(AXES)
    bin_weight = jnp.where(error_mask == 1, upweight, 1).astype(F32).reshape(positions, 1)
    weight_part = jnp.sum(bin_weight)
    first, last = (xl + z + y + c == 0), (xl == 1) & (z == 3) & (y == 3) & (c == 1)

    def inside(v, width):
        row = lax.broadcasted_iota(jnp.int32, (v.shape[0], 1), 0)
        out = (first & (row < width)) | (last & (row >= v.shape[0] - width))
        return jnp.where(out, jnp.zeros_like(v), v)

    def conv(rows, weights, d, count):
        total = jnp.dot(rows[d : d + count], weights[1], preferred_element_type=F32)
        total = total + jnp.dot(rows[:count], weights[0], preferred_element_type=F32)
        return total + jnp.dot(
            rows[2 * d : 2 * d + count], weights[2], preferred_element_type=F32
        )

    def conv_back(rows, weights, d, count):
        total = jnp.dot(rows[d : d + count], weights[1].T, preferred_element_type=F32)
        total = total + jnp.dot(
            rows[2 * d : 2 * d + count], weights[0].T, preferred_element_type=F32
        )
        return total + jnp.dot(rows[:count], weights[2].T, preferred_element_type=F32)

    def activate(v):
        return smooth(v.astype(F32)).astype(BF)

    def through(v, grad):
        return jax.vjp(smooth, v.astype(F32))[1](grad)[0]

    wide0 = extended(trunk[0], 192, c)
    act0 = activate(wide0)
    wide1 = (wide0[64:576].astype(F32) + conv(act0, conv_weight[0], 64, 512)).astype(BF)
    wide1 = inside(wide1, 128)
    act1 = activate(wide1)
    stream2 = (wide1[128:384].astype(F32) + conv(act1, conv_weight[1], 128, 256)).astype(BF)
    act2 = activate(stream2)
    before, after = edges(act2, 256, c)
    far_acts = [send(act0[128:512], CORE), send(act1, CORE)]
    before, far_acts[0], far_acts[1] = lax.optimization_barrier((before, *far_acts))
    act2 = jnp.concatenate([before, act2, after], axis=0)
    far_acts.append(send(act2, CORE))
    stream = (stream2.astype(F32) + conv(act2, conv_weight[2], 256, 256)).astype(BF)
    padded_acts = [act0[128:512], act1, act2]
    logits = jnp.dot(stream, head_weight, preferred_element_type=F32)
    predicted = jax.nn.softplus(logits)
    slope = jax.nn.sigmoid(logits)
    counts = targets[0].astype(F32)
    partial_loss = jnp.sum(bin_weight * (predicted - counts * jnp.log(predicted)))
    logit_grad = (bin_weight * (1.0 - counts / predicted) * slope).astype(BF)
    logit_grad, far_acts[2] = lax.optimization_barrier((logit_grad, far_acts[2]))
    lanes = lax.broadcasted_iota(jnp.int32, (1, 1408), 1)
    spare = lanes - 1344 * (1 - c)

    def with_scalars(v, scalars):
        for n, s in enumerate(scalars):
            inside = (spare >= 32 * n) & (spare < 32 * n + 32)
            v = jnp.where(inside, s * (1.0 + (spare - 32 * n).astype(F32) / 32), v)
        return v

    def halves(v, width):
        low, high = v[:, :width], v[:, v.shape[1] - width :]
        return jnp.where(c == 0, low, high), jnp.where(c == 0, high, low)

    def pair_dot(a, b, far_a, far_b):
        return jnp.dot(a.T, b, preferred_element_type=F32) + jnp.dot(
            far_a.T, far_b, preferred_element_type=F32
        )

    near, far = halves(logit_grad, 1408)
    scal = jnp.stack([weight_part, partial_loss])
    scal = scal + send(scal, CORE)
    head_half = pair_dot(stream, near, send(stream, CORE), send(far, CORE))
    head_half = with_scalars(head_half, (scal[0], scal[1])).astype(BF)
    g_top = jnp.dot(logit_grad, head_weight.T, preferred_element_type=F32)

    def conv_grad(layer, grad_bf):
        d = BASE_DILATION * 2**layer
        padded = padded_acts[layer]
        far_padded = far_acts[layer]
        near, far = halves(grad_bf, 384)
        far = send(far, CORE)
        return jnp.concatenate(
            [
                pair_dot(padded[rows], near, far_padded[rows], far).astype(BF)
                for rows in (slice(tap * d, tap * d + positions) for tap in range(3))
            ],
            axis=0,
        )

    gb2 = g_top.astype(BF)
    before, after = edges(gb2, 256, c)
    half2 = conv_grad(2, gb2)
    head_rows = jnp.pad(head_half, ((0, 0), (0, 128))).reshape(32, 24, 1536)
    early = jnp.concatenate(
        [half2.reshape(32, 72, 384)]
        + [head_rows[..., 384 * k : 384 * k + 384] for k in range(4)],
        axis=1,
    )
    early = early.reshape(2, 16, 168, 384).transpose(1, 0, 2, 3).reshape(16 * 336, 384)
    before, early = lax.optimization_barrier((before, early))
    early = lax.psum_scatter(early, ("z", "y"), scatter_dimension=0, tiled=True)
    wide = jnp.concatenate([before, gb2, after], axis=0)
    g2 = g_top + through(stream2, conv_back(wide, conv_weight[2], 256, 256))
    gb1 = g2.astype(BF)
    before, after = edges(gb1, 192, c)
    half1 = conv_grad(1, gb1)
    half1 = half1.reshape(2, 1152, 384)
    got1 = send(pick(half1, 1 - xl), ALONG_X)
    before, half1 = lax.optimization_barrier((before, half1))
    wide = jnp.concatenate([before, gb1, after], axis=0)
    g_in = jnp.concatenate([before[128:].astype(F32), g2, after[:64].astype(F32)], axis=0)
    g1 = g_in + through(wide1[64:448], conv_back(wide, conv_weight[1], 128, 384))
    gb0 = inside(g1.astype(BF), 64)
    half0 = conv_grad(0, gb0[64:320])
    half1 = (pick(half1, xl).astype(F32) + got1.astype(F32)).astype(BF).reshape(16, 72, 384)
    half0 = half0.reshape(2, 16, 72, 384)
    late = jnp.concatenate([half0[0], half0[1], half1], axis=1)
    gb0, late = lax.optimization_barrier((gb0, late))
    late = over_plane(late)
    g0 = g1[64:320] + through(trunk[0], conv_back(gb0, conv_weight[0], 64, 256))
    g0, late = lax.optimization_barrier((g0, late))
    early = early.reshape(2, 168, 384)
    half0, half1 = late[:144].reshape(2, 72, 384), late[144:]
    near = jnp.concatenate([pick(early, xl), pick(half0, xl), half1], axis=0)
    rest = jnp.concatenate([pick(early, 1 - xl), pick(half0, 1 - xl)], axis=0)
    total = last_sum(near, rest)
    early, late = total[:168], total[168:]

    def own(v):
        half = v.shape[0] // 2
        return jnp.where(c == 0, v[:half], v[half:])

    conv_total = jnp.stack([own(late[:72]), own(late[72:]), own(early[:72])])
    head_total = jnp.concatenate(
        [own(early[72 + 24 * k : 96 + 24 * k]) for k in range(4)], axis=1
    )
    low = head_total[:, :1344]
    high = head_total[:, 64:1408]
    row = head_total[0]
    found = jnp.where(xh == 0, row[1344:1408], row[:64])
    weight_sum = jnp.sum(found[:32]) / 47.5
    loss_sum = jnp.sum(found[32:]) / 47.5
    factor = bins_all / weight_sum
    loss = loss_sum / (OUTPUT_TRACKS * weight_sum)
    return (
        loss,
        conv_total * factor,
        jnp.where(xh == 0, low, high) * factor,
        (g0 * factor).astype(BF)[None],
    )


def solution(mesh):
    parts = Mesh(mesh.devices.reshape(2, 4, 4, 2, 2), ("xl", "z", "y", "c", "xh"))
    seq = ("xl", "z", "y", "c")
    return jax.shard_map(
        per_device,
        mesh=parts,
        in_specs=(
            P("xh", seq, None),
            P(),
            P(),
            P("xh", seq, None),
            P("xh", seq),
            P("xh", seq),
        ),
        out_specs=(P(), P(None, seq, "xh"), P(seq, "xh"), P("xh", seq, None)),
        check_vma=False,
    )
```

```python
import jax
import jax.numpy as jnp
from jax import lax
from jax.sharding import Mesh
from jax.sharding import PartitionSpec as P

OUTPUT_TRACKS = 2688
LAYERS = 3
BASE_DILATION = 64
AXES = ("xl", "z", "y", "c", "xh")
BF = jnp.bfloat16
F32 = jnp.float32


def perm_of(target):
    pairs = []
    for xl in range(2):
        for z in range(4):
            for y in range(4):
                for c in range(2):
                    for xh in range(2):
                        goal = target(xl, z, y, c, xh)
                        pairs.append((lin(xl, z, y, c, xh), lin(*goal)))
    return pairs


def lin(xl, z, y, c, xh):
    return (((xl * 4 + z) * 4 + y) * 2 + c) * 2 + xh


CORE = perm_of(lambda xl, z, y, c, xh: (xl, z, y, 1 - c, xh))
NEXT_CHIP = [(a * 2 + xh, (a + 1) * 2 + xh) for a in range(1, 63, 2) for xh in range(2)]
NEXT_CHIP = NEXT_CHIP + [(b, a) for a, b in NEXT_CHIP]
ALONG_Y = [perm_of(lambda xl, z, y, c, xh, k=k: (xl, z, y ^ k, c, xh)) for k in range(4)]
ALONG_Z = [perm_of(lambda xl, z, y, c, xh, k=k: (xl, z ^ k, y, c, xh)) for k in range(4)]


def last_hop(dx, m):
    return perm_of(lambda xl, z, y, c, xh: (xl ^ dx, z, y, xh ^ m, c))


def send(v, pairs):
    return lax.ppermute(v, AXES, pairs)


def edges(shard, width, c):
    first, last = shard[:width], shard[shard.shape[0] - width :]
    if width == shard.shape[0]:
        inner = outer = shard
    else:
        inner = jnp.where(c == 0, last, first)
        outer = jnp.where(c == 0, first, last)
    outer = send(outer, NEXT_CHIP)
    inner = send(inner, CORE)
    return jnp.where(c == 0, outer, inner), jnp.where(c == 0, inner, outer)


def extended(shard, width, c):
    before, after = edges(shard, width, c)
    return jnp.concatenate([before, shard, after], axis=0)


def smooth(values):
    return jax.nn.gelu(values, approximate=True)


def pick(blocks, place, axis=0):
    return lax.dynamic_index_in_dim(blocks, place, axis, keepdims=False)


def give(part, bit, route, outer=1):
    rows, lanes = part.shape
    halves = part.reshape(outer, 2, rows // (2 * outer), lanes)
    return send(pick(halves, 1 - bit, 1), route)


def take(part, got, bit):
    rows, lanes = part.shape
    outer = got.shape[0]
    halves = part.reshape(outer, 2, rows // (2 * outer), lanes)
    total = pick(halves, bit, 1).astype(F32) + got.astype(F32)
    return total.astype(BF).reshape(rows // 2, lanes)


def plane_sum(blocks):
    got = lax.all_to_all(blocks, ("z", "y"), 0, 0, tiled=True)
    return jnp.sum(got.astype(F32), axis=0).astype(BF)


def last_sum(near, rest):
    total = sum(send(near, last_hop(0, m)).astype(F32) for m in range(2))
    return total + sum(send(rest, last_hop(1, m)).astype(F32) for m in range(2))


def per_device(trunk, conv_weight, head_weight, targets, error_mask, upweight):
    _, positions, channels = trunk.shape
    xl, z, y, c, xh = (lax.axis_index(axis) for axis in AXES)
    bins_all = positions * lax.axis_size(AXES)
    bin_weight = jnp.where(error_mask == 1, upweight, 1).astype(F32).reshape(positions, 1)
    weight_part = jnp.sum(bin_weight)
    first, last = (xl + z + y + c == 0), (xl == 1) & (z == 3) & (y == 3) & (c == 1)

    def inside(v, width):
        row = lax.broadcasted_iota(jnp.int32, (v.shape[0], 1), 0)
        out = (first & (row < width)) | (last & (row >= v.shape[0] - width))
        return jnp.where(out, jnp.zeros_like(v), v)

    def conv(rows, weights, d, count):
        total = jnp.dot(rows[d : d + count], weights[1], preferred_element_type=F32)
        total = total + jnp.dot(rows[:count], weights[0], preferred_element_type=F32)
        return total + jnp.dot(
            rows[2 * d : 2 * d + count], weights[2], preferred_element_type=F32
        )

    def conv_back(rows, weights, d, count):
        total = jnp.dot(rows[d : d + count], weights[1].T, preferred_element_type=F32)
        total = total + jnp.dot(
            rows[2 * d : 2 * d + count], weights[0].T, preferred_element_type=F32
        )
        return total + jnp.dot(rows[:count], weights[2].T, preferred_element_type=F32)

    def activate(v):
        return smooth(v.astype(F32)).astype(BF)

    def through(v, grad):
        return jax.vjp(smooth, v.astype(F32))[1](grad)[0]

    wide0 = extended(trunk[0], 192, c)
    act0 = activate(wide0)
    wide1 = (wide0[64:576].astype(F32) + conv(act0, conv_weight[0], 64, 512)).astype(BF)
    wide1 = inside(wide1, 128)
    act1 = activate(wide1)
    stream2 = (wide1[128:384].astype(F32) + conv(act1, conv_weight[1], 128, 256)).astype(BF)
    act2 = activate(stream2)
    before, after = edges(act2, 256, c)
    far_acts = [send(act0[128:512], CORE), send(act1, CORE)]
    before, far_acts[0], far_acts[1] = lax.optimization_barrier((before, *far_acts))
    act2 = jnp.concatenate([before, act2, after], axis=0)
    far_acts.append(send(act2, CORE))
    stream = (stream2.astype(F32) + conv(act2, conv_weight[2], 256, 256)).astype(BF)
    padded_acts = [act0[128:512], act1, act2]
    logits = jnp.dot(stream, head_weight, preferred_element_type=F32)
    predicted = jax.nn.softplus(logits)
    slope = jax.nn.sigmoid(logits)
    counts = targets[0].astype(F32)
    partial_loss = jnp.sum(bin_weight * (predicted - counts * jnp.log(predicted)))
    logit_grad = (bin_weight * (1.0 - counts / predicted) * slope).astype(BF)
    logit_grad, far_acts[2] = lax.optimization_barrier((logit_grad, far_acts[2]))
    lanes = lax.broadcasted_iota(jnp.int32, (1, 1408), 1)
    spare = lanes - 1344 * (1 - c)

    def with_scalars(v, scalars):
        for n, s in enumerate(scalars):
            inside = (spare >= 32 * n) & (spare < 32 * n + 32)
            v = jnp.where(inside, s * (1.0 + (spare - 32 * n).astype(F32) / 32), v)
        return v

    def halves(v, width):
        low, high = v[:, :width], v[:, v.shape[1] - width :]
        return jnp.where(c == 0, low, high), jnp.where(c == 0, high, low)

    def pair_dot(a, b, far_a, far_b):
        return jnp.dot(a.T, b, preferred_element_type=F32) + jnp.dot(
            far_a.T, far_b, preferred_element_type=F32
        )

    g_top = jnp.dot(logit_grad, head_weight.T, preferred_element_type=F32)
    gb2 = g_top.astype(BF)
    gb2, logit_grad, partial_loss, far_stream = lax.optimization_barrier(
        (gb2, logit_grad, partial_loss, send(stream, CORE))
    )
    near, far = halves(logit_grad, 1408)
    scal = jnp.stack([weight_part, partial_loss])
    scal = scal + send(scal, CORE)
    head_half = pair_dot(stream, near, far_stream, send(far, CORE))
    head_half = with_scalars(head_half, (scal[0], scal[1])).astype(BF)
    head_got = give(head_half, z // 2, ALONG_Z[3], 2)

    def conv_grad(layer, grad_bf):
        d = BASE_DILATION * 2**layer
        padded = padded_acts[layer]
        far_padded = far_acts[layer]
        near, far = halves(grad_bf, 384)
        far = send(far, CORE)
        return jnp.concatenate(
            [
                pair_dot(padded[rows], near, far_padded[rows], far).astype(BF)
                for rows in (slice(tap * d, tap * d + positions) for tap in range(3))
            ],
            axis=0,
        )

    before, after = edges(gb2, 256, c)
    half2 = conv_grad(2, gb2)
    got2 = give(half2, z // 2, ALONG_Z[3], 2)
    before, head_half, half2 = lax.optimization_barrier((before, head_half, half2))
    wide = jnp.concatenate([before, gb2, after], axis=0)
    g2 = g_top + through(stream2, conv_back(wide, conv_weight[2], 256, 256))
    gb1 = g2.astype(BF)
    before, after = edges(gb1, 192, c)
    half1 = conv_grad(1, gb1)
    got1 = give(half1, z // 2, ALONG_Z[3], 2)
    before, half1 = lax.optimization_barrier((before, half1))
    wide = jnp.concatenate([before, gb1, after], axis=0)
    g_in = jnp.concatenate([before[128:].astype(F32), g2, after[:64].astype(F32)], axis=0)
    g1 = g_in + through(wide1[64:448], conv_back(wide, conv_weight[1], 128, 384))
    gb0 = inside(g1.astype(BF), 64)
    head_z = take(head_half, head_got, z // 2)
    part2_z = take(half2, got2, z // 2)
    head_got = give(head_z, z % 2, ALONG_Z[1], 2)
    got2 = give(part2_z, z % 2, ALONG_Z[1], 2)
    gb0, head_z, part2_z = lax.optimization_barrier((gb0, head_z, part2_z))
    half0 = conv_grad(0, gb0[64:320])
    half0 = half0.reshape(2, 16, 72, 384).transpose(1, 0, 2, 3)
    half0, half1, part2_z, head_z = lax.optimization_barrier((half0, half1, part2_z, head_z))
    plane0 = plane_sum(half0)
    part1_z = take(half1, got1, z // 2)
    head_zz = take(head_z, head_got, z % 2)
    part2 = take(part2_z, got2, z % 2)
    part1 = take(part1_z, give(part1_z, z % 2, ALONG_Z[1], 2), z % 2)
    g0 = g1[64:320] + through(trunk[0], conv_back(gb0, conv_weight[0], 64, 256))
    g0 = lax.optimization_barrier(g0)
    head_rows = jnp.pad(head_zz, ((0, 0), (0, 128))).reshape(2, 4, 24, 1536)
    early = jnp.concatenate(
        [part1.reshape(2, 4, 72, 384), part2.reshape(2, 4, 72, 384)]
        + [head_rows[..., 384 * k : 384 * k + 384] for k in range(4)],
        axis=2,
    )
    got = [send(pick(early, y ^ k, 1), ALONG_Y[k]) for k in (1, 3, 2)]
    early = sum((g.astype(F32) for g in got), pick(early, y, 1).astype(F32)).astype(BF)
    both = jnp.concatenate([plane0, early], axis=1)
    total = last_sum(pick(both, xl), pick(both, 1 - xl))
    part0, early = total[:72], total[72:]

    def own(v):
        half = v.shape[0] // 2
        return jnp.where(c == 0, v[:half], v[half:])

    conv_total = jnp.stack([own(part0), own(early[:72]), own(early[72:144])])
    head_total = jnp.concatenate(
        [own(early[144 + 24 * k : 168 + 24 * k]) for k in range(4)], axis=1
    )
    low = head_total[:, :1344]
    high = head_total[:, 64:1408]
    row = head_total[0]
    found = jnp.where(xh == 0, row[1344:1408], row[:64])
    weight_sum = jnp.sum(found[:32]) / 47.5
    loss_sum = jnp.sum(found[32:]) / 47.5
    factor = bins_all / weight_sum
    loss = loss_sum / (OUTPUT_TRACKS * weight_sum)
    return (
        loss,
        conv_total * factor,
        jnp.where(xh == 0, low, high) * factor,
        (g0 * factor).astype(BF)[None],
    )


def solution(mesh):
    parts = Mesh(mesh.devices.reshape(2, 4, 4, 2, 2), ("xl", "z", "y", "c", "xh"))
    seq = ("xl", "z", "y", "c")
    return jax.shard_map(
        per_device,
        mesh=parts,
        in_specs=(
            P("xh", seq, None),
            P(),
            P(),
            P("xh", seq, None),
            P("xh", seq),
            P("xh", seq),
        ),
        out_specs=(P(), P(None, seq, "xh"), P(seq, "xh"), P("xh", seq, None)),
        check_vma=False,
    )
```

```python
import jax
import jax.numpy as jnp
from jax import lax
from jax.sharding import Mesh
from jax.sharding import PartitionSpec as P

OUTPUT_TRACKS = 2688
LAYERS = 3
BASE_DILATION = 64
AXES = ("xl", "z", "y", "c", "xh")
BF = jnp.bfloat16
F32 = jnp.float32


def perm_of(target):
    pairs = []
    for xl in range(2):
        for z in range(4):
            for y in range(4):
                for c in range(2):
                    for xh in range(2):
                        goal = target(xl, z, y, c, xh)
                        pairs.append((lin(xl, z, y, c, xh), lin(*goal)))
    return pairs


def lin(xl, z, y, c, xh):
    return (((xl * 4 + z) * 4 + y) * 2 + c) * 2 + xh


CORE = perm_of(lambda xl, z, y, c, xh: (xl, z, y, 1 - c, xh))
NEXT_CHIP = [(a * 2 + xh, (a + 1) * 2 + xh) for a in range(1, 63, 2) for xh in range(2)]
NEXT_CHIP = NEXT_CHIP + [(b, a) for a, b in NEXT_CHIP]
ALONG_X = perm_of(lambda xl, z, y, c, xh: (1 - xl, z, y, c, xh))
ALONG_Y = [perm_of(lambda xl, z, y, c, xh, k=k: (xl, z, y ^ k, c, xh)) for k in range(4)]
ALONG_Z = [perm_of(lambda xl, z, y, c, xh, k=k: (xl, z ^ k, y, c, xh)) for k in range(4)]


def last_hop(dx, m):
    return perm_of(lambda xl, z, y, c, xh: (xl ^ dx, z, y, xh ^ m, c))


def send(v, pairs):
    return lax.ppermute(v, AXES, pairs)


def edges(shard, width, c):
    first, last = shard[:width], shard[shard.shape[0] - width :]
    if width == shard.shape[0]:
        inner = outer = shard
    else:
        inner = jnp.where(c == 0, last, first)
        outer = jnp.where(c == 0, first, last)
    outer = send(outer, NEXT_CHIP)
    inner = send(inner, CORE)
    return jnp.where(c == 0, outer, inner), jnp.where(c == 0, inner, outer)


def extended(shard, width, c):
    before, after = edges(shard, width, c)
    return jnp.concatenate([before, shard, after], axis=0)


def smooth(values):
    return jax.nn.gelu(values, approximate=True)


def pick(blocks, place, axis=0):
    return lax.dynamic_index_in_dim(blocks, place, axis, keepdims=False)


def give(part, bit, route, outer=1):
    rows, lanes = part.shape
    halves = part.reshape(outer, 2, rows // (2 * outer), lanes)
    return send(pick(halves, 1 - bit, 1), route)


def take(part, got, bit):
    rows, lanes = part.shape
    outer = got.shape[0]
    halves = part.reshape(outer, 2, rows // (2 * outer), lanes)
    total = pick(halves, bit, 1).astype(F32) + got.astype(F32)
    return total.astype(BF).reshape(rows // 2, lanes)


def plane_sum(blocks):
    got = lax.all_to_all(blocks, ("z", "y"), 0, 0, tiled=True)
    return jnp.sum(got.astype(F32), axis=0).astype(BF)


def last_sum(near, rest):
    total = sum(send(near, last_hop(0, m)).astype(F32) for m in range(2))
    more = sum(send(rest, last_hop(1, m)).astype(F32) for m in range(2))
    return total[: rest.shape[0]] + more, total[rest.shape[0] :]


def per_device(trunk, conv_weight, head_weight, targets, error_mask, upweight):
    _, positions, channels = trunk.shape
    xl, z, y, c, xh = (lax.axis_index(axis) for axis in AXES)
    bins_all = positions * lax.axis_size(AXES)
    bin_weight = jnp.where(error_mask == 1, upweight, 1).astype(F32).reshape(positions, 1)
    weight_part = jnp.sum(bin_weight)
    first, last = (xl + z + y + c == 0), (xl == 1) & (z == 3) & (y == 3) & (c == 1)

    def inside(v, width):
        row = lax.broadcasted_iota(jnp.int32, (v.shape[0], 1), 0)
        out = (first & (row < width)) | (last & (row >= v.shape[0] - width))
        return jnp.where(out, jnp.zeros_like(v), v)

    def conv(rows, weights, d, count):
        total = jnp.dot(rows[d : d + count], weights[1], preferred_element_type=F32)
        total = total + jnp.dot(rows[:count], weights[0], preferred_element_type=F32)
        return total + jnp.dot(
            rows[2 * d : 2 * d + count], weights[2], preferred_element_type=F32
        )

    def conv_back(rows, weights, d, count):
        total = jnp.dot(rows[d : d + count], weights[1].T, preferred_element_type=F32)
        total = total + jnp.dot(
            rows[2 * d : 2 * d + count], weights[0].T, preferred_element_type=F32
        )
        return total + jnp.dot(rows[:count], weights[2].T, preferred_element_type=F32)

    def activate(v):
        return smooth(v.astype(F32)).astype(BF)

    def through(v, grad):
        return jax.vjp(smooth, v.astype(F32))[1](grad)[0]

    wide0 = extended(trunk[0], 192, c)
    act0 = activate(wide0)
    wide1 = (wide0[64:576].astype(F32) + conv(act0, conv_weight[0], 64, 512)).astype(BF)
    wide1 = inside(wide1, 128)
    act1 = activate(wide1)
    stream2 = (wide1[128:384].astype(F32) + conv(act1, conv_weight[1], 128, 256)).astype(BF)
    act2 = activate(stream2)
    before, after = edges(act2, 256, c)
    far_acts = [send(act0[128:512], CORE), send(act1, CORE)]
    before, far_acts[0], far_acts[1] = lax.optimization_barrier((before, *far_acts))
    act2 = jnp.concatenate([before, act2, after], axis=0)
    far_acts.append(send(act2, CORE))
    stream = (stream2.astype(F32) + conv(act2, conv_weight[2], 256, 256)).astype(BF)
    padded_acts = [act0[128:512], act1, act2]
    logits = jnp.dot(stream, head_weight, preferred_element_type=F32)
    predicted = jax.nn.softplus(logits)
    slope = jax.nn.sigmoid(logits)
    counts = targets[0].astype(F32)
    partial_loss = jnp.sum(bin_weight * (predicted - counts * jnp.log(predicted)))
    logit_grad = (bin_weight * (1.0 - counts / predicted) * slope).astype(BF)
    logit_grad, far_acts[2] = lax.optimization_barrier((logit_grad, far_acts[2]))
    lanes = lax.broadcasted_iota(jnp.int32, (1, 1408), 1)
    spare = lanes - 1344 * (1 - c)

    def with_scalars(v, scalars):
        for n, s in enumerate(scalars):
            inside = (spare >= 32 * n) & (spare < 32 * n + 32)
            v = jnp.where(inside, s * (1.0 + (spare - 32 * n).astype(F32) / 32), v)
        return v

    def halves(v, width):
        low, high = v[:, :width], v[:, v.shape[1] - width :]
        return jnp.where(c == 0, low, high), jnp.where(c == 0, high, low)

    def pair_dot(a, b, far_a, far_b):
        return jnp.dot(a.T, b, preferred_element_type=F32) + jnp.dot(
            far_a.T, far_b, preferred_element_type=F32
        )

    g_top = jnp.dot(logit_grad, head_weight.T, preferred_element_type=F32)
    gb2 = g_top.astype(BF)
    gb2, logit_grad, partial_loss, far_stream = lax.optimization_barrier(
        (gb2, logit_grad, partial_loss, send(stream, CORE))
    )
    near, far = halves(logit_grad, 1408)
    scal = jnp.stack([weight_part, partial_loss])
    scal = scal + send(scal, CORE)
    head_half = pair_dot(stream, near, far_stream, send(far, CORE))
    head_half = with_scalars(head_half, (scal[0], scal[1])).astype(BF)
    head_got = give(head_half, xl, ALONG_X)

    def conv_grad(layer, grad_bf):
        d = BASE_DILATION * 2**layer
        padded = padded_acts[layer]
        far_padded = far_acts[layer]
        near, far = halves(grad_bf, 384)
        far = send(far, CORE)
        return jnp.concatenate(
            [
                pair_dot(padded[rows], near, far_padded[rows], far).astype(BF)
                for rows in (slice(tap * d, tap * d + positions) for tap in range(3))
            ],
            axis=0,
        )

    before, after = edges(gb2, 256, c)
    half2 = conv_grad(2, gb2)
    got2 = give(half2, z // 2, ALONG_Z[3], 2)
    before, head_half, half2 = lax.optimization_barrier((before, head_half, half2))
    wide = jnp.concatenate([before, gb2, after], axis=0)
    g2 = g_top + through(stream2, conv_back(wide, conv_weight[2], 256, 256))
    gb1 = g2.astype(BF)
    before, after = edges(gb1, 192, c)
    half1 = conv_grad(1, gb1)
    half1 = half1.reshape(2, 4, 288, 384)
    got1 = send(jnp.stack([pick(half1, z ^ 1, 1), pick(half1, z ^ 2, 1)]), ALONG_Z[1])
    before, half1 = lax.optimization_barrier((before, half1))
    wide = jnp.concatenate([before, gb1, after], axis=0)
    g_in = jnp.concatenate([before[128:].astype(F32), g2, after[:64].astype(F32)], axis=0)
    g1 = g_in + through(wide1[64:448], conv_back(wide, conv_weight[1], 128, 384))
    gb0 = inside(g1.astype(BF), 64)
    part2_z = take(half2, got2, z // 2)
    got2 = give(part2_z, z % 2, ALONG_Z[1], 2)
    gb0, part2_z = lax.optimization_barrier((gb0, part2_z))
    half0 = conv_grad(0, gb0[64:320])
    head_x = take(head_half, head_got, xl)
    head_rows = jnp.pad(head_x, ((0, 0), (0, 128))).reshape(16, 24, 1536)
    half0 = half0.reshape(2, 16, 72, 384)
    late = jnp.concatenate(
        [half0[0], half0[1]] + [head_rows[..., 384 * k : 384 * k + 384] for k in range(4)], axis=1
    )
    late, half1, part2_z = lax.optimization_barrier((late, half1, part2_z))
    late = plane_sum(late)
    keep1 = jnp.stack([pick(half1, z, 1), pick(half1, z ^ 3, 1)])
    keep1 = (keep1.astype(F32) + got1.astype(F32)).astype(BF)
    got1 = send(keep1[1], ALONG_Z[3])
    part1 = (keep1[0].astype(F32) + got1.astype(F32)).astype(BF)
    part2 = take(part2_z, got2, z % 2)
    g0 = g1[64:320] + through(trunk[0], conv_back(gb0, conv_weight[0], 64, 256))
    g0 = lax.optimization_barrier(g0)
    early = jnp.concatenate([part1.reshape(2, 4, 72, 384), part2.reshape(2, 4, 72, 384)], axis=2)
    got = [send(pick(early, y ^ k, 1), ALONG_Y[k]) for k in (1, 3, 2)]
    early = sum((g.astype(F32) for g in got), pick(early, y, 1).astype(F32)).astype(BF)
    both = jnp.concatenate([late[:144].reshape(2, 72, 384), early], axis=1)
    conv_sum, head_sum = last_sum(
        jnp.concatenate([pick(both, xl), late[144:]], axis=0), pick(both, 1 - xl)
    )

    def own(v):
        half = v.shape[0] // 2
        return jnp.where(c == 0, v[:half], v[half:])

    conv_total = jnp.stack([own(conv_sum[72 * k : 72 * k + 72]) for k in range(LAYERS)])
    head_total = jnp.concatenate([own(head_sum[24 * k : 24 * k + 24]) for k in range(4)], axis=1)
    low = head_total[:, :1344]
    high = head_total[:, 64:1408]
    row = head_total[0]
    found = jnp.where(xh == 0, row[1344:1408], row[:64])
    weight_sum = jnp.sum(found[:32]) / 47.5
    loss_sum = jnp.sum(found[32:]) / 47.5
    factor = bins_all / weight_sum
    loss = loss_sum / (OUTPUT_TRACKS * weight_sum)
    return (
        loss,
        conv_total * factor,
        jnp.where(xh == 0, low, high) * factor,
        (g0 * factor).astype(BF)[None],
    )


def solution(mesh):
    parts = Mesh(mesh.devices.reshape(2, 4, 4, 2, 2), ("xl", "z", "y", "c", "xh"))
    seq = ("xl", "z", "y", "c")
    return jax.shard_map(
        per_device,
        mesh=parts,
        in_specs=(
            P("xh", seq, None),
            P(),
            P(),
            P("xh", seq, None),
            P("xh", seq),
            P("xh", seq),
        ),
        out_specs=(P(), P(None, seq, "xh"), P(seq, "xh"), P("xh", seq, None)),
        check_vma=False,
    )
```

```python
import jax
import jax.numpy as jnp
from jax import lax
from jax.experimental import pallas as pl
from jax.experimental.pallas import tpu as pltpu
from jax.sharding import Mesh
from jax.sharding import PartitionSpec as P

OUTPUT_TRACKS = 2688
LAYERS = 3
BASE_DILATION = 64
AXES = ("xl", "z", "y", "c", "xh")
BF = jnp.bfloat16
F32 = jnp.float32


def perm_of(target):
    pairs = []
    for xl in range(2):
        for z in range(4):
            for y in range(4):
                for c in range(2):
                    for xh in range(2):
                        goal = target(xl, z, y, c, xh)
                        pairs.append((lin(xl, z, y, c, xh), lin(*goal)))
    return pairs


def lin(xl, z, y, c, xh):
    return (((xl * 4 + z) * 4 + y) * 2 + c) * 2 + xh


CORE = perm_of(lambda xl, z, y, c, xh: (xl, z, y, 1 - c, xh))
NEXT_CHIP = [(a * 2 + xh, (a + 1) * 2 + xh) for a in range(1, 63, 2) for xh in range(2)]
NEXT_CHIP = NEXT_CHIP + [(b, a) for a, b in NEXT_CHIP]
ALONG_X = perm_of(lambda xl, z, y, c, xh: (1 - xl, z, y, c, xh))
ALONG_Y = [perm_of(lambda xl, z, y, c, xh, k=k: (xl, z, y ^ k, c, xh)) for k in range(4)]
ALONG_Z = [perm_of(lambda xl, z, y, c, xh, k=k: (xl, z ^ k, y, c, xh)) for k in range(4)]


def last_hop(dx, m):
    return perm_of(lambda xl, z, y, c, xh: (xl ^ dx, z, y, xh ^ m, c))


def send(v, pairs):
    return lax.ppermute(v, AXES, pairs)


def edges(shard, width, c):
    first, last = shard[:width], shard[shard.shape[0] - width :]
    if width == shard.shape[0]:
        inner = outer = shard
    else:
        inner = jnp.where(c == 0, last, first)
        outer = jnp.where(c == 0, first, last)
    outer = send(outer, NEXT_CHIP)
    inner = send(inner, CORE)
    return jnp.where(c == 0, outer, inner), jnp.where(c == 0, inner, outer)


def copies_in(w_ref, scratch, sems, layers):
    order = [(n, layer, tap) for n, layer in enumerate(layers) for tap in (1, 0, 2)]
    made = {
        (n, tap): pltpu.make_async_copy(
            w_ref.at[layer, tap], scratch.at[n, tap], sems.at[n, tap]
        )
        for n, layer, tap in order
    }
    for n, layer, tap in order:
        made[n, tap].start()
    return made


def three_taps(rows, weights, n, d, start, count, cols, back):
    total = None
    for tap in (1, 0, 2):
        at = start + (2 - tap if back else tap) * d
        left = rows[at : at + count, :]
        if back:
            part = lax.dot_general(
                left, weights[n, tap, cols, :], (((1,), (1,)), ((), ())), preferred_element_type=F32
            )
        else:
            part = jnp.dot(left, weights[n, tap, :, cols], preferred_element_type=F32)
        total = part if total is None else total + part
    return total


def tanh_gelu(x):
    return 0.5 * x * (1.0 + jnp.tanh(0.7978845608028654 * (x + 0.044715 * x * x * x)))


def tanh_gelu_slope(x):
    t = jnp.tanh(0.7978845608028654 * (x + 0.044715 * x * x * x))
    return 0.5 * (1.0 + t) + 0.5 * x * (1.0 - t * t) * 0.7978845608028654 * (
        1.0 + 0.134145 * x * x
    )


def zero_outside(v, flags, start, width, total):
    row = start + lax.broadcasted_iota(jnp.int32, v.shape, 0)
    out = ((flags[0] == 1) & (row < width)) | ((flags[1] == 1) & (row >= total - width))
    return jnp.where(out, 0.0, v)


COLS = [slice(256 * n, 256 * n + 256) for n in range(3)]


def front_kernel(flags, before, own, after, w_ref, act0, wide1, act1, stream2, act2, wide, acts, weights, sems):
    made = copies_in(w_ref, weights, sems, (0, 1))
    wide[0:192, :] = before[...]
    wide[192:448, :] = own[...]
    wide[448:640, :] = after[...]
    for r in range(0, 640, 64):
        acts[r : r + 64, :] = tanh_gelu(wide[r : r + 64, :].astype(F32)).astype(BF)
    act0[...] = acts[128:512, :]
    for tap in (1, 0, 2):
        made[0, tap].wait()
    for start in (0, 256):
        for cols in COLS:
            conv = three_taps(acts, weights, 0, 64, start, 256, cols, False)
            stream = (wide[start + 64 : start + 320, cols].astype(F32) + conv).astype(BF)
            stream = zero_outside(stream.astype(F32), flags, start, 128, 512)
            wide1[start : start + 256, cols] = stream.astype(BF)
            act1[start : start + 256, cols] = tanh_gelu(stream).astype(BF)
    for tap in (1, 0, 2):
        made[1, tap].wait()
    for cols in COLS:
        conv = three_taps(act1, weights, 1, 128, 0, 256, cols, False)
        stream = (wide1[128:384, cols].astype(F32) + conv).astype(BF)
        stream2[:, cols] = stream
        act2[:, cols] = tanh_gelu(stream.astype(F32)).astype(BF)


def middle_kernel(before, own, after, stream, w_ref, padded, out, weights, sems):
    made = copies_in(w_ref, weights, sems, (2,))
    padded[0:256, :] = before[...]
    padded[256:512, :] = own[...]
    padded[512:768, :] = after[...]
    for tap in (1, 0, 2):
        made[0, tap].wait()
    for cols in COLS:
        conv = three_taps(padded, weights, 0, 256, 0, 256, cols, False)
        out[:, cols] = (stream[:, cols].astype(F32) + conv).astype(BF)


def back2_kernel(before, own, after, stream, grad, w_ref, out, out_bf, wide, weights, sems):
    made = copies_in(w_ref, weights, sems, (2,))
    wide[0:256, :] = before[...]
    wide[256:512, :] = own[...]
    wide[512:768, :] = after[...]
    for tap in (1, 0, 2):
        made[0, tap].wait()
    for cols in COLS:
        act_grad = three_taps(wide, weights, 0, 256, 0, 256, cols, True)
        total = grad[:, cols] + tanh_gelu_slope(stream[:, cols].astype(F32)) * act_grad
        out[:, cols] = total
        out_bf[:, cols] = total.astype(BF)


def back1_kernel(flags, before, own, after, stream, grad, w_ref, out, out_bf, wide, g_in, weights, sems):
    made = copies_in(w_ref, weights, sems, (1,))
    wide[0:192, :] = before[...]
    wide[192:448, :] = own[...]
    wide[448:640, :] = after[...]
    g_in[0:64, :] = before[128:192, :].astype(F32)
    g_in[64:320, :] = grad[...]
    g_in[320:384, :] = after[0:64, :].astype(F32)
    for tap in (1, 0, 2):
        made[0, tap].wait()
    for start in (0, 192):
        for cols in COLS:
            act_grad = three_taps(wide, weights, 0, 128, start, 192, cols, True)
            slope = tanh_gelu_slope(stream[start + 64 : start + 256, cols].astype(F32))
            total = g_in[start : start + 192, cols] + slope * act_grad
            g_in[start : start + 192, cols] = total
            out_bf[start : start + 192, cols] = zero_outside(total, flags, start, 64, 384).astype(BF)
    out[...] = g_in[64:320, :]


def on_core(kernel, outs, scratch, count, flops, *operands):
    def place(v):
        if v.ndim == 4:
            return pl.BlockSpec(memory_space=pl.ANY)
        if v.ndim == 1:
            return pl.BlockSpec(memory_space=pltpu.SMEM)
        return pl.BlockSpec(memory_space=pltpu.VMEM)

    return pl.pallas_call(
        kernel,
        out_shape=[jax.ShapeDtypeStruct((rows, 768), kind) for rows, kind in outs],
        in_specs=[place(v) for v in operands],
        out_specs=[pl.BlockSpec(memory_space=pltpu.VMEM) for _ in outs],
        scratch_shapes=[pltpu.VMEM((rows, 768), kind) for rows, kind in scratch]
        + [pltpu.VMEM((count, 3, 768, 768), BF), pltpu.SemaphoreType.DMA((count, 3))],
        compiler_params=pltpu.CompilerParams(vmem_limit_bytes=36 * 2**20),
        cost_estimate=pl.CostEstimate(
            flops=flops, bytes_accessed=count * 3 * 768 * 768 * 2, transcendentals=0
        ),
    )(*operands)


def smooth(values):
    return jax.nn.gelu(values, approximate=True)


def pick(blocks, place, axis=0):
    return lax.dynamic_index_in_dim(blocks, place, axis, keepdims=False)


def give(part, bit, route, outer=1):
    rows, lanes = part.shape
    halves = part.reshape(outer, 2, rows // (2 * outer), lanes)
    return send(pick(halves, 1 - bit, 1), route)


def take(part, got, bit):
    rows, lanes = part.shape
    outer = got.shape[0]
    halves = part.reshape(outer, 2, rows // (2 * outer), lanes)
    total = pick(halves, bit, 1).astype(F32) + got.astype(F32)
    return total.astype(BF).reshape(rows // 2, lanes)


def plane_sum(blocks):
    got = lax.all_to_all(blocks, ("z", "y"), 0, 0, tiled=True)
    return jnp.sum(got.astype(F32), axis=0).astype(BF)


def last_sum(near, rest):
    total = sum(send(near, last_hop(0, m)).astype(F32) for m in range(2))
    more = sum(send(rest, last_hop(1, m)).astype(F32) for m in range(2))
    return total[: rest.shape[0]] + more, total[rest.shape[0] :]


def per_device(trunk, conv_weight, head_weight, targets, error_mask, upweight):
    _, positions, channels = trunk.shape
    xl, z, y, c, xh = (lax.axis_index(axis) for axis in AXES)
    bins_all = positions * lax.axis_size(AXES)
    bin_weight = jnp.where(error_mask == 1, upweight, 1).astype(F32).reshape(positions, 1)
    weight_part = jnp.sum(bin_weight)
    first, last = (xl + z + y + c == 0), (xl == 1) & (z == 3) & (y == 3) & (c == 1)

    def conv_back(rows, weights, d, count):
        total = jnp.dot(rows[d : d + count], weights[1].T, preferred_element_type=F32)
        total = total + jnp.dot(
            rows[2 * d : 2 * d + count], weights[0].T, preferred_element_type=F32
        )
        return total + jnp.dot(rows[:count], weights[2].T, preferred_element_type=F32)

    def through(v, grad):
        return jax.vjp(smooth, v.astype(F32))[1](grad)[0]

    flags = jnp.stack([first, last]).astype(jnp.int32)
    tap_flops = 2 * 768 * 768 * 3
    before, after = edges(trunk[0], 192, c)
    act0, wide1, act1, stream2, act2 = on_core(
        front_kernel,
        [(384, BF), (512, BF), (512, BF), (256, BF), (256, BF)],
        [(640, BF), (640, BF)],
        2,
        768 * tap_flops,
        *(flags, before, trunk[0], after, conv_weight),
    )
    before, after = edges(act2, 256, c)
    far_acts = [send(act0, CORE), send(act1, CORE)]
    before, far_acts[0], far_acts[1] = lax.optimization_barrier((before, *far_acts))
    act2, stream = on_core(
        middle_kernel,
        [(768, BF), (256, BF)],
        [],
        1,
        256 * tap_flops,
        *(before, act2, after, stream2, conv_weight),
    )
    far_acts.append(send(act2, CORE))
    padded_acts = [act0, act1, act2]
    logits = jnp.dot(stream, head_weight, preferred_element_type=F32)
    predicted = jax.nn.softplus(logits)
    slope = jax.nn.sigmoid(logits)
    counts = targets[0].astype(F32)
    partial_loss = jnp.sum(bin_weight * (predicted - counts * jnp.log(predicted)))
    logit_grad = (bin_weight * (1.0 - counts / predicted) * slope).astype(BF)
    logit_grad, far_acts[2] = lax.optimization_barrier((logit_grad, far_acts[2]))
    lanes = lax.broadcasted_iota(jnp.int32, (1, 1408), 1)
    spare = lanes - 1344 * (1 - c)

    def with_scalars(v, scalars):
        for n, s in enumerate(scalars):
            inside = (spare >= 32 * n) & (spare < 32 * n + 32)
            v = jnp.where(inside, s * (1.0 + (spare - 32 * n).astype(F32) / 32), v)
        return v

    def halves(v, width):
        low, high = v[:, :width], v[:, v.shape[1] - width :]
        return jnp.where(c == 0, low, high), jnp.where(c == 0, high, low)

    def pair_dot(a, b, far_a, far_b):
        return jnp.dot(a.T, b, preferred_element_type=F32) + jnp.dot(
            far_a.T, far_b, preferred_element_type=F32
        )

    g_top = jnp.dot(logit_grad, head_weight.T, preferred_element_type=F32)
    gb2 = g_top.astype(BF)
    gb2, logit_grad, partial_loss, far_stream = lax.optimization_barrier(
        (gb2, logit_grad, partial_loss, send(stream, CORE))
    )
    near, far = halves(logit_grad, 1408)
    scal = jnp.stack([weight_part, partial_loss])
    scal = scal + send(scal, CORE)
    head_half = pair_dot(stream, near, far_stream, send(far, CORE))
    head_half = with_scalars(head_half, (scal[0], scal[1])).astype(BF)
    head_got = give(head_half, xl, ALONG_X)

    def conv_grad(layer, grad_bf):
        d = BASE_DILATION * 2**layer
        padded = padded_acts[layer]
        far_padded = far_acts[layer]
        near, far = halves(grad_bf, 384)
        far = send(far, CORE)
        return jnp.concatenate(
            [
                pair_dot(padded[rows], near, far_padded[rows], far).astype(BF)
                for rows in (slice(tap * d, tap * d + positions) for tap in range(3))
            ],
            axis=0,
        )

    before, after = edges(gb2, 256, c)
    half2 = conv_grad(2, gb2)
    got2 = give(half2, z // 2, ALONG_Z[3], 2)
    before, head_half, half2 = lax.optimization_barrier((before, head_half, half2))
    g2, gb1 = on_core(
        back2_kernel,
        [(256, F32), (256, BF)],
        [(768, BF)],
        1,
        256 * tap_flops,
        *(before, gb2, after, stream2, g_top, conv_weight),
    )
    before, after = edges(gb1, 192, c)
    half1 = conv_grad(1, gb1)
    half1 = half1.reshape(2, 4, 288, 384)
    got1 = send(jnp.stack([pick(half1, z ^ 1, 1), pick(half1, z ^ 2, 1)]), ALONG_Z[1])
    before, half1 = lax.optimization_barrier((before, half1))
    g1, gb0 = on_core(
        back1_kernel,
        [(256, F32), (384, BF)],
        [(640, BF), (384, F32)],
        1,
        384 * tap_flops,
        *(flags, before, gb1, after, wide1, g2, conv_weight),
    )
    part2_z = take(half2, got2, z // 2)
    got2 = give(part2_z, z % 2, ALONG_Z[1], 2)
    gb0, part2_z = lax.optimization_barrier((gb0, part2_z))
    half0 = conv_grad(0, gb0[64:320])
    head_x = take(head_half, head_got, xl)
    head_rows = jnp.pad(head_x, ((0, 0), (0, 128))).reshape(16, 24, 1536)
    half0 = half0.reshape(2, 16, 72, 384)
    late = jnp.concatenate(
        [half0[0], half0[1]] + [head_rows[..., 384 * k : 384 * k + 384] for k in range(4)], axis=1
    )
    late, half1, part2_z = lax.optimization_barrier((late, half1, part2_z))
    late = plane_sum(late)
    keep1 = jnp.stack([pick(half1, z, 1), pick(half1, z ^ 3, 1)])
    keep1 = (keep1.astype(F32) + got1.astype(F32)).astype(BF)
    got1 = send(keep1[1], ALONG_Z[3])
    part1 = (keep1[0].astype(F32) + got1.astype(F32)).astype(BF)
    part2 = take(part2_z, got2, z % 2)
    g0 = g1 + through(trunk[0], conv_back(gb0, conv_weight[0], 64, 256))
    g0 = lax.optimization_barrier(g0)
    early = jnp.concatenate([part1.reshape(2, 4, 72, 384), part2.reshape(2, 4, 72, 384)], axis=2)
    got = [send(pick(early, y ^ k, 1), ALONG_Y[k]) for k in (1, 3, 2)]
    early = sum((g.astype(F32) for g in got), pick(early, y, 1).astype(F32)).astype(BF)
    both = jnp.concatenate([late[:144].reshape(2, 72, 384), early], axis=1)
    conv_sum, head_sum = last_sum(
        jnp.concatenate([pick(both, xl), late[144:]], axis=0), pick(both, 1 - xl)
    )

    def own(v):
        half = v.shape[0] // 2
        return jnp.where(c == 0, v[:half], v[half:])

    conv_total = jnp.stack([own(conv_sum[72 * k : 72 * k + 72]) for k in range(LAYERS)])
    head_total = jnp.concatenate([own(head_sum[24 * k : 24 * k + 24]) for k in range(4)], axis=1)
    low = head_total[:, :1344]
    high = head_total[:, 64:1408]
    row = head_total[0]
    found = jnp.where(xh == 0, row[1344:1408], row[:64])
    weight_sum = jnp.sum(found[:32]) / 47.5
    loss_sum = jnp.sum(found[32:]) / 47.5
    factor = bins_all / weight_sum
    loss = loss_sum / (OUTPUT_TRACKS * weight_sum)
    return (
        loss,
        conv_total * factor,
        jnp.where(xh == 0, low, high) * factor,
        (g0 * factor).astype(BF)[None],
    )


def solution(mesh):
    parts = Mesh(mesh.devices.reshape(2, 4, 4, 2, 2), ("xl", "z", "y", "c", "xh"))
    seq = ("xl", "z", "y", "c")
    return jax.shard_map(
        per_device,
        mesh=parts,
        in_specs=(
            P("xh", seq, None),
            P(),
            P(),
            P("xh", seq, None),
            P("xh", seq),
            P("xh", seq),
        ),
        out_specs=(P(), P(None, seq, "xh"), P(seq, "xh"), P("xh", seq, None)),
        check_vma=False,
    )
```

```python
import jax
import jax.numpy as jnp
from jax import lax
from jax.experimental import pallas as pl
from jax.experimental.pallas import tpu as pltpu
from jax.sharding import Mesh
from jax.sharding import PartitionSpec as P

OUTPUT_TRACKS = 2688
LAYERS = 3
BASE_DILATION = 64
AXES = ("xl", "z", "y", "c", "xh")
BF = jnp.bfloat16
F32 = jnp.float32


def perm_of(target):
    pairs = []
    for xl in range(2):
        for z in range(4):
            for y in range(4):
                for c in range(2):
                    for xh in range(2):
                        goal = target(xl, z, y, c, xh)
                        pairs.append((lin(xl, z, y, c, xh), lin(*goal)))
    return pairs


def lin(xl, z, y, c, xh):
    return (((xl * 4 + z) * 4 + y) * 2 + c) * 2 + xh


CORE = perm_of(lambda xl, z, y, c, xh: (xl, z, y, 1 - c, xh))
NEXT_CHIP = [(a * 2 + xh, (a + 1) * 2 + xh) for a in range(1, 63, 2) for xh in range(2)]
NEXT_CHIP = NEXT_CHIP + [(b, a) for a, b in NEXT_CHIP]
ALONG_X = perm_of(lambda xl, z, y, c, xh: (1 - xl, z, y, c, xh))
ALONG_Y = [perm_of(lambda xl, z, y, c, xh, k=k: (xl, z, y ^ k, c, xh)) for k in range(4)]
ALONG_Z = [perm_of(lambda xl, z, y, c, xh, k=k: (xl, z ^ k, y, c, xh)) for k in range(4)]


def last_hop(dx, m):
    return perm_of(lambda xl, z, y, c, xh: (xl ^ dx, z, y, xh ^ m, c))


def send(v, pairs):
    return lax.ppermute(v, AXES, pairs)


def edges(shard, width, c):
    first, last = shard[:width], shard[shard.shape[0] - width :]
    if width == shard.shape[0]:
        inner = outer = shard
    else:
        inner = jnp.where(c == 0, last, first)
        outer = jnp.where(c == 0, first, last)
    outer = send(outer, NEXT_CHIP)
    inner = send(inner, CORE)
    return jnp.where(c == 0, outer, inner), jnp.where(c == 0, inner, outer)


def copies_in(w_ref, scratch, sems, layers):
    order = [(n, layer, tap) for n, layer in enumerate(layers) for tap in (1, 0, 2)]
    made = {
        (n, tap): pltpu.make_async_copy(
            w_ref.at[layer, tap], scratch.at[n, tap], sems.at[n, tap]
        )
        for n, layer, tap in order
    }
    for n, layer, tap in order:
        made[n, tap].start()
    return made


def three_taps(rows, weights, n, d, start, count, cols, back):
    total = None
    for tap in (1, 0, 2):
        at = start + (2 - tap if back else tap) * d
        left = rows[at : at + count, :]
        if back:
            part = lax.dot_general(
                left, weights[n, tap, cols, :], (((1,), (1,)), ((), ())), preferred_element_type=F32
            )
        else:
            part = jnp.dot(left, weights[n, tap, :, cols], preferred_element_type=F32)
        total = part if total is None else total + part
    return total


def tanh_gelu(x):
    return 0.5 * x * (1.0 + jnp.tanh(0.7978845608028654 * (x + 0.044715 * x * x * x)))


def tanh_gelu_slope(x):
    t = jnp.tanh(0.7978845608028654 * (x + 0.044715 * x * x * x))
    return 0.5 * (1.0 + t) + 0.5 * x * (1.0 - t * t) * 0.7978845608028654 * (
        1.0 + 0.134145 * x * x
    )


def zero_outside(v, flags, start, width, total):
    row = start + lax.broadcasted_iota(jnp.int32, v.shape, 0)
    out = ((flags[0] == 1) & (row < width)) | ((flags[1] == 1) & (row >= total - width))
    return jnp.where(out, 0.0, v)


COLS = [slice(256 * n, 256 * n + 256) for n in range(3)]


def front_kernel(flags, before, own, after, w_ref, act0, wide1, act1, stream2, act2, wide, acts, weights, sems):
    made = copies_in(w_ref, weights, sems, (0, 1))
    wide[0:192, :] = before[...]
    wide[192:448, :] = own[...]
    wide[448:640, :] = after[...]
    for r in range(0, 640, 64):
        acts[r : r + 64, :] = tanh_gelu(wide[r : r + 64, :].astype(F32)).astype(BF)
    act0[...] = acts[128:512, :]
    for tap in (1, 0, 2):
        made[0, tap].wait()
    for start in (0, 256):
        for cols in COLS:
            conv = three_taps(acts, weights, 0, 64, start, 256, cols, False)
            stream = (wide[start + 64 : start + 320, cols].astype(F32) + conv).astype(BF)
            stream = zero_outside(stream.astype(F32), flags, start, 128, 512)
            wide1[start : start + 256, cols] = stream.astype(BF)
            act1[start : start + 256, cols] = tanh_gelu(stream).astype(BF)
    for tap in (1, 0, 2):
        made[1, tap].wait()
    for cols in COLS:
        conv = three_taps(act1, weights, 1, 128, 0, 256, cols, False)
        stream = (wide1[128:384, cols].astype(F32) + conv).astype(BF)
        stream2[:, cols] = stream
        act2[:, cols] = tanh_gelu(stream.astype(F32)).astype(BF)


def middle_kernel(before, own, after, stream, w_ref, padded, out, weights, sems):
    made = copies_in(w_ref, weights, sems, (2,))
    padded[0:256, :] = before[...]
    padded[256:512, :] = own[...]
    padded[512:768, :] = after[...]
    for tap in (1, 0, 2):
        made[0, tap].wait()
    for cols in COLS:
        conv = three_taps(padded, weights, 0, 256, 0, 256, cols, False)
        out[:, cols] = (stream[:, cols].astype(F32) + conv).astype(BF)


def back2_kernel(before, own, after, stream, grad, w_ref, out, out_bf, wide, weights, sems):
    made = copies_in(w_ref, weights, sems, (2,))
    wide[0:256, :] = before[...]
    wide[256:512, :] = own[...]
    wide[512:768, :] = after[...]
    for tap in (1, 0, 2):
        made[0, tap].wait()
    for cols in COLS:
        act_grad = three_taps(wide, weights, 0, 256, 0, 256, cols, True)
        total = grad[:, cols] + tanh_gelu_slope(stream[:, cols].astype(F32)) * act_grad
        out[:, cols] = total
        out_bf[:, cols] = total.astype(BF)


def back1_kernel(flags, before, own, after, stream, grad, w_ref, out, out_bf, wide, g_in, weights, sems):
    made = copies_in(w_ref, weights, sems, (1,))
    wide[0:192, :] = before[...]
    wide[192:448, :] = own[...]
    wide[448:640, :] = after[...]
    g_in[0:64, :] = before[128:192, :].astype(F32)
    g_in[64:320, :] = grad[...]
    g_in[320:384, :] = after[0:64, :].astype(F32)
    for tap in (1, 0, 2):
        made[0, tap].wait()
    for start in (0, 192):
        for cols in COLS:
            act_grad = three_taps(wide, weights, 0, 128, start, 192, cols, True)
            slope = tanh_gelu_slope(stream[start + 64 : start + 256, cols].astype(F32))
            total = g_in[start : start + 192, cols] + slope * act_grad
            g_in[start : start + 192, cols] = total
            out_bf[start : start + 192, cols] = zero_outside(total, flags, start, 64, 384).astype(BF)
    out[...] = g_in[64:320, :]


def on_core(kernel, outs, scratch, count, flops, *operands):
    def place(v):
        if v.ndim == 4:
            return pl.BlockSpec(memory_space=pltpu.HBM)
        if v.ndim == 1:
            return pl.BlockSpec(memory_space=pltpu.SMEM)
        return pl.BlockSpec(memory_space=pltpu.VMEM)

    return pl.pallas_call(
        kernel,
        out_shape=[jax.ShapeDtypeStruct((rows, 768), kind) for rows, kind in outs],
        in_specs=[place(v) for v in operands],
        out_specs=[pl.BlockSpec(memory_space=pltpu.VMEM) for _ in outs],
        scratch_shapes=[pltpu.VMEM((rows, 768), kind) for rows, kind in scratch]
        + [pltpu.VMEM((count, 3, 768, 768), BF), pltpu.SemaphoreType.DMA((count, 3))],
        compiler_params=pltpu.CompilerParams(vmem_limit_bytes=36 * 2**20),
        cost_estimate=pl.CostEstimate(
            flops=flops, bytes_accessed=count * 3 * 768 * 768 * 2, transcendentals=0
        ),
    )(*operands)


def smooth(values):
    return jax.nn.gelu(values, approximate=True)


def pick(blocks, place, axis=0):
    return lax.dynamic_index_in_dim(blocks, place, axis, keepdims=False)


def give(part, bit, route, outer=1):
    rows, lanes = part.shape
    halves = part.reshape(outer, 2, rows // (2 * outer), lanes)
    return send(pick(halves, 1 - bit, 1), route)


def take(part, got, bit):
    rows, lanes = part.shape
    outer = got.shape[0]
    halves = part.reshape(outer, 2, rows // (2 * outer), lanes)
    total = pick(halves, bit, 1).astype(F32) + got.astype(F32)
    return total.astype(BF).reshape(rows // 2, lanes)


def plane_sum(blocks):
    got = lax.all_to_all(blocks, ("z", "y"), 0, 0, tiled=True)
    return jnp.sum(got.astype(F32), axis=0).astype(BF)


def last_sum(near, rest):
    total = sum(send(near, last_hop(0, m)).astype(F32) for m in range(2))
    more = sum(send(rest, last_hop(1, m)).astype(F32) for m in range(2))
    return total[: rest.shape[0]] + more, total[rest.shape[0] :]


def per_device(trunk, conv_weight, head_weight, targets, error_mask, upweight):
    _, positions, channels = trunk.shape
    xl, z, y, c, xh = (lax.axis_index(axis) for axis in AXES)
    bins_all = positions * lax.axis_size(AXES)
    bin_weight = jnp.where(error_mask == 1, upweight, 1).astype(F32).reshape(positions, 1)
    weight_part = jnp.sum(bin_weight)
    first, last = (xl + z + y + c == 0), (xl == 1) & (z == 3) & (y == 3) & (c == 1)

    def conv_back(rows, weights, d, count):
        total = jnp.dot(rows[d : d + count], weights[1].T, preferred_element_type=F32)
        total = total + jnp.dot(
            rows[2 * d : 2 * d + count], weights[0].T, preferred_element_type=F32
        )
        return total + jnp.dot(rows[:count], weights[2].T, preferred_element_type=F32)

    def through(v, grad):
        return jax.vjp(smooth, v.astype(F32))[1](grad)[0]

    flags = jnp.stack([first, last]).astype(jnp.int32)
    tap_flops = 2 * 768 * 768 * 3
    before, after = edges(trunk[0], 192, c)
    act0, wide1, act1, stream2, act2 = on_core(
        front_kernel,
        [(384, BF), (512, BF), (512, BF), (256, BF), (256, BF)],
        [(640, BF), (640, BF)],
        2,
        768 * tap_flops,
        *(flags, before, trunk[0], after, conv_weight),
    )
    before, after = edges(act2, 256, c)
    far_acts = [send(act0, CORE), send(act1, CORE)]
    before, far_acts[0], far_acts[1] = lax.optimization_barrier((before, *far_acts))
    act2, stream = on_core(
        middle_kernel,
        [(768, BF), (256, BF)],
        [],
        1,
        256 * tap_flops,
        *(before, act2, after, stream2, conv_weight),
    )
    far_acts.append(send(act2, CORE))
    padded_acts = [act0, act1, act2]
    logits = jnp.dot(stream, head_weight, preferred_element_type=F32)
    predicted = jax.nn.softplus(logits)
    slope = jax.nn.sigmoid(logits)
    counts = targets[0].astype(F32)
    partial_loss = jnp.sum(bin_weight * (predicted - counts * jnp.log(predicted)))
    logit_grad = (bin_weight * (1.0 - counts / predicted) * slope).astype(BF)
    logit_grad, far_acts[2] = lax.optimization_barrier((logit_grad, far_acts[2]))
    lanes = lax.broadcasted_iota(jnp.int32, (1, 1408), 1)
    spare = lanes - 1344 * (1 - c)

    def with_scalars(v, scalars):
        for n, s in enumerate(scalars):
            inside = (spare >= 32 * n) & (spare < 32 * n + 32)
            v = jnp.where(inside, s * (1.0 + (spare - 32 * n).astype(F32) / 32), v)
        return v

    def halves(v, width):
        low, high = v[:, :width], v[:, v.shape[1] - width :]
        return jnp.where(c == 0, low, high), jnp.where(c == 0, high, low)

    def pair_dot(a, b, far_a, far_b):
        return jnp.dot(a.T, b, preferred_element_type=F32) + jnp.dot(
            far_a.T, far_b, preferred_element_type=F32
        )

    g_top = jnp.dot(logit_grad, head_weight.T, preferred_element_type=F32)
    gb2 = g_top.astype(BF)
    gb2, logit_grad, partial_loss, far_stream = lax.optimization_barrier(
        (gb2, logit_grad, partial_loss, send(stream, CORE))
    )
    near, far = halves(logit_grad, 1408)
    scal = jnp.stack([weight_part, partial_loss])
    scal = scal + send(scal, CORE)
    head_half = pair_dot(stream, near, far_stream, send(far, CORE))
    head_half = with_scalars(head_half, (scal[0], scal[1])).astype(BF)
    head_got = give(head_half, xl, ALONG_X)

    def conv_grad(layer, grad_bf):
        d = BASE_DILATION * 2**layer
        padded = padded_acts[layer]
        far_padded = far_acts[layer]
        near, far = halves(grad_bf, 384)
        far = send(far, CORE)
        return jnp.concatenate(
            [
                pair_dot(padded[rows], near, far_padded[rows], far).astype(BF)
                for rows in (slice(tap * d, tap * d + positions) for tap in range(3))
            ],
            axis=0,
        )

    before, after = edges(gb2, 256, c)
    half2 = conv_grad(2, gb2)
    got2 = give(half2, z // 2, ALONG_Z[3], 2)
    before, head_half, half2 = lax.optimization_barrier((before, head_half, half2))
    g2, gb1 = on_core(
        back2_kernel,
        [(256, F32), (256, BF)],
        [(768, BF)],
        1,
        256 * tap_flops,
        *(before, gb2, after, stream2, g_top, conv_weight),
    )
    before, after = edges(gb1, 192, c)
    half1 = conv_grad(1, gb1)
    half1 = half1.reshape(2, 4, 288, 384)
    got1 = send(jnp.stack([pick(half1, z ^ 1, 1), pick(half1, z ^ 2, 1)]), ALONG_Z[1])
    before, half1 = lax.optimization_barrier((before, half1))
    g1, gb0 = on_core(
        back1_kernel,
        [(256, F32), (384, BF)],
        [(640, BF), (384, F32)],
        1,
        384 * tap_flops,
        *(flags, before, gb1, after, wide1, g2, conv_weight),
    )
    part2_z = take(half2, got2, z // 2)
    got2 = give(part2_z, z % 2, ALONG_Z[1], 2)
    gb0, part2_z = lax.optimization_barrier((gb0, part2_z))
    half0 = conv_grad(0, gb0[64:320])
    got0 = give(half0, xl, ALONG_X)
    half0, half1, head_half, part2_z = lax.optimization_barrier((half0, half1, head_half, part2_z))
    head_x = take(head_half, head_got, xl)
    head_x, half1, part2_z = lax.optimization_barrier((head_x, half1, part2_z))
    head_plane = plane_sum(head_x.reshape(16, 24, 1408))
    keep1 = jnp.stack([pick(half1, z, 1), pick(half1, z ^ 3, 1)])
    keep1 = (keep1.astype(F32) + got1.astype(F32)).astype(BF)
    got1 = send(keep1[1], ALONG_Z[3])
    keep1, gb0 = lax.optimization_barrier((keep1, gb0))
    g0 = g1 + through(trunk[0], conv_back(gb0, conv_weight[0], 64, 256))
    g0, half0, head_plane = lax.optimization_barrier((g0, half0, head_plane))
    plane0 = plane_sum(take(half0, got0, xl).reshape(16, 72, 384))
    part1 = (keep1[0].astype(F32) + got1.astype(F32)).astype(BF)
    part2 = take(part2_z, got2, z % 2)
    early = jnp.concatenate([part1.reshape(2, 4, 72, 384), part2.reshape(2, 4, 72, 384)], axis=2)
    got = [send(pick(early, y ^ k, 1), ALONG_Y[k]) for k in (1, 3, 2)]
    early = sum((g.astype(F32) for g in got), pick(early, y, 1).astype(F32)).astype(BF)
    head_plane = jnp.pad(head_plane, ((0, 0), (0, 128)))
    near = [pick(early, xl), plane0] + [head_plane[:, 384 * k : 384 * k + 384] for k in range(4)]
    early, late = last_sum(jnp.concatenate(near, axis=0), pick(early, 1 - xl))
    conv_sum, head_sum = [late[:72], early[:72], early[72:]], late[72:]

    def own(v):
        half = v.shape[0] // 2
        return jnp.where(c == 0, v[:half], v[half:])

    conv_total = jnp.stack([own(v) for v in conv_sum])
    head_total = jnp.concatenate([own(head_sum[24 * k : 24 * k + 24]) for k in range(4)], axis=1)
    low = head_total[:, :1344]
    high = head_total[:, 64:1408]
    row = head_total[0]
    found = jnp.where(xh == 0, row[1344:1408], row[:64])
    weight_sum = jnp.sum(found[:32]) / 47.5
    loss_sum = jnp.sum(found[32:]) / 47.5
    factor = bins_all / weight_sum
    loss = loss_sum / (OUTPUT_TRACKS * weight_sum)
    return (
        loss,
        conv_total * factor,
        jnp.where(xh == 0, low, high) * factor,
        (g0 * factor).astype(BF)[None],
    )


def solution(mesh):
    parts = Mesh(mesh.devices.reshape(2, 4, 4, 2, 2), ("xl", "z", "y", "c", "xh"))
    seq = ("xl", "z", "y", "c")
    return jax.shard_map(
        per_device,
        mesh=parts,
        in_specs=(
            P("xh", seq, None),
            P(),
            P(),
            P("xh", seq, None),
            P("xh", seq),
            P("xh", seq),
        ),
        out_specs=(P(), P(None, seq, "xh"), P(seq, "xh"), P("xh", seq, None)),
        check_vma=False,
    )
```

```python
import jax
import jax.numpy as jnp
from jax import lax
from jax.experimental import pallas as pl
from jax.experimental.pallas import tpu as pltpu
from jax.sharding import Mesh
from jax.sharding import PartitionSpec as P

OUTPUT_TRACKS = 2688
LAYERS = 3
BASE_DILATION = 64
AXES = ("xl", "z", "y", "c", "xh")
BF = jnp.bfloat16
F32 = jnp.float32


def perm_of(target):
    pairs = []
    for xl in range(2):
        for z in range(4):
            for y in range(4):
                for c in range(2):
                    for xh in range(2):
                        goal = target(xl, z, y, c, xh)
                        pairs.append((lin(xl, z, y, c, xh), lin(*goal)))
    return pairs


def lin(xl, z, y, c, xh):
    return (((xl * 4 + z) * 4 + y) * 2 + c) * 2 + xh


CORE = perm_of(lambda xl, z, y, c, xh: (xl, z, y, 1 - c, xh))
NEXT_CHIP = [(a * 2 + xh, (a + 1) * 2 + xh) for a in range(1, 63, 2) for xh in range(2)]
NEXT_CHIP = NEXT_CHIP + [(b, a) for a, b in NEXT_CHIP]
ALONG_X = perm_of(lambda xl, z, y, c, xh: (1 - xl, z, y, c, xh))
ALONG_Y = [perm_of(lambda xl, z, y, c, xh, k=k: (xl, z, y ^ k, c, xh)) for k in range(4)]
ALONG_Z = [perm_of(lambda xl, z, y, c, xh, k=k: (xl, z ^ k, y, c, xh)) for k in range(4)]


def last_hop(dx, m):
    return perm_of(lambda xl, z, y, c, xh: (xl ^ dx, z, y, xh ^ m, c))


def send(v, pairs):
    return lax.ppermute(v, AXES, pairs)


def edges(shard, width, c):
    first, last = shard[:width], shard[shard.shape[0] - width :]
    if width == shard.shape[0]:
        inner = outer = shard
    else:
        inner = jnp.where(c == 0, last, first)
        outer = jnp.where(c == 0, first, last)
    outer = send(outer, NEXT_CHIP)
    inner = send(inner, CORE)
    return jnp.where(c == 0, outer, inner), jnp.where(c == 0, inner, outer)


def copies_in(w_ref, scratch, sems, layers):
    order = [(n, layer, tap) for n, layer in enumerate(layers) for tap in (1, 0, 2)]
    made = {
        (n, tap): pltpu.make_async_copy(
            w_ref.at[layer, tap], scratch.at[n, tap], sems.at[n, tap]
        )
        for n, layer, tap in order
    }
    for n, layer, tap in order:
        made[n, tap].start()
    return made


def three_taps(rows, weights, n, d, start, count, cols, back):
    total = None
    for tap in (1, 0, 2):
        at = start + (2 - tap if back else tap) * d
        left = rows[at : at + count, :]
        if back:
            part = lax.dot_general(
                left, weights[n, tap, cols, :], (((1,), (1,)), ((), ())), preferred_element_type=F32
            )
        else:
            part = jnp.dot(left, weights[n, tap, :, cols], preferred_element_type=F32)
        total = part if total is None else total + part
    return total


def tanh_gelu(x):
    return 0.5 * x * (1.0 + jnp.tanh(0.7978845608028654 * (x + 0.044715 * x * x * x)))


def tanh_gelu_slope(x):
    t = jnp.tanh(0.7978845608028654 * (x + 0.044715 * x * x * x))
    return 0.5 * (1.0 + t) + 0.5 * x * (1.0 - t * t) * 0.7978845608028654 * (
        1.0 + 0.134145 * x * x
    )


def zero_outside(v, flags, start, width, total):
    row = start + lax.broadcasted_iota(jnp.int32, v.shape, 0)
    out = ((flags[0] == 1) & (row < width)) | ((flags[1] == 1) & (row >= total - width))
    return jnp.where(out, 0.0, v)


COLS = [slice(256 * n, 256 * n + 256) for n in range(3)]


def front_kernel(flags, before, own, after, w_ref, act0, wide1, act1, stream2, act2, wide, acts, weights, sems):
    made = copies_in(w_ref, weights, sems, (0, 1))
    wide[0:192, :] = before[...]
    wide[192:448, :] = own[...]
    wide[448:640, :] = after[...]
    for r in range(0, 640, 64):
        acts[r : r + 64, :] = tanh_gelu(wide[r : r + 64, :].astype(F32)).astype(BF)
    act0[...] = acts[128:512, :]
    for tap in (1, 0, 2):
        made[0, tap].wait()
    for start in (0, 256):
        for cols in COLS:
            conv = three_taps(acts, weights, 0, 64, start, 256, cols, False)
            stream = (wide[start + 64 : start + 320, cols].astype(F32) + conv).astype(BF)
            stream = zero_outside(stream.astype(F32), flags, start, 128, 512)
            wide1[start : start + 256, cols] = stream.astype(BF)
            act1[start : start + 256, cols] = tanh_gelu(stream).astype(BF)
    for tap in (1, 0, 2):
        made[1, tap].wait()
    for cols in COLS:
        conv = three_taps(act1, weights, 1, 128, 0, 256, cols, False)
        stream = (wide1[128:384, cols].astype(F32) + conv).astype(BF)
        stream2[:, cols] = stream
        act2[:, cols] = tanh_gelu(stream.astype(F32)).astype(BF)


def middle_kernel(before, own, after, stream, w_ref, padded, out, weights, sems):
    made = copies_in(w_ref, weights, sems, (2,))
    padded[0:256, :] = before[...]
    padded[256:512, :] = own[...]
    padded[512:768, :] = after[...]
    for tap in (1, 0, 2):
        made[0, tap].wait()
    for cols in COLS:
        conv = three_taps(padded, weights, 0, 256, 0, 256, cols, False)
        out[:, cols] = (stream[:, cols].astype(F32) + conv).astype(BF)


def back2_kernel(before, own, after, stream, grad, w_ref, out, out_bf, wide, weights, sems):
    made = copies_in(w_ref, weights, sems, (2,))
    wide[0:256, :] = before[...]
    wide[256:512, :] = own[...]
    wide[512:768, :] = after[...]
    for tap in (1, 0, 2):
        made[0, tap].wait()
    for cols in COLS:
        act_grad = three_taps(wide, weights, 0, 256, 0, 256, cols, True)
        total = grad[:, cols] + tanh_gelu_slope(stream[:, cols].astype(F32)) * act_grad
        out[:, cols] = total
        out_bf[:, cols] = total.astype(BF)


def on_core(kernel, outs, scratch, count, flops, *operands):
    def place(v):
        if v.ndim == 4:
            return pl.BlockSpec(memory_space=pltpu.HBM)
        if v.ndim == 1:
            return pl.BlockSpec(memory_space=pltpu.SMEM)
        return pl.BlockSpec(memory_space=pltpu.VMEM)

    return pl.pallas_call(
        kernel,
        out_shape=[jax.ShapeDtypeStruct((rows, 768), kind) for rows, kind in outs],
        in_specs=[place(v) for v in operands],
        out_specs=[pl.BlockSpec(memory_space=pltpu.VMEM) for _ in outs],
        scratch_shapes=[pltpu.VMEM((rows, 768), kind) for rows, kind in scratch]
        + [pltpu.VMEM((count, 3, 768, 768), BF), pltpu.SemaphoreType.DMA((count, 3))],
        compiler_params=pltpu.CompilerParams(vmem_limit_bytes=36 * 2**20),
        cost_estimate=pl.CostEstimate(
            flops=flops, bytes_accessed=count * 3 * 768 * 768 * 2, transcendentals=0
        ),
    )(*operands)


def smooth(values):
    return jax.nn.gelu(values, approximate=True)


def pick(blocks, place, axis=0):
    return lax.dynamic_index_in_dim(blocks, place, axis, keepdims=False)


def give(part, bit, route, outer=1):
    rows, lanes = part.shape
    halves = part.reshape(outer, 2, rows // (2 * outer), lanes)
    return send(pick(halves, 1 - bit, 1), route)


def take(part, got, bit):
    rows, lanes = part.shape
    outer = got.shape[0]
    halves = part.reshape(outer, 2, rows // (2 * outer), lanes)
    total = pick(halves, bit, 1).astype(F32) + got.astype(F32)
    return total.astype(BF).reshape(rows // 2, lanes)


def plane_sum(blocks):
    got = lax.all_to_all(blocks, ("z", "y"), 0, 0, tiled=True)
    return jnp.sum(got.astype(F32), axis=0).astype(BF)


def last_sum(near, rest):
    total = sum(send(near, last_hop(0, m)).astype(F32) for m in range(2))
    more = sum(send(rest, last_hop(1, m)).astype(F32) for m in range(2))
    return total[: rest.shape[0]] + more, total[rest.shape[0] :]


def per_device(trunk, conv_weight, head_weight, targets, error_mask, upweight):
    _, positions, channels = trunk.shape
    xl, z, y, c, xh = (lax.axis_index(axis) for axis in AXES)
    bins_all = positions * lax.axis_size(AXES)
    bin_weight = jnp.where(error_mask == 1, upweight, 1).astype(F32).reshape(positions, 1)
    weight_part = jnp.sum(bin_weight)
    first, last = (xl + z + y + c == 0), (xl == 1) & (z == 3) & (y == 3) & (c == 1)

    def inside(v, width):
        row = lax.broadcasted_iota(jnp.int32, (v.shape[0], 1), 0)
        out = (first & (row < width)) | (last & (row >= v.shape[0] - width))
        return jnp.where(out, jnp.zeros_like(v), v)

    def conv_back(rows, weights, d, count):
        total = jnp.dot(rows[d : d + count], weights[1].T, preferred_element_type=F32)
        total = total + jnp.dot(
            rows[2 * d : 2 * d + count], weights[0].T, preferred_element_type=F32
        )
        return total + jnp.dot(rows[:count], weights[2].T, preferred_element_type=F32)

    def through(v, grad):
        return jax.vjp(smooth, v.astype(F32))[1](grad)[0]

    flags = jnp.stack([first, last]).astype(jnp.int32)
    tap_flops = 2 * 768 * 768 * 3
    before, after = edges(trunk[0], 192, c)
    act0, wide1, act1, stream2, act2 = on_core(
        front_kernel,
        [(384, BF), (512, BF), (512, BF), (256, BF), (256, BF)],
        [(640, BF), (640, BF)],
        2,
        768 * tap_flops,
        *(flags, before, trunk[0], after, conv_weight),
    )
    before, after = edges(act2, 256, c)
    far_acts = [send(act0, CORE), send(act1, CORE)]
    before, far_acts[0], far_acts[1] = lax.optimization_barrier((before, *far_acts))
    act2, stream = on_core(
        middle_kernel,
        [(768, BF), (256, BF)],
        [],
        1,
        256 * tap_flops,
        *(before, act2, after, stream2, conv_weight),
    )
    far_acts.append(send(act2, CORE))
    padded_acts = [act0, act1, act2]
    logits = jnp.dot(stream, head_weight, preferred_element_type=F32)
    predicted = jax.nn.softplus(logits)
    slope = jax.nn.sigmoid(logits)
    counts = targets[0].astype(F32)
    partial_loss = jnp.sum(bin_weight * (predicted - counts * jnp.log(predicted)))
    logit_grad = (bin_weight * (1.0 - counts / predicted) * slope).astype(BF)
    logit_grad, far_acts[2] = lax.optimization_barrier((logit_grad, far_acts[2]))
    lanes = lax.broadcasted_iota(jnp.int32, (1, 1408), 1)
    spare = lanes - 1344 * (1 - c)

    def with_scalars(v, scalars):
        for n, s in enumerate(scalars):
            inside = (spare >= 32 * n) & (spare < 32 * n + 32)
            v = jnp.where(inside, s * (1.0 + (spare - 32 * n).astype(F32) / 32), v)
        return v

    def halves(v, width):
        low, high = v[:, :width], v[:, v.shape[1] - width :]
        return jnp.where(c == 0, low, high), jnp.where(c == 0, high, low)

    def pair_dot(a, b, far_a, far_b):
        return jnp.dot(a.T, b, preferred_element_type=F32) + jnp.dot(
            far_a.T, far_b, preferred_element_type=F32
        )

    g_top = jnp.dot(logit_grad, head_weight.T, preferred_element_type=F32)
    gb2 = g_top.astype(BF)
    gb2, logit_grad, partial_loss, far_stream = lax.optimization_barrier(
        (gb2, logit_grad, partial_loss, send(stream, CORE))
    )
    near, far = halves(logit_grad, 1408)
    scal = jnp.stack([weight_part, partial_loss])
    scal = scal + send(scal, CORE)
    head_half = pair_dot(stream, near, far_stream, send(far, CORE))
    head_half = with_scalars(head_half, (scal[0], scal[1])).astype(BF)
    head_got = give(head_half, xl, ALONG_X)

    def conv_grad(layer, grad_bf):
        d = BASE_DILATION * 2**layer
        padded = padded_acts[layer]
        far_padded = far_acts[layer]
        near, far = halves(grad_bf, 384)
        far = send(far, CORE)
        return jnp.concatenate(
            [
                pair_dot(padded[rows], near, far_padded[rows], far).astype(BF)
                for rows in (slice(tap * d, tap * d + positions) for tap in range(3))
            ],
            axis=0,
        )

    before, after = edges(gb2, 256, c)
    half2 = conv_grad(2, gb2)
    got2 = give(half2, z // 2, ALONG_Z[3], 2)
    before, head_half, half2 = lax.optimization_barrier((before, head_half, half2))
    g2, gb1 = on_core(
        back2_kernel,
        [(256, F32), (256, BF)],
        [(768, BF)],
        1,
        256 * tap_flops,
        *(before, gb2, after, stream2, g_top, conv_weight),
    )
    before, after = edges(gb1, 192, c)
    half1 = conv_grad(1, gb1)
    half1 = half1.reshape(2, 4, 288, 384)
    got1 = send(jnp.stack([pick(half1, z ^ 1, 1), pick(half1, z ^ 2, 1)]), ALONG_Z[1])
    before, half1 = lax.optimization_barrier((before, half1))
    wide = jnp.concatenate([before, gb1, after], axis=0)
    g_in = jnp.concatenate([before[128:].astype(F32), g2, after[:64].astype(F32)], axis=0)
    g1 = g_in + through(wide1[64:448], conv_back(wide, conv_weight[1], 128, 384))
    gb0 = inside(g1.astype(BF), 64)
    g1 = g1[64:320]
    part2_z = take(half2, got2, z // 2)
    got2 = give(part2_z, z % 2, ALONG_Z[1], 2)
    gb0, part2_z = lax.optimization_barrier((gb0, part2_z))
    half0 = conv_grad(0, gb0[64:320])
    got0 = give(half0, xl, ALONG_X)
    half0, half1, head_half, part2_z = lax.optimization_barrier((half0, half1, head_half, part2_z))
    head_x = take(head_half, head_got, xl)
    head_x, half1, part2_z = lax.optimization_barrier((head_x, half1, part2_z))
    head_plane = plane_sum(head_x.reshape(16, 24, 1408))
    g0 = g1 + through(trunk[0], conv_back(gb0, conv_weight[0], 64, 256))
    g0, half1, part2_z = lax.optimization_barrier((g0, half1, part2_z))
    keep1 = jnp.stack([pick(half1, z, 1), pick(half1, z ^ 3, 1)])
    keep1 = (keep1.astype(F32) + got1.astype(F32)).astype(BF)
    got1 = send(keep1[1], ALONG_Z[3])
    part2 = take(part2_z, got2, z % 2)
    part1 = (keep1[0].astype(F32) + got1.astype(F32)).astype(BF)
    early = jnp.concatenate([part1.reshape(2, 4, 72, 384), part2.reshape(2, 4, 72, 384)], axis=2)
    got = [send(pick(early, y ^ k, 1), ALONG_Y[k]) for k in (1, 3, 2)]
    half0, head_plane, early = lax.optimization_barrier((half0, head_plane, early))
    plane0 = plane_sum(take(half0, got0, xl).reshape(16, 72, 384))
    early = sum((g.astype(F32) for g in got), pick(early, y, 1).astype(F32)).astype(BF)
    head_plane = jnp.pad(head_plane, ((0, 0), (0, 128)))
    near = [pick(early, xl), plane0] + [head_plane[:, 384 * k : 384 * k + 384] for k in range(4)]
    early, late = last_sum(jnp.concatenate(near, axis=0), pick(early, 1 - xl))
    conv_sum, head_sum = [late[:72], early[:72], early[72:]], late[72:]

    def own(v):
        half = v.shape[0] // 2
        return jnp.where(c == 0, v[:half], v[half:])

    conv_total = jnp.stack([own(v) for v in conv_sum])
    head_total = jnp.concatenate([own(head_sum[24 * k : 24 * k + 24]) for k in range(4)], axis=1)
    low = head_total[:, :1344]
    high = head_total[:, 64:1408]
    row = head_total[0]
    found = jnp.where(xh == 0, row[1344:1408], row[:64])
    weight_sum = jnp.sum(found[:32]) / 47.5
    loss_sum = jnp.sum(found[32:]) / 47.5
    factor = bins_all / weight_sum
    loss = loss_sum / (OUTPUT_TRACKS * weight_sum)
    return (
        loss,
        conv_total * factor,
        jnp.where(xh == 0, low, high) * factor,
        (g0 * factor).astype(BF)[None],
    )


def solution(mesh):
    parts = Mesh(mesh.devices.reshape(2, 4, 4, 2, 2), ("xl", "z", "y", "c", "xh"))
    seq = ("xl", "z", "y", "c")
    return jax.shard_map(
        per_device,
        mesh=parts,
        in_specs=(
            P("xh", seq, None),
            P(),
            P(),
            P("xh", seq, None),
            P("xh", seq),
            P("xh", seq),
        ),
        out_specs=(P(), P(None, seq, "xh"), P(seq, "xh"), P("xh", seq, None)),
        check_vma=False,
    )
```

```python
import jax
import jax.numpy as jnp
from jax import lax
from jax.experimental import pallas as pl
from jax.experimental.pallas import tpu as pltpu
from jax.sharding import Mesh
from jax.sharding import PartitionSpec as P

OUTPUT_TRACKS = 2688
LAYERS = 3
BASE_DILATION = 64
AXES = ("xl", "z", "y", "c", "xh")
BF = jnp.bfloat16
F32 = jnp.float32


def perm_of(target):
    pairs = []
    for xl in range(2):
        for z in range(4):
            for y in range(4):
                for c in range(2):
                    for xh in range(2):
                        goal = target(xl, z, y, c, xh)
                        pairs.append((lin(xl, z, y, c, xh), lin(*goal)))
    return pairs


def lin(xl, z, y, c, xh):
    return (((xl * 4 + z) * 4 + y) * 2 + c) * 2 + xh


CORE = perm_of(lambda xl, z, y, c, xh: (xl, z, y, 1 - c, xh))
NEXT_CHIP = [(a * 2 + xh, (a + 1) * 2 + xh) for a in range(1, 63, 2) for xh in range(2)]
NEXT_CHIP = NEXT_CHIP + [(b, a) for a, b in NEXT_CHIP]
ALONG_X = perm_of(lambda xl, z, y, c, xh: (1 - xl, z, y, c, xh))
ALONG_Y = [perm_of(lambda xl, z, y, c, xh, k=k: (xl, z, y ^ k, c, xh)) for k in range(4)]
ALONG_Z = [perm_of(lambda xl, z, y, c, xh, k=k: (xl, z ^ k, y, c, xh)) for k in range(4)]


def last_hop(dx, m):
    return perm_of(lambda xl, z, y, c, xh: (xl ^ dx, z, y, xh ^ m, c))


def send(v, pairs):
    return lax.ppermute(v, AXES, pairs)


def edges(shard, width, c):
    first, last = shard[:width], shard[shard.shape[0] - width :]
    if width == shard.shape[0]:
        inner = outer = shard
    else:
        inner = jnp.where(c == 0, last, first)
        outer = jnp.where(c == 0, first, last)
    outer = send(outer, NEXT_CHIP)
    inner = send(inner, CORE)
    return jnp.where(c == 0, outer, inner), jnp.where(c == 0, inner, outer)


def copies_in(w_ref, scratch, sems, layers):
    order = [(n, layer, tap) for n, layer in enumerate(layers) for tap in (1, 0, 2)]
    made = {
        (n, tap): pltpu.make_async_copy(
            w_ref.at[layer, tap], scratch.at[n, tap], sems.at[n, tap]
        )
        for n, layer, tap in order
    }
    for n, layer, tap in order:
        made[n, tap].start()
    return made


def three_taps(rows, weights, n, d, start, count, cols, back):
    total = None
    for tap in (1, 0, 2):
        at = start + (2 - tap if back else tap) * d
        left = rows[at : at + count, :]
        if back:
            part = lax.dot_general(
                left, weights[n, tap, cols, :], (((1,), (1,)), ((), ())), preferred_element_type=F32
            )
        else:
            part = jnp.dot(left, weights[n, tap, :, cols], preferred_element_type=F32)
        total = part if total is None else total + part
    return total


def tanh_gelu(x):
    return 0.5 * x * (1.0 + jnp.tanh(0.7978845608028654 * (x + 0.044715 * x * x * x)))


def tanh_gelu_slope(x):
    t = jnp.tanh(0.7978845608028654 * (x + 0.044715 * x * x * x))
    return 0.5 * (1.0 + t) + 0.5 * x * (1.0 - t * t) * 0.7978845608028654 * (
        1.0 + 0.134145 * x * x
    )


def zero_outside(v, flags, start, width, total):
    row = start + lax.broadcasted_iota(jnp.int32, v.shape, 0)
    out = ((flags[0] == 1) & (row < width)) | ((flags[1] == 1) & (row >= total - width))
    return jnp.where(out, 0.0, v)


COLS = [slice(256 * n, 256 * n + 256) for n in range(3)]


def front_kernel(flags, before, own, after, w_ref, act0, wide1, act1, stream2, act2, wide, acts, weights, sems):
    made = copies_in(w_ref, weights, sems, (0, 1))
    wide[0:192, :] = before[...]
    wide[192:448, :] = own[...]
    wide[448:640, :] = after[...]
    for r in range(0, 640, 64):
        acts[r : r + 64, :] = tanh_gelu(wide[r : r + 64, :].astype(F32)).astype(BF)
    act0[...] = acts[128:512, :]
    for tap in (1, 0, 2):
        made[0, tap].wait()
    for start in (0, 256):
        for cols in COLS:
            conv = three_taps(acts, weights, 0, 64, start, 256, cols, False)
            stream = (wide[start + 64 : start + 320, cols].astype(F32) + conv).astype(BF)
            stream = zero_outside(stream.astype(F32), flags, start, 128, 512)
            wide1[start : start + 256, cols] = stream.astype(BF)
            act1[start : start + 256, cols] = tanh_gelu(stream).astype(BF)
    for tap in (1, 0, 2):
        made[1, tap].wait()
    for cols in COLS:
        conv = three_taps(act1, weights, 1, 128, 0, 256, cols, False)
        stream = (wide1[128:384, cols].astype(F32) + conv).astype(BF)
        stream2[:, cols] = stream
        act2[:, cols] = tanh_gelu(stream.astype(F32)).astype(BF)


def middle_kernel(before, own, after, stream, w_ref, padded, out, weights, sems):
    made = copies_in(w_ref, weights, sems, (2,))
    padded[0:256, :] = before[...]
    padded[256:512, :] = own[...]
    padded[512:768, :] = after[...]
    for tap in (1, 0, 2):
        made[0, tap].wait()
    for cols in COLS:
        conv = three_taps(padded, weights, 0, 256, 0, 256, cols, False)
        out[:, cols] = (stream[:, cols].astype(F32) + conv).astype(BF)


def back2_kernel(before, own, after, stream, grad, w_ref, out, out_bf, wide, weights, sems):
    made = copies_in(w_ref, weights, sems, (2,))
    wide[0:256, :] = before[...]
    wide[256:512, :] = own[...]
    wide[512:768, :] = after[...]
    for tap in (1, 0, 2):
        made[0, tap].wait()
    for cols in COLS:
        act_grad = three_taps(wide, weights, 0, 256, 0, 256, cols, True)
        total = grad[:, cols] + tanh_gelu_slope(stream[:, cols].astype(F32)) * act_grad
        out[:, cols] = total
        out_bf[:, cols] = total.astype(BF)


def on_core(kernel, outs, scratch, count, flops, *operands):
    def place(v):
        if v.ndim == 4:
            return pl.BlockSpec(memory_space=pltpu.HBM)
        if v.ndim == 1:
            return pl.BlockSpec(memory_space=pltpu.SMEM)
        return pl.BlockSpec(memory_space=pltpu.VMEM)

    return pl.pallas_call(
        kernel,
        out_shape=[jax.ShapeDtypeStruct((rows, 768), kind) for rows, kind in outs],
        in_specs=[place(v) for v in operands],
        out_specs=[pl.BlockSpec(memory_space=pltpu.VMEM) for _ in outs],
        scratch_shapes=[pltpu.VMEM((rows, 768), kind) for rows, kind in scratch]
        + [pltpu.VMEM((count, 3, 768, 768), BF), pltpu.SemaphoreType.DMA((count, 3))],
        compiler_params=pltpu.CompilerParams(vmem_limit_bytes=56 * 2**20),
        cost_estimate=pl.CostEstimate(
            flops=flops, bytes_accessed=count * 3 * 768 * 768 * 2, transcendentals=0
        ),
    )(*operands)


def smooth(values):
    return jax.nn.gelu(values, approximate=True)


def pick(blocks, place, axis=0):
    return lax.dynamic_index_in_dim(blocks, place, axis, keepdims=False)


def give(part, bit, route, outer=1):
    rows, lanes = part.shape
    halves = part.reshape(outer, 2, rows // (2 * outer), lanes)
    return send(pick(halves, 1 - bit, 1), route)


def take(part, got, bit):
    rows, lanes = part.shape
    outer = got.shape[0]
    halves = part.reshape(outer, 2, rows // (2 * outer), lanes)
    total = pick(halves, bit, 1).astype(F32) + got.astype(F32)
    return total.astype(BF).reshape(rows // 2, lanes)


def plane_sum(blocks):
    got = lax.all_to_all(blocks, ("z", "y"), 0, 0, tiled=True)
    return jnp.sum(got.astype(F32), axis=0).astype(BF)


def last_sum(near, rest):
    total = sum(send(near, last_hop(0, m)).astype(F32) for m in range(2))
    more = sum(send(rest, last_hop(1, m)).astype(F32) for m in range(2))
    return total[: rest.shape[0]] + more, total[rest.shape[0] :]


def per_device(trunk, conv_weight, head_weight, targets, error_mask, upweight):
    _, positions, channels = trunk.shape
    xl, z, y, c, xh = (lax.axis_index(axis) for axis in AXES)
    bins_all = positions * lax.axis_size(AXES)
    bin_weight = jnp.where(error_mask == 1, upweight, 1).astype(F32).reshape(positions, 1)
    weight_part = jnp.sum(bin_weight)
    first, last = (xl + z + y + c == 0), (xl == 1) & (z == 3) & (y == 3) & (c == 1)

    def inside(v, width):
        row = lax.broadcasted_iota(jnp.int32, (v.shape[0], 1), 0)
        out = (first & (row < width)) | (last & (row >= v.shape[0] - width))
        return jnp.where(out, jnp.zeros_like(v), v)

    def conv_back(rows, weights, d, count):
        total = jnp.dot(rows[d : d + count], weights[1].T, preferred_element_type=F32)
        total = total + jnp.dot(
            rows[2 * d : 2 * d + count], weights[0].T, preferred_element_type=F32
        )
        return total + jnp.dot(rows[:count], weights[2].T, preferred_element_type=F32)

    def through(v, grad):
        return jax.vjp(smooth, v.astype(F32))[1](grad)[0]

    flags = jnp.stack([first, last]).astype(jnp.int32)
    tap_flops = 2 * 768 * 768 * 3
    before, after = edges(trunk[0], 192, c)
    act0, wide1, act1, stream2, act2 = on_core(
        front_kernel,
        [(384, BF), (512, BF), (512, BF), (256, BF), (256, BF)],
        [(640, BF), (640, BF)],
        2,
        768 * tap_flops,
        *(flags, before, trunk[0], after, conv_weight),
    )
    before, after = edges(act2, 256, c)
    far_acts = [send(act0, CORE), send(act1, CORE)]
    before, far_acts[0], far_acts[1] = lax.optimization_barrier((before, *far_acts))
    act2, stream = on_core(
        middle_kernel,
        [(768, BF), (256, BF)],
        [],
        1,
        256 * tap_flops,
        *(before, act2, after, stream2, conv_weight),
    )
    far_acts.append(send(act2, CORE))
    padded_acts = [act0, act1, act2]
    logits = jnp.dot(stream, head_weight, preferred_element_type=F32)
    predicted = jax.nn.softplus(logits)
    slope = jax.nn.sigmoid(logits)
    counts = targets[0].astype(F32)
    partial_loss = jnp.sum(bin_weight * (predicted - counts * jnp.log(predicted)))
    logit_grad = (bin_weight * (1.0 - counts / predicted) * slope).astype(BF)
    logit_grad, far_acts[2] = lax.optimization_barrier((logit_grad, far_acts[2]))
    lanes = lax.broadcasted_iota(jnp.int32, (1, 1408), 1)
    spare = lanes - 1344 * (1 - c)

    def with_scalars(v, scalars):
        for n, s in enumerate(scalars):
            inside = (spare >= 32 * n) & (spare < 32 * n + 32)
            v = jnp.where(inside, s * (1.0 + (spare - 32 * n).astype(F32) / 32), v)
        return v

    def halves(v, width):
        low, high = v[:, :width], v[:, v.shape[1] - width :]
        return jnp.where(c == 0, low, high), jnp.where(c == 0, high, low)

    def pair_dot(a, b, far_a, far_b):
        return jnp.dot(a.T, b, preferred_element_type=F32) + jnp.dot(
            far_a.T, far_b, preferred_element_type=F32
        )

    g_top = jnp.dot(logit_grad, head_weight.T, preferred_element_type=F32)
    gb2 = g_top.astype(BF)
    gb2, logit_grad, partial_loss, far_stream = lax.optimization_barrier(
        (gb2, logit_grad, partial_loss, send(stream, CORE))
    )
    near, far = halves(logit_grad, 1408)
    scal = jnp.stack([weight_part, partial_loss])
    scal = scal + send(scal, CORE)
    head_half = pair_dot(stream, near, far_stream, send(far, CORE))
    head_half = with_scalars(head_half, (scal[0], scal[1])).astype(BF)
    head_got = give(head_half, xl, ALONG_X)

    def conv_grad(layer, grad_bf):
        d = BASE_DILATION * 2**layer
        padded = padded_acts[layer]
        far_padded = far_acts[layer]
        near, far = halves(grad_bf, 384)
        far = send(far, CORE)
        return jnp.concatenate(
            [
                pair_dot(padded[rows], near, far_padded[rows], far).astype(BF)
                for rows in (slice(tap * d, tap * d + positions) for tap in range(3))
            ],
            axis=0,
        )

    before, after = edges(gb2, 256, c)
    half2 = conv_grad(2, gb2)
    got2 = give(half2, z // 2, ALONG_Z[3], 2)
    before, head_half, half2 = lax.optimization_barrier((before, head_half, half2))
    g2, gb1 = on_core(
        back2_kernel,
        [(256, F32), (256, BF)],
        [(768, BF)],
        1,
        256 * tap_flops,
        *(before, gb2, after, stream2, g_top, conv_weight),
    )
    before, after = edges(gb1, 192, c)
    half1 = conv_grad(1, gb1)
    half1 = half1.reshape(2, 4, 288, 384)
    got1 = send(jnp.stack([pick(half1, z ^ 1, 1), pick(half1, z ^ 2, 1)]), ALONG_Z[1])
    before, half1 = lax.optimization_barrier((before, half1))
    wide = jnp.concatenate([before, gb1, after], axis=0)
    g_in = jnp.concatenate([before[128:].astype(F32), g2, after[:64].astype(F32)], axis=0)
    g1 = g_in + through(wide1[64:448], conv_back(wide, conv_weight[1], 128, 384))
    gb0 = inside(g1.astype(BF), 64)
    g1 = g1[64:320]
    part2_z = take(half2, got2, z // 2)
    got2 = give(part2_z, z % 2, ALONG_Z[1], 2)
    gb0, part2_z = lax.optimization_barrier((gb0, part2_z))
    half0 = conv_grad(0, gb0[64:320])
    got0 = give(half0, xl, ALONG_X)
    half0, half1, head_half, part2_z = lax.optimization_barrier((half0, half1, head_half, part2_z))
    head_x = take(head_half, head_got, xl)
    head_x, half1, part2_z = lax.optimization_barrier((head_x, half1, part2_z))
    head_plane = plane_sum(head_x.reshape(16, 24, 1408))
    g0 = g1 + through(trunk[0], conv_back(gb0, conv_weight[0], 64, 256))
    g0, half1, part2_z = lax.optimization_barrier((g0, half1, part2_z))
    keep1 = jnp.stack([pick(half1, z, 1), pick(half1, z ^ 3, 1)])
    keep1 = (keep1.astype(F32) + got1.astype(F32)).astype(BF)
    got1 = send(keep1[1], ALONG_Z[3])
    part2 = take(part2_z, got2, z % 2)
    half0, head_plane = lax.optimization_barrier((half0, head_plane))
    half0 = take(half0, got0, xl)
    half0, keep1 = lax.optimization_barrier((half0, keep1))
    plane0 = plane_sum(half0.reshape(16, 72, 384))
    part1 = (keep1[0].astype(F32) + got1.astype(F32)).astype(BF)
    early = jnp.concatenate([part1.reshape(2, 4, 72, 384), part2.reshape(2, 4, 72, 384)], axis=2)
    got = [send(pick(early, y ^ k, 1), ALONG_Y[k]) for k in (1, 3, 2)]
    early = sum((g.astype(F32) for g in got), pick(early, y, 1).astype(F32)).astype(BF)
    head_plane = jnp.pad(head_plane, ((0, 0), (0, 128)))
    head_plane = jnp.concatenate(
        [head_plane[:, 384 * k : 384 * k + 384] for k in range(4)], axis=0
    )
    head_sum = sum(send(head_plane, last_hop(0, m)).astype(F32) for m in range(2))
    early, late = last_sum(
        jnp.concatenate([pick(early, xl), plane0], axis=0), pick(early, 1 - xl)
    )
    conv_sum = [late, early[:72], early[72:]]

    def own(v):
        half = v.shape[0] // 2
        return jnp.where(c == 0, v[:half], v[half:])

    conv_total = jnp.stack([own(v) for v in conv_sum])
    head_total = jnp.concatenate([own(head_sum[24 * k : 24 * k + 24]) for k in range(4)], axis=1)
    low = head_total[:, :1344]
    high = head_total[:, 64:1408]
    row = head_total[0]
    found = jnp.where(xh == 0, row[1344:1408], row[:64])
    weight_sum = jnp.sum(found[:32]) / 47.5
    loss_sum = jnp.sum(found[32:]) / 47.5
    factor = bins_all / weight_sum
    loss = loss_sum / (OUTPUT_TRACKS * weight_sum)
    return (
        loss,
        conv_total * factor,
        jnp.where(xh == 0, low, high) * factor,
        (g0 * factor).astype(BF)[None],
    )


def solution(mesh):
    parts = Mesh(mesh.devices.reshape(2, 4, 4, 2, 2), ("xl", "z", "y", "c", "xh"))
    seq = ("xl", "z", "y", "c")
    return jax.shard_map(
        per_device,
        mesh=parts,
        in_specs=(
            P("xh", seq, None),
            P(),
            P(),
            P("xh", seq, None),
            P("xh", seq),
            P("xh", seq),
        ),
        out_specs=(P(), P(None, seq, "xh"), P(seq, "xh"), P("xh", seq, None)),
        check_vma=False,
    )
```

```python
import jax
import jax.numpy as jnp
from jax import lax
from jax.experimental import pallas as pl
from jax.experimental.pallas import tpu as pltpu
from jax.sharding import Mesh
from jax.sharding import PartitionSpec as P

OUTPUT_TRACKS = 2688
LAYERS = 3
BASE_DILATION = 64
AXES = ("xl", "z", "y", "c", "xh")
BF = jnp.bfloat16
F32 = jnp.float32


def perm_of(target):
    pairs = []
    for xl in range(2):
        for z in range(4):
            for y in range(4):
                for c in range(2):
                    for xh in range(2):
                        goal = target(xl, z, y, c, xh)
                        pairs.append((lin(xl, z, y, c, xh), lin(*goal)))
    return pairs


def lin(xl, z, y, c, xh):
    return (((xl * 4 + z) * 4 + y) * 2 + c) * 2 + xh


CORE = perm_of(lambda xl, z, y, c, xh: (xl, z, y, 1 - c, xh))
NEXT_CHIP = [(a * 2 + xh, (a + 1) * 2 + xh) for a in range(1, 63, 2) for xh in range(2)]
NEXT_CHIP = NEXT_CHIP + [(b, a) for a, b in NEXT_CHIP]
ALONG_X = perm_of(lambda xl, z, y, c, xh: (1 - xl, z, y, c, xh))
ALONG_Y = [perm_of(lambda xl, z, y, c, xh, k=k: (xl, z, y ^ k, c, xh)) for k in range(4)]
ALONG_Z = [perm_of(lambda xl, z, y, c, xh, k=k: (xl, z ^ k, y, c, xh)) for k in range(4)]


def last_hop(dx, m):
    return perm_of(lambda xl, z, y, c, xh: (xl ^ dx, z, y, xh ^ m, c))


def send(v, pairs):
    return lax.ppermute(v, AXES, pairs)


def edges(shard, width, c):
    first, last = shard[:width], shard[shard.shape[0] - width :]
    if width == shard.shape[0]:
        inner = outer = shard
    else:
        inner = jnp.where(c == 0, last, first)
        outer = jnp.where(c == 0, first, last)
    outer = send(outer, NEXT_CHIP)
    inner = send(inner, CORE)
    return jnp.where(c == 0, outer, inner), jnp.where(c == 0, inner, outer)


def copies_in(w_ref, scratch, sems, layers):
    made = []
    for n, layer in enumerate(layers):
        made.append([])
        for tap in (1, 0, 2):
            for part in range(4):
                rows = slice(192 * part, 192 * part + 192)
                copy = pltpu.make_async_copy(
                    w_ref.at[layer, tap, rows, :],
                    scratch.at[n, tap, rows, :],
                    sems.at[n, tap, part],
                )
                copy.start()
                made[n].append(copy)
    return made


def three_taps(rows, weights, n, d, start, count, cols, back):
    total = None
    for tap in (1, 0, 2):
        at = start + (2 - tap if back else tap) * d
        left = rows[at : at + count, :]
        if back:
            part = lax.dot_general(
                left, weights[n, tap, cols, :], (((1,), (1,)), ((), ())), preferred_element_type=F32
            )
        else:
            part = jnp.dot(left, weights[n, tap, :, cols], preferred_element_type=F32)
        total = part if total is None else total + part
    return total


def tanh_gelu(x):
    return 0.5 * x * (1.0 + jnp.tanh(0.7978845608028654 * (x + 0.044715 * x * x * x)))


def tanh_gelu_slope(x):
    t = jnp.tanh(0.7978845608028654 * (x + 0.044715 * x * x * x))
    return 0.5 * (1.0 + t) + 0.5 * x * (1.0 - t * t) * 0.7978845608028654 * (
        1.0 + 0.134145 * x * x
    )


def zero_outside(v, flags, start, width, total):
    row = start + lax.broadcasted_iota(jnp.int32, v.shape, 0)
    out = ((flags[0] == 1) & (row < width)) | ((flags[1] == 1) & (row >= total - width))
    return jnp.where(out, 0.0, v)


COLS = [slice(256 * n, 256 * n + 256) for n in range(3)]


def front_kernel(flags, before, own, after, w_ref, act0, wide1, act1, stream2, act2, wide, acts, weights, sems):
    made = copies_in(w_ref, weights, sems, (0, 1))
    wide[0:192, :] = before[...]
    wide[192:448, :] = own[...]
    wide[448:640, :] = after[...]
    for r in range(0, 640, 64):
        acts[r : r + 64, :] = tanh_gelu(wide[r : r + 64, :].astype(F32)).astype(BF)
    act0[...] = acts[128:512, :]
    for copy in made[0]:
        copy.wait()
    for start in (0, 256):
        for cols in COLS:
            conv = three_taps(acts, weights, 0, 64, start, 256, cols, False)
            stream = (wide[start + 64 : start + 320, cols].astype(F32) + conv).astype(BF)
            stream = zero_outside(stream.astype(F32), flags, start, 128, 512)
            wide1[start : start + 256, cols] = stream.astype(BF)
            act1[start : start + 256, cols] = tanh_gelu(stream).astype(BF)
    for copy in made[1]:
        copy.wait()
    for cols in COLS:
        conv = three_taps(act1, weights, 1, 128, 0, 256, cols, False)
        stream = (wide1[128:384, cols].astype(F32) + conv).astype(BF)
        stream2[:, cols] = stream
        act2[:, cols] = tanh_gelu(stream.astype(F32)).astype(BF)


def middle_kernel(before, own, after, stream, w_ref, padded, out, weights, sems):
    made = copies_in(w_ref, weights, sems, (2,))
    padded[0:256, :] = before[...]
    padded[256:512, :] = own[...]
    padded[512:768, :] = after[...]
    for copy in made[0]:
        copy.wait()
    for cols in COLS:
        conv = three_taps(padded, weights, 0, 256, 0, 256, cols, False)
        out[:, cols] = (stream[:, cols].astype(F32) + conv).astype(BF)


def back2_kernel(before, own, after, stream, grad, w_ref, out, out_bf, wide, weights, sems):
    made = copies_in(w_ref, weights, sems, (2,))
    wide[0:256, :] = before[...]
    wide[256:512, :] = own[...]
    wide[512:768, :] = after[...]
    for copy in made[0]:
        copy.wait()
    for cols in COLS:
        act_grad = three_taps(wide, weights, 0, 256, 0, 256, cols, True)
        total = grad[:, cols] + tanh_gelu_slope(stream[:, cols].astype(F32)) * act_grad
        out[:, cols] = total
        out_bf[:, cols] = total.astype(BF)


def on_core(kernel, room, outs, scratch, count, flops, *operands):
    def place(v):
        if v.ndim == 4:
            return pl.BlockSpec(memory_space=pltpu.HBM)
        if v.ndim == 1:
            return pl.BlockSpec(memory_space=pltpu.SMEM)
        return pl.BlockSpec(memory_space=pltpu.VMEM)

    return pl.pallas_call(
        kernel,
        out_shape=[jax.ShapeDtypeStruct((rows, 768), kind) for rows, kind in outs],
        in_specs=[place(v) for v in operands],
        out_specs=[pl.BlockSpec(memory_space=pltpu.VMEM) for _ in outs],
        scratch_shapes=[pltpu.VMEM((rows, 768), kind) for rows, kind in scratch]
        + [pltpu.VMEM((count, 3, 768, 768), BF), pltpu.SemaphoreType.DMA((count, 3, 4))],
        compiler_params=pltpu.CompilerParams(vmem_limit_bytes=room * 2**20),
        cost_estimate=pl.CostEstimate(
            flops=flops, bytes_accessed=count * 3 * 768 * 768 * 2, transcendentals=0
        ),
    )(*operands)


def smooth(values):
    return jax.nn.gelu(values, approximate=True)


def pick(blocks, place, axis=0):
    return lax.dynamic_index_in_dim(blocks, place, axis, keepdims=False)


def give(part, bit, route, outer=1):
    rows, lanes = part.shape
    halves = part.reshape(outer, 2, rows // (2 * outer), lanes)
    return send(pick(halves, 1 - bit, 1), route)


def take(part, got, bit):
    rows, lanes = part.shape
    outer = got.shape[0]
    halves = part.reshape(outer, 2, rows // (2 * outer), lanes)
    total = pick(halves, bit, 1).astype(F32) + got.astype(F32)
    return total.astype(BF).reshape(rows // 2, lanes)


def last_sum(near, rest):
    total = sum(send(near, last_hop(0, m)).astype(F32) for m in range(2))
    more = sum(send(rest, last_hop(1, m)).astype(F32) for m in range(2))
    return total[: rest.shape[0]] + more, total[rest.shape[0] :]


def per_device(trunk, conv_weight, head_weight, targets, error_mask, upweight):
    _, positions, channels = trunk.shape
    xl, z, y, c, xh = (lax.axis_index(axis) for axis in AXES)
    bins_all = positions * lax.axis_size(AXES)
    bin_weight = jnp.where(error_mask == 1, upweight, 1).astype(F32).reshape(positions, 1)
    weight_part = jnp.sum(bin_weight)
    first, last = (xl + z + y + c == 0), (xl == 1) & (z == 3) & (y == 3) & (c == 1)

    def inside(v, width):
        row = lax.broadcasted_iota(jnp.int32, (v.shape[0], 1), 0)
        out = (first & (row < width)) | (last & (row >= v.shape[0] - width))
        return jnp.where(out, jnp.zeros_like(v), v)

    def conv_back(rows, weights, d, count):
        total = jnp.dot(rows[d : d + count], weights[1].T, preferred_element_type=F32)
        total = total + jnp.dot(
            rows[2 * d : 2 * d + count], weights[0].T, preferred_element_type=F32
        )
        return total + jnp.dot(rows[:count], weights[2].T, preferred_element_type=F32)

    def through(v, grad):
        return jax.vjp(smooth, v.astype(F32))[1](grad)[0]

    flags = jnp.stack([first, last]).astype(jnp.int32)
    tap_flops = 2 * 768 * 768 * 3
    before, after = edges(trunk[0], 192, c)
    act0, wide1, act1, stream2, act2 = on_core(
        front_kernel,
        56,
        [(384, BF), (512, BF), (512, BF), (256, BF), (256, BF)],
        [(640, BF), (640, BF)],
        2,
        768 * tap_flops,
        *(flags, before, trunk[0], after, conv_weight),
    )
    before, after = edges(act2, 256, c)
    far_acts = [send(act0, CORE), send(act1, CORE)]
    before, far_acts[0], far_acts[1] = lax.optimization_barrier((before, *far_acts))
    act2, stream = on_core(
        middle_kernel,
        46,
        [(768, BF), (256, BF)],
        [],
        1,
        256 * tap_flops,
        *(before, act2, after, stream2, conv_weight),
    )
    far_acts.append(send(act2, CORE))
    padded_acts = [act0, act1, act2]
    logits = jnp.dot(stream, head_weight, preferred_element_type=F32)
    predicted = jax.nn.softplus(logits)
    slope = jax.nn.sigmoid(logits)
    counts = targets[0].astype(F32)
    partial_loss = jnp.sum(bin_weight * (predicted - counts * jnp.log(predicted)))
    logit_grad = (bin_weight * (1.0 - counts / predicted) * slope).astype(BF)
    logit_grad, far_acts[2] = lax.optimization_barrier((logit_grad, far_acts[2]))
    lanes = lax.broadcasted_iota(jnp.int32, (1, 1408), 1)
    spare = lanes - 1344 * (1 - c)

    def with_scalars(v, scalars):
        for n, s in enumerate(scalars):
            inside = (spare >= 32 * n) & (spare < 32 * n + 32)
            v = jnp.where(inside, s * (1.0 + (spare - 32 * n).astype(F32) / 32), v)
        return v

    def halves(v, width):
        low, high = v[:, :width], v[:, v.shape[1] - width :]
        return jnp.where(c == 0, low, high), jnp.where(c == 0, high, low)

    def pair_dot(a, b, far_a, far_b):
        return jnp.dot(a.T, b, preferred_element_type=F32) + jnp.dot(
            far_a.T, far_b, preferred_element_type=F32
        )

    g_top = jnp.dot(logit_grad, head_weight.T, preferred_element_type=F32)
    gb2 = g_top.astype(BF)
    gb2, logit_grad, partial_loss, far_stream = lax.optimization_barrier(
        (gb2, logit_grad, partial_loss, send(stream, CORE))
    )
    near, far = halves(logit_grad, 1408)
    scal = jnp.stack([weight_part, partial_loss])
    scal = scal + send(scal, CORE)
    head_half = pair_dot(stream, near, far_stream, send(far, CORE))
    head_half = with_scalars(head_half, (scal[0], scal[1])).astype(BF)
    head_got = give(head_half, xl, ALONG_X)

    def conv_grad(layer, grad_bf):
        d = BASE_DILATION * 2**layer
        padded = padded_acts[layer]
        far_padded = far_acts[layer]
        near, far = halves(grad_bf, 384)
        far = send(far, CORE)
        return jnp.concatenate(
            [
                pair_dot(padded[rows], near, far_padded[rows], far).astype(BF)
                for rows in (slice(tap * d, tap * d + positions) for tap in range(3))
            ],
            axis=0,
        )

    before, after = edges(gb2, 256, c)
    half2 = conv_grad(2, gb2)
    got2 = give(half2, z // 2, ALONG_Z[3], 2)
    before, head_half, half2 = lax.optimization_barrier((before, head_half, half2))
    g2, gb1 = on_core(
        back2_kernel,
        46,
        [(256, F32), (256, BF)],
        [(768, BF)],
        1,
        256 * tap_flops,
        *(before, gb2, after, stream2, g_top, conv_weight),
    )
    before, after = edges(gb1, 192, c)
    half1 = conv_grad(1, gb1)
    half1 = half1.reshape(2, 4, 288, 384)
    got1 = send(jnp.stack([pick(half1, z ^ 1, 1), pick(half1, z ^ 2, 1)]), ALONG_Z[1])
    before, half1 = lax.optimization_barrier((before, half1))
    wide = jnp.concatenate([before, gb1, after], axis=0)
    g_in = jnp.concatenate([before[128:].astype(F32), g2, after[:64].astype(F32)], axis=0)
    g1 = g_in + through(wide1[64:448], conv_back(wide, conv_weight[1], 128, 384))
    gb0 = inside(g1.astype(BF), 64)
    g1 = g1[64:320]
    part2_z = take(half2, got2, z // 2)
    got2 = give(part2_z, z % 2, ALONG_Z[1], 2)
    gb0, part2_z = lax.optimization_barrier((gb0, part2_z))
    half0 = conv_grad(0, gb0[64:320])
    got0 = give(half0, xl, ALONG_X)
    half0, half1, head_half, part2_z = lax.optimization_barrier((half0, half1, head_half, part2_z))
    head_x = take(head_half, head_got, xl)
    head_x, half1, part2_z = lax.optimization_barrier((head_x, half1, part2_z))
    head_plane = lax.all_to_all(head_x.reshape(16, 24, 1408), ("z", "y"), 0, 0, tiled=True)
    g0 = g1 + through(trunk[0], conv_back(gb0, conv_weight[0], 64, 256))
    g0, half1, part2_z = lax.optimization_barrier((g0, half1, part2_z))
    keep1 = jnp.stack([pick(half1, z, 1), pick(half1, z ^ 3, 1)])
    keep1 = (keep1.astype(F32) + got1.astype(F32)).astype(BF)
    got1 = send(keep1[1], ALONG_Z[3])
    part2 = take(part2_z, got2, z % 2)
    half0 = take(half0, got0, xl).reshape(4, 288, 384)
    got0 = [send(pick(half0, z ^ k), ALONG_Z[k]) for k in (1, 3, 2)]
    half0, keep1 = lax.optimization_barrier((half0, keep1))
    part1 = (keep1[0].astype(F32) + got1.astype(F32)).astype(BF)
    part0 = sum((g.astype(F32) for g in got0), pick(half0, z).astype(F32)).astype(BF)
    early = jnp.concatenate(
        [v.reshape(-1, 4, 72, 384) for v in (part1[0], part1[1], part2[:288], part2[288:], part0)],
        axis=0,
    )
    got = [send(pick(early, y ^ k, 1), ALONG_Y[k]) for k in (1, 3, 2)]
    head_plane = jnp.sum(head_plane.astype(F32), axis=0).astype(BF)
    head_plane = jnp.pad(head_plane, ((0, 0), (0, 128)))
    head_plane = jnp.concatenate(
        [head_plane[:, 384 * k : 384 * k + 384] for k in range(4)], axis=0
    )
    head_sum = sum(send(head_plane, last_hop(0, m)).astype(F32) for m in range(2))
    early, head_sum = lax.optimization_barrier((early, head_sum))
    early = sum((g.astype(F32) for g in got), pick(early, y, 1).astype(F32)).astype(BF)
    both = early[:4].reshape(2, 2, 72, 384)
    near = jnp.concatenate([pick(both, xl, 1), early[4:]], axis=0).reshape(216, 384)
    early, late = last_sum(near, pick(both, 1 - xl, 1).reshape(144, 384))
    conv_sum = [late, early[:72], early[72:]]

    def own(v):
        half = v.shape[0] // 2
        return jnp.where(c == 0, v[:half], v[half:])

    conv_total = jnp.stack([own(v) for v in conv_sum])
    head_total = jnp.concatenate([own(head_sum[24 * k : 24 * k + 24]) for k in range(4)], axis=1)
    low = head_total[:, :1344]
    high = head_total[:, 64:1408]
    row = head_total[0]
    found = jnp.where(xh == 0, row[1344:1408], row[:64])
    weight_sum = jnp.sum(found[:32]) / 47.5
    loss_sum = jnp.sum(found[32:]) / 47.5
    factor = bins_all / weight_sum
    loss = loss_sum / (OUTPUT_TRACKS * weight_sum)
    return (
        loss,
        conv_total * factor,
        jnp.where(xh == 0, low, high) * factor,
        (g0 * factor).astype(BF)[None],
    )


def solution(mesh):
    parts = Mesh(mesh.devices.reshape(2, 4, 4, 2, 2), ("xl", "z", "y", "c", "xh"))
    seq = ("xl", "z", "y", "c")
    return jax.shard_map(
        per_device,
        mesh=parts,
        in_specs=(
            P("xh", seq, None),
            P(),
            P(),
            P("xh", seq, None),
            P("xh", seq),
            P("xh", seq),
        ),
        out_specs=(P(), P(None, seq, "xh"), P(seq, "xh"), P("xh", seq, None)),
        check_vma=False,
    )
```

```python
import jax
import jax.numpy as jnp
from jax import lax
from jax.experimental import pallas as pl
from jax.experimental.pallas import tpu as pltpu
from jax.sharding import Mesh
from jax.sharding import PartitionSpec as P

OUTPUT_TRACKS = 2688
LAYERS = 3
BASE_DILATION = 64
AXES = ("xl", "z", "y", "c", "xh")
BF = jnp.bfloat16
F32 = jnp.float32


def perm_of(target):
    pairs = []
    for xl in range(2):
        for z in range(4):
            for y in range(4):
                for c in range(2):
                    for xh in range(2):
                        goal = target(xl, z, y, c, xh)
                        pairs.append((lin(xl, z, y, c, xh), lin(*goal)))
    return pairs


def lin(xl, z, y, c, xh):
    return (((xl * 4 + z) * 4 + y) * 2 + c) * 2 + xh


CORE = perm_of(lambda xl, z, y, c, xh: (xl, z, y, 1 - c, xh))
NEXT_CHIP = [(a * 2 + xh, (a + 1) * 2 + xh) for a in range(1, 63, 2) for xh in range(2)]
NEXT_CHIP = NEXT_CHIP + [(b, a) for a, b in NEXT_CHIP]
ALONG_X = perm_of(lambda xl, z, y, c, xh: (1 - xl, z, y, c, xh))
ALONG_Y = [perm_of(lambda xl, z, y, c, xh, k=k: (xl, z, y ^ k, c, xh)) for k in range(4)]
ALONG_Z = [perm_of(lambda xl, z, y, c, xh, k=k: (xl, z ^ k, y, c, xh)) for k in range(4)]


def last_hop(dx, m):
    return perm_of(lambda xl, z, y, c, xh: (xl ^ dx, z, y, xh ^ m, c))


def send(v, pairs):
    return lax.ppermute(v, AXES, pairs)


def edges(shard, width, c):
    first, last = shard[:width], shard[shard.shape[0] - width :]
    if width == shard.shape[0]:
        inner = outer = shard
    else:
        inner = jnp.where(c == 0, last, first)
        outer = jnp.where(c == 0, first, last)
    outer = send(outer, NEXT_CHIP)
    inner = send(inner, CORE)
    return jnp.where(c == 0, outer, inner), jnp.where(c == 0, inner, outer)


def copies_in(w_ref, scratch, sems, layers):
    made = []
    for n, layer in enumerate(layers):
        made.append([])
        for tap in (1, 0, 2):
            for part in range(4):
                rows = slice(192 * part, 192 * part + 192)
                copy = pltpu.make_async_copy(
                    w_ref.at[layer, tap, rows, :],
                    scratch.at[n, tap, rows, :],
                    sems.at[n, tap, part],
                )
                copy.start()
                made[n].append(copy)
    return made


def three_taps(rows, weights, n, d, start, count, cols, back):
    total = None
    for tap in (1, 0, 2):
        at = start + (2 - tap if back else tap) * d
        left = rows[at : at + count, :]
        if back:
            part = lax.dot_general(
                left, weights[n, tap, cols, :], (((1,), (1,)), ((), ())), preferred_element_type=F32
            )
        else:
            part = jnp.dot(left, weights[n, tap, :, cols], preferred_element_type=F32)
        total = part if total is None else total + part
    return total


def tanh_gelu(x):
    return 0.5 * x * (1.0 + jnp.tanh(0.7978845608028654 * (x + 0.044715 * x * x * x)))


def tanh_gelu_slope(x):
    t = jnp.tanh(0.7978845608028654 * (x + 0.044715 * x * x * x))
    return 0.5 * (1.0 + t) + 0.5 * x * (1.0 - t * t) * 0.7978845608028654 * (
        1.0 + 0.134145 * x * x
    )


def zero_outside(v, flags, start, width, total):
    row = start + lax.broadcasted_iota(jnp.int32, v.shape, 0)
    out = ((flags[0] == 1) & (row < width)) | ((flags[1] == 1) & (row >= total - width))
    return jnp.where(out, 0.0, v)


COLS = [slice(256 * n, 256 * n + 256) for n in range(3)]


def front_kernel(flags, before, own, after, w_ref, act0, wide1, act1, stream2, act2, wide, acts, weights, sems):
    made = copies_in(w_ref, weights, sems, (0, 1))
    wide[0:192, :] = before[...]
    wide[192:448, :] = own[...]
    wide[448:640, :] = after[...]
    for r in range(0, 640, 64):
        acts[r : r + 64, :] = tanh_gelu(wide[r : r + 64, :].astype(F32)).astype(BF)
    act0[...] = acts[128:512, :]
    for copy in made[0]:
        copy.wait()
    for start in (0, 256):
        for cols in COLS:
            conv = three_taps(acts, weights, 0, 64, start, 256, cols, False)
            stream = (wide[start + 64 : start + 320, cols].astype(F32) + conv).astype(BF)
            stream = zero_outside(stream.astype(F32), flags, start, 128, 512)
            wide1[start : start + 256, cols] = stream.astype(BF)
            act1[start : start + 256, cols] = tanh_gelu(stream).astype(BF)
    for copy in made[1]:
        copy.wait()
    for cols in COLS:
        conv = three_taps(act1, weights, 1, 128, 0, 256, cols, False)
        stream = (wide1[128:384, cols].astype(F32) + conv).astype(BF)
        stream2[:, cols] = stream
        act2[:, cols] = tanh_gelu(stream.astype(F32)).astype(BF)


def middle_kernel(before, own, after, stream, w_ref, padded, out, weights, sems):
    made = copies_in(w_ref, weights, sems, (2,))
    padded[0:256, :] = before[...]
    padded[256:512, :] = own[...]
    padded[512:768, :] = after[...]
    for copy in made[0]:
        copy.wait()
    for cols in COLS:
        conv = three_taps(padded, weights, 0, 256, 0, 256, cols, False)
        out[:, cols] = (stream[:, cols].astype(F32) + conv).astype(BF)


def back2_kernel(before, own, after, stream, grad, w_ref, out, out_bf, wide, weights, sems):
    made = copies_in(w_ref, weights, sems, (2,))
    wide[0:256, :] = before[...]
    wide[256:512, :] = own[...]
    wide[512:768, :] = after[...]
    for copy in made[0]:
        copy.wait()
    for cols in COLS:
        act_grad = three_taps(wide, weights, 0, 256, 0, 256, cols, True)
        total = grad[:, cols] + tanh_gelu_slope(stream[:, cols].astype(F32)) * act_grad
        out[:, cols] = total
        out_bf[:, cols] = total.astype(BF)


def on_core(kernel, room, outs, scratch, count, flops, *operands):
    def place(v):
        if v.ndim == 4:
            return pl.BlockSpec(memory_space=pltpu.HBM)
        if v.ndim == 1:
            return pl.BlockSpec(memory_space=pltpu.SMEM)
        return pl.BlockSpec(memory_space=pltpu.VMEM)

    return pl.pallas_call(
        kernel,
        out_shape=[jax.ShapeDtypeStruct((rows, 768), kind) for rows, kind in outs],
        in_specs=[place(v) for v in operands],
        out_specs=[pl.BlockSpec(memory_space=pltpu.VMEM) for _ in outs],
        scratch_shapes=[pltpu.VMEM((rows, 768), kind) for rows, kind in scratch]
        + [pltpu.VMEM((count, 3, 768, 768), BF), pltpu.SemaphoreType.DMA((count, 3, 4))],
        compiler_params=pltpu.CompilerParams(vmem_limit_bytes=room * 2**20),
        cost_estimate=pl.CostEstimate(
            flops=flops, bytes_accessed=count * 3 * 768 * 768 * 2, transcendentals=0
        ),
    )(*operands)


def smooth(values):
    return jax.nn.gelu(values, approximate=True)


def pick(blocks, place, axis=0):
    return lax.dynamic_index_in_dim(blocks, place, axis, keepdims=False)


def give(part, bit, route, outer=1):
    rows, lanes = part.shape
    halves = part.reshape(outer, 2, rows // (2 * outer), lanes)
    return send(pick(halves, 1 - bit, 1), route)


def take(part, got, bit):
    rows, lanes = part.shape
    outer = got.shape[0]
    halves = part.reshape(outer, 2, rows // (2 * outer), lanes)
    total = pick(halves, bit, 1).astype(F32) + got.astype(F32)
    return total.astype(BF).reshape(rows // 2, lanes)


def last_sum(near, rest):
    total = sum(send(near, last_hop(0, m)).astype(F32) for m in range(2))
    more = sum(send(rest, last_hop(1, m)).astype(F32) for m in range(2))
    return total[: rest.shape[0]] + more, total[rest.shape[0] :]


def per_device(trunk, conv_weight, head_weight, targets, error_mask, upweight):
    _, positions, channels = trunk.shape
    xl, z, y, c, xh = (lax.axis_index(axis) for axis in AXES)
    bins_all = positions * lax.axis_size(AXES)
    bin_weight = jnp.where(error_mask == 1, upweight, 1).astype(F32).reshape(positions, 1)
    weight_part = jnp.sum(bin_weight)
    first, last = (xl + z + y + c == 0), (xl == 1) & (z == 3) & (y == 3) & (c == 1)

    def inside(v, width):
        row = lax.broadcasted_iota(jnp.int32, (v.shape[0], 1), 0)
        out = (first & (row < width)) | (last & (row >= v.shape[0] - width))
        return jnp.where(out, jnp.zeros_like(v), v)

    def conv_back(rows, weights, d, count):
        total = jnp.dot(rows[d : d + count], weights[1].T, preferred_element_type=F32)
        total = total + jnp.dot(
            rows[2 * d : 2 * d + count], weights[0].T, preferred_element_type=F32
        )
        return total + jnp.dot(rows[:count], weights[2].T, preferred_element_type=F32)

    def through(v, grad):
        return jax.vjp(smooth, v.astype(F32))[1](grad)[0]

    flags = jnp.stack([first, last]).astype(jnp.int32)
    tap_flops = 2 * 768 * 768 * 3
    before, after = edges(trunk[0], 192, c)
    act0, wide1, act1, stream2, act2 = on_core(
        front_kernel,
        56,
        [(384, BF), (512, BF), (512, BF), (256, BF), (256, BF)],
        [(640, BF), (640, BF)],
        2,
        768 * tap_flops,
        *(flags, before, trunk[0], after, conv_weight),
    )
    before, after = edges(act2, 256, c)
    far_acts = [send(act0, CORE), send(act1, CORE)]
    before, far_acts[0], far_acts[1] = lax.optimization_barrier((before, *far_acts))
    act2, stream = on_core(
        middle_kernel,
        46,
        [(768, BF), (256, BF)],
        [],
        1,
        256 * tap_flops,
        *(before, act2, after, stream2, conv_weight),
    )
    far_acts.append(send(act2, CORE))
    padded_acts = [act0, act1, act2]
    logits = jnp.dot(stream, head_weight, preferred_element_type=F32)
    predicted = jax.nn.softplus(logits)
    slope = jax.nn.sigmoid(logits)
    counts = targets[0].astype(F32)
    partial_loss = jnp.sum(bin_weight * (predicted - counts * jnp.log(predicted)))
    logit_grad = (bin_weight * (1.0 - counts / predicted) * slope).astype(BF)
    logit_grad, far_acts[2] = lax.optimization_barrier((logit_grad, far_acts[2]))
    lanes = lax.broadcasted_iota(jnp.int32, (1, 1408), 1)
    spare = lanes - 1344 * (1 - c)

    def with_scalars(v, scalars):
        mark = jnp.where(spare < 32, scalars[0], scalars[1]) * (1.0 + (spare % 32).astype(F32) / 32)
        v = jnp.where((spare >= 0) & (spare < 64), mark, v)
        return v

    def halves(v, width):
        low, high = v[:, :width], v[:, v.shape[1] - width :]
        return jnp.where(c == 0, low, high), jnp.where(c == 0, high, low)

    def pair_dot(a, b, far_a, far_b):
        return jnp.dot(a.T, b, preferred_element_type=F32) + jnp.dot(
            far_a.T, far_b, preferred_element_type=F32
        )

    g_top = jnp.dot(logit_grad, head_weight.T, preferred_element_type=F32)
    gb2 = g_top.astype(BF)
    gb2, logit_grad, partial_loss, far_stream = lax.optimization_barrier(
        (gb2, logit_grad, partial_loss, send(stream, CORE))
    )
    near, far = halves(logit_grad, 1408)
    lane = lax.broadcasted_iota(jnp.int32, (1, 128), 1)
    scal = jnp.where(lane == 0, weight_part, partial_loss)
    scal = scal + send(scal, CORE)
    head_half = pair_dot(stream, near, far_stream, send(far, CORE))
    head_half = with_scalars(head_half, (scal[0, 0], scal[0, 1])).astype(BF)
    head_got = give(head_half, xl, ALONG_X)

    def conv_grad(layer, grad_bf):
        d = BASE_DILATION * 2**layer
        padded = padded_acts[layer]
        far_padded = far_acts[layer]
        near, far = halves(grad_bf, 384)
        far = send(far, CORE)
        return jnp.concatenate(
            [
                pair_dot(padded[rows], near, far_padded[rows], far).astype(BF)
                for rows in (slice(tap * d, tap * d + positions) for tap in range(3))
            ],
            axis=0,
        )

    before, after = edges(gb2, 256, c)
    half2 = conv_grad(2, gb2)
    got2 = give(half2, z // 2, ALONG_Z[3], 2)
    before, head_half, half2 = lax.optimization_barrier((before, head_half, half2))
    g2, gb1 = on_core(
        back2_kernel,
        46,
        [(256, F32), (256, BF)],
        [(768, BF)],
        1,
        256 * tap_flops,
        *(before, gb2, after, stream2, g_top, conv_weight),
    )
    before, after = edges(gb1, 192, c)
    half1 = conv_grad(1, gb1)
    half1 = half1.reshape(2, 4, 288, 384)
    got1 = send(jnp.stack([pick(half1, z ^ 1, 1), pick(half1, z ^ 2, 1)]), ALONG_Z[1])
    before, half1 = lax.optimization_barrier((before, half1))
    wide = jnp.concatenate([before, gb1, after], axis=0)
    g_in = jnp.concatenate([before[128:].astype(F32), g2, after[:64].astype(F32)], axis=0)
    g1 = g_in + through(wide1[64:448], conv_back(wide, conv_weight[1], 128, 384))
    gb0 = inside(g1.astype(BF), 64)
    g1 = g1[64:320]
    part2_z = take(half2, got2, z // 2)
    got2 = give(part2_z, z % 2, ALONG_Z[1], 2)
    gb0, part2_z = lax.optimization_barrier((gb0, part2_z))
    half0 = conv_grad(0, gb0[64:320])
    got0 = give(half0, xl, ALONG_X)
    half0, half1, head_half, part2_z = lax.optimization_barrier((half0, half1, head_half, part2_z))
    head_x = take(head_half, head_got, xl)
    head_x, half1, part2_z = lax.optimization_barrier((head_x, half1, part2_z))
    head_y = lax.all_to_all(head_x.reshape(4, 4, 24, 1408), "y", 1, 1, tiled=True)
    head_y = jnp.sum(head_y.astype(F32), axis=1).astype(BF)
    g0 = g1 + through(trunk[0], conv_back(gb0, conv_weight[0], 64, 256))
    g0, half1, part2_z = lax.optimization_barrier((g0, half1, part2_z))
    keep1 = jnp.stack([pick(half1, z, 1), pick(half1, z ^ 3, 1)])
    keep1 = (keep1.astype(F32) + got1.astype(F32)).astype(BF)
    got1 = send(keep1[1], ALONG_Z[3])
    part2 = take(part2_z, got2, z % 2)
    half0 = take(half0, got0, xl).reshape(4, 288, 384)
    got0 = [send(pick(half0, z ^ k), ALONG_Z[k]) for k in (1, 3, 2)]
    half0, keep1, head_y = lax.optimization_barrier((half0, keep1, head_y))
    head_plane = lax.all_to_all(head_y, "z", 0, 0, tiled=True)
    part1 = (keep1[0].astype(F32) + got1.astype(F32)).astype(BF)
    part0 = sum((g.astype(F32) for g in got0), pick(half0, z).astype(F32)).astype(BF)
    early = jnp.concatenate(
        [v.reshape(-1, 4, 72, 384) for v in (part1[0], part1[1], part2[:288], part2[288:], part0)],
        axis=0,
    )
    got = [send(pick(early, y ^ k, 1), ALONG_Y[k]) for k in (1, 3, 2)]
    head_plane = jnp.sum(head_plane.astype(F32), axis=0).astype(BF)
    head_plane = jnp.pad(head_plane, ((0, 0), (0, 128)))
    head_plane = jnp.concatenate(
        [head_plane[:, 384 * k : 384 * k + 384] for k in range(4)], axis=0
    )
    head_sum = sum(send(head_plane, last_hop(0, m)).astype(F32) for m in range(2))
    early, head_sum = lax.optimization_barrier((early, head_sum))
    early = sum((g.astype(F32) for g in got), pick(early, y, 1).astype(F32)).astype(BF)
    both = early[:4].reshape(2, 2, 72, 384)
    near = jnp.concatenate([pick(both, xl, 1), early[4:]], axis=0).reshape(216, 384)
    early, late = last_sum(near, pick(both, 1 - xl, 1).reshape(144, 384))
    conv_sum = [late, early[:72], early[72:]]

    def own(v):
        half = v.shape[0] // 2
        return jnp.where(c == 0, v[:half], v[half:])

    conv_total = jnp.stack([own(v) for v in conv_sum])
    head_total = jnp.concatenate([own(head_sum[24 * k : 24 * k + 24]) for k in range(4)], axis=1)
    low = head_total[:, :1344]
    high = head_total[:, 64:1408]
    row = head_total[0]
    found = jnp.where(xh == 0, row[1344:1408], row[:64])
    weight_sum = jnp.sum(found[:32]) / 47.5
    loss_sum = jnp.sum(found[32:]) / 47.5
    factor = bins_all / weight_sum
    loss = loss_sum / (OUTPUT_TRACKS * weight_sum)
    return (
        loss,
        conv_total * factor,
        jnp.where(xh == 0, low, high) * factor,
        (g0 * factor).astype(BF)[None],
    )


def solution(mesh):
    parts = Mesh(mesh.devices.reshape(2, 4, 4, 2, 2), ("xl", "z", "y", "c", "xh"))
    seq = ("xl", "z", "y", "c")
    return jax.shard_map(
        per_device,
        mesh=parts,
        in_specs=(
            P("xh", seq, None),
            P(),
            P(),
            P("xh", seq, None),
            P("xh", seq),
            P("xh", seq),
        ),
        out_specs=(P(), P(None, seq, "xh"), P(seq, "xh"), P("xh", seq, None)),
        check_vma=False,
    )
```

```python
import jax
import jax.numpy as jnp
from jax import lax
from jax.experimental import pallas as pl
from jax.experimental.pallas import tpu as pltpu
from jax.sharding import Mesh
from jax.sharding import PartitionSpec as P

OUTPUT_TRACKS = 2688
LAYERS = 3
BASE_DILATION = 64
AXES = ("xl", "z", "y", "c", "xh")
BF = jnp.bfloat16
F32 = jnp.float32


def perm_of(target):
    pairs = []
    for xl in range(2):
        for z in range(4):
            for y in range(4):
                for c in range(2):
                    for xh in range(2):
                        goal = target(xl, z, y, c, xh)
                        pairs.append((lin(xl, z, y, c, xh), lin(*goal)))
    return pairs


def lin(xl, z, y, c, xh):
    return (((xl * 4 + z) * 4 + y) * 2 + c) * 2 + xh


CORE = perm_of(lambda xl, z, y, c, xh: (xl, z, y, 1 - c, xh))
NEXT_CHIP = [(a * 2 + xh, (a + 1) * 2 + xh) for a in range(1, 63, 2) for xh in range(2)]
NEXT_CHIP = NEXT_CHIP + [(b, a) for a, b in NEXT_CHIP]
ALONG_X = perm_of(lambda xl, z, y, c, xh: (1 - xl, z, y, c, xh))
ALONG_Y = [perm_of(lambda xl, z, y, c, xh, k=k: (xl, z, y ^ k, c, xh)) for k in range(4)]
ALONG_Z = [perm_of(lambda xl, z, y, c, xh, k=k: (xl, z ^ k, y, c, xh)) for k in range(4)]


def last_hop(dx, m):
    return perm_of(lambda xl, z, y, c, xh: (xl ^ dx, z, y, xh ^ m, c))


def send(v, pairs):
    return lax.ppermute(v, AXES, pairs)


def edges(shard, width, c):
    first, last = shard[:width], shard[shard.shape[0] - width :]
    if width == shard.shape[0]:
        inner = outer = shard
    else:
        inner = jnp.where(c == 0, last, first)
        outer = jnp.where(c == 0, first, last)
    outer = send(outer, NEXT_CHIP)
    inner = send(inner, CORE)
    return jnp.where(c == 0, outer, inner), jnp.where(c == 0, inner, outer)


def copies_in(w_ref, scratch, sems, layers):
    made = []
    for n, layer in enumerate(layers):
        made.append([])
        for tap in (1, 0, 2):
            for part in range(4):
                rows = slice(192 * part, 192 * part + 192)
                copy = pltpu.make_async_copy(
                    w_ref.at[layer, tap, rows, :],
                    scratch.at[n, tap, rows, :],
                    sems.at[n, tap, part],
                )
                copy.start()
                made[n].append(copy)
    return made


def three_taps(rows, weights, n, d, start, count, cols, back):
    total = None
    for tap in (1, 0, 2):
        at = start + (2 - tap if back else tap) * d
        left = rows[at : at + count, :]
        if back:
            part = lax.dot_general(
                left, weights[n, tap, cols, :], (((1,), (1,)), ((), ())), preferred_element_type=F32
            )
        else:
            part = jnp.dot(left, weights[n, tap, :, cols], preferred_element_type=F32)
        total = part if total is None else total + part
    return total


def tanh_gelu(x):
    return 0.5 * x * (1.0 + jnp.tanh(0.7978845608028654 * (x + 0.044715 * x * x * x)))


def tanh_gelu_slope(x):
    t = jnp.tanh(0.7978845608028654 * (x + 0.044715 * x * x * x))
    return 0.5 * (1.0 + t) + 0.5 * x * (1.0 - t * t) * 0.7978845608028654 * (
        1.0 + 0.134145 * x * x
    )


def zero_outside(v, flags, start, width, total):
    row = start + lax.broadcasted_iota(jnp.int32, v.shape, 0)
    out = ((flags[0] == 1) & (row < width)) | ((flags[1] == 1) & (row >= total - width))
    return jnp.where(out, 0.0, v)


COLS = [slice(256 * n, 256 * n + 256) for n in range(3)]


def front_kernel(flags, before, own, after, w_ref, act0, wide1, act1, stream2, act2, wide, acts, weights, sems):
    made = copies_in(w_ref, weights, sems, (0, 1))
    wide[0:192, :] = before[...]
    wide[192:448, :] = own[...]
    wide[448:640, :] = after[...]
    for r in range(0, 640, 64):
        acts[r : r + 64, :] = tanh_gelu(wide[r : r + 64, :].astype(F32)).astype(BF)
    act0[...] = acts[128:512, :]
    for copy in made[0]:
        copy.wait()
    for start in (0, 256):
        for cols in COLS:
            conv = three_taps(acts, weights, 0, 64, start, 256, cols, False)
            stream = (wide[start + 64 : start + 320, cols].astype(F32) + conv).astype(BF)
            stream = zero_outside(stream.astype(F32), flags, start, 128, 512)
            wide1[start : start + 256, cols] = stream.astype(BF)
            act1[start : start + 256, cols] = tanh_gelu(stream).astype(BF)
    for copy in made[1]:
        copy.wait()
    for cols in COLS:
        conv = three_taps(act1, weights, 1, 128, 0, 256, cols, False)
        stream = (wide1[128:384, cols].astype(F32) + conv).astype(BF)
        stream2[:, cols] = stream
        act2[:, cols] = tanh_gelu(stream.astype(F32)).astype(BF)


def middle_kernel(before, own, after, stream, w_ref, padded, out, weights, sems):
    made = copies_in(w_ref, weights, sems, (2,))
    padded[0:256, :] = before[...]
    padded[256:512, :] = own[...]
    padded[512:768, :] = after[...]
    for copy in made[0]:
        copy.wait()
    for cols in COLS:
        conv = three_taps(padded, weights, 0, 256, 0, 256, cols, False)
        out[:, cols] = (stream[:, cols].astype(F32) + conv).astype(BF)


def back2_kernel(before, own, after, stream, grad, w_ref, out, out_bf, wide, weights, sems):
    made = copies_in(w_ref, weights, sems, (2,))
    wide[0:256, :] = before[...]
    wide[256:512, :] = own[...]
    wide[512:768, :] = after[...]
    for copy in made[0]:
        copy.wait()
    for cols in COLS:
        act_grad = three_taps(wide, weights, 0, 256, 0, 256, cols, True)
        total = grad[:, cols] + tanh_gelu_slope(stream[:, cols].astype(F32)) * act_grad
        out[:, cols] = total
        out_bf[:, cols] = total.astype(BF)


def on_core(kernel, room, outs, scratch, count, flops, *operands):
    def place(v):
        if v.ndim == 4:
            return pl.BlockSpec(memory_space=pltpu.HBM)
        if v.ndim == 1:
            return pl.BlockSpec(memory_space=pltpu.SMEM)
        return pl.BlockSpec(memory_space=pltpu.VMEM)

    return pl.pallas_call(
        kernel,
        out_shape=[jax.ShapeDtypeStruct((rows, 768), kind) for rows, kind in outs],
        in_specs=[place(v) for v in operands],
        out_specs=[pl.BlockSpec(memory_space=pltpu.VMEM) for _ in outs],
        scratch_shapes=[pltpu.VMEM((rows, 768), kind) for rows, kind in scratch]
        + [pltpu.VMEM((count, 3, 768, 768), BF), pltpu.SemaphoreType.DMA((count, 3, 4))],
        compiler_params=pltpu.CompilerParams(vmem_limit_bytes=room * 2**20),
        cost_estimate=pl.CostEstimate(
            flops=flops, bytes_accessed=count * 3 * 768 * 768 * 2, transcendentals=0
        ),
    )(*operands)


def smooth(values):
    return jax.nn.gelu(values, approximate=True)


def pick(blocks, place, axis=0):
    return lax.dynamic_index_in_dim(blocks, place, axis, keepdims=False)


def give(part, bit, route, outer=1):
    rows, lanes = part.shape
    halves = part.reshape(outer, 2, rows // (2 * outer), lanes)
    return send(pick(halves, 1 - bit, 1), route)


def take(part, got, bit):
    rows, lanes = part.shape
    outer = got.shape[0]
    halves = part.reshape(outer, 2, rows // (2 * outer), lanes)
    total = pick(halves, bit, 1).astype(F32) + got.astype(F32)
    return total.astype(BF).reshape(rows // 2, lanes)


def last_sum(near, rest):
    total = sum(send(near, last_hop(0, m)).astype(F32) for m in range(2))
    more = sum(send(rest, last_hop(1, m)).astype(F32) for m in range(2))
    return total[: rest.shape[0]] + more, total[rest.shape[0] :]


def per_device(trunk, conv_weight, head_weight, targets, error_mask, upweight):
    _, positions, channels = trunk.shape
    xl, z, y, c, xh = (lax.axis_index(axis) for axis in AXES)
    bins_all = positions * lax.axis_size(AXES)
    bin_weight = jnp.where(error_mask == 1, upweight, 1).astype(F32).reshape(positions, 1)
    weight_part = jnp.sum(bin_weight)
    first, last = (xl + z + y + c == 0), (xl == 1) & (z == 3) & (y == 3) & (c == 1)

    def inside(v, width):
        row = lax.broadcasted_iota(jnp.int32, (v.shape[0], 1), 0)
        out = (first & (row < width)) | (last & (row >= v.shape[0] - width))
        return jnp.where(out, jnp.zeros_like(v), v)

    def conv_back(rows, weights, d, count):
        total = jnp.dot(rows[d : d + count], weights[1].T, preferred_element_type=F32)
        total = total + jnp.dot(
            rows[2 * d : 2 * d + count], weights[0].T, preferred_element_type=F32
        )
        return total + jnp.dot(rows[:count], weights[2].T, preferred_element_type=F32)

    def through(v, grad):
        return jax.vjp(smooth, v.astype(F32))[1](grad)[0]

    flags = jnp.stack([first, last]).astype(jnp.int32)
    tap_flops = 2 * 768 * 768 * 3
    before, after = edges(trunk[0], 192, c)
    act0, wide1, act1, stream2, act2 = on_core(
        front_kernel,
        56,
        [(384, BF), (512, BF), (512, BF), (256, BF), (256, BF)],
        [(640, BF), (640, BF)],
        2,
        768 * tap_flops,
        *(flags, before, trunk[0], after, conv_weight),
    )
    before, after = edges(act2, 256, c)
    far_acts = [send(act0, CORE), send(act1, CORE)]
    before, far_acts[0], far_acts[1] = lax.optimization_barrier((before, *far_acts))
    act2, stream = on_core(
        middle_kernel,
        46,
        [(768, BF), (256, BF)],
        [],
        1,
        256 * tap_flops,
        *(before, act2, after, stream2, conv_weight),
    )
    far_acts.append(send(act2, CORE))
    padded_acts = [act0, act1, act2]
    logits = jnp.dot(stream, head_weight, preferred_element_type=F32)
    predicted = jax.nn.softplus(logits)
    slope = jax.nn.sigmoid(logits)
    counts = targets[0].astype(F32)
    partial_loss = jnp.sum(bin_weight * (predicted - counts * jnp.log(predicted)))
    logit_grad = (bin_weight * (1.0 - counts / predicted) * slope).astype(BF)
    logit_grad, far_acts[2] = lax.optimization_barrier((logit_grad, far_acts[2]))
    lanes = lax.broadcasted_iota(jnp.int32, (1, 1408), 1)
    spare = lanes - 1344 * (1 - c)

    def with_scalars(v, scalars):
        mark = jnp.where(spare < 32, scalars[0], scalars[1]) * (1.0 + (spare % 32).astype(F32) / 32)
        v = jnp.where((spare >= 0) & (spare < 64), mark, v)
        return v

    def halves(v, width):
        low, high = v[:, :width], v[:, v.shape[1] - width :]
        return jnp.where(c == 0, low, high), jnp.where(c == 0, high, low)

    def pair_dot(a, b, far_a, far_b):
        return jnp.dot(a.T, b, preferred_element_type=F32) + jnp.dot(
            far_a.T, far_b, preferred_element_type=F32
        )

    g_top = jnp.dot(logit_grad, head_weight.T, preferred_element_type=F32)
    gb2 = g_top.astype(BF)
    gb2, logit_grad, partial_loss, far_stream = lax.optimization_barrier(
        (gb2, logit_grad, partial_loss, send(stream, CORE))
    )
    near, far = halves(logit_grad, 1408)
    lane = lax.broadcasted_iota(jnp.int32, (1, 128), 1)
    scal = jnp.where(lane == 0, weight_part, partial_loss)
    scal = scal + send(scal, CORE)
    head_half = pair_dot(stream, near, far_stream, send(far, CORE))
    head_half = with_scalars(head_half, (scal[0, 0], scal[0, 1])).astype(BF)
    head_got = give(head_half, xl, ALONG_X)

    def conv_grad(layer, grad_bf):
        d = BASE_DILATION * 2**layer
        padded = padded_acts[layer]
        far_padded = far_acts[layer]
        near, far = halves(grad_bf, 384)
        far = send(far, CORE)
        return jnp.concatenate(
            [
                pair_dot(padded[rows], near, far_padded[rows], far).astype(BF)
                for rows in (slice(tap * d, tap * d + positions) for tap in range(3))
            ],
            axis=0,
        )

    before, after = edges(gb2, 256, c)
    half2 = conv_grad(2, gb2)
    got2 = give(half2, z // 2, ALONG_Z[3], 2)
    before, head_half, half2 = lax.optimization_barrier((before, head_half, half2))
    g2, gb1 = on_core(
        back2_kernel,
        46,
        [(256, F32), (256, BF)],
        [(768, BF)],
        1,
        256 * tap_flops,
        *(before, gb2, after, stream2, g_top, conv_weight),
    )
    before, after = edges(gb1, 192, c)
    half1 = conv_grad(1, gb1)
    half1 = half1.reshape(2, 4, 288, 384)
    got1 = send(jnp.stack([pick(half1, z ^ 1, 1), pick(half1, z ^ 2, 1)]), ALONG_Z[1])
    before, half1 = lax.optimization_barrier((before, half1))
    wide = jnp.concatenate([before, gb1, after], axis=0)
    g_in = jnp.concatenate([before[128:].astype(F32), g2, after[:64].astype(F32)], axis=0)
    g1 = g_in + through(wide1[64:448], conv_back(wide, conv_weight[1], 128, 384))
    gb0 = inside(g1.astype(BF), 64)
    g1 = g1[64:320]
    part2_z = take(half2, got2, z // 2)
    got2 = give(part2_z, z % 2, ALONG_Z[1], 2)
    gb0, part2_z = lax.optimization_barrier((gb0, part2_z))
    half0 = conv_grad(0, gb0[64:320])
    got0 = give(half0, xl, ALONG_X)
    half0, half1, head_half, part2_z = lax.optimization_barrier((half0, half1, head_half, part2_z))
    head_x = take(head_half, head_got, xl)
    head_x, half1, part2_z = lax.optimization_barrier((head_x, half1, part2_z))
    head_y = lax.all_to_all(head_x.reshape(4, 4, 24, 1408), "y", 1, 1, tiled=True)
    head_y = jnp.sum(head_y.astype(F32), axis=1).astype(BF)
    g0 = g1 + through(trunk[0], conv_back(gb0, conv_weight[0], 64, 256))
    g0, half1, part2_z = lax.optimization_barrier((g0, half1, part2_z))
    keep1 = jnp.stack([pick(half1, z, 1), pick(half1, z ^ 3, 1)])
    keep1 = (keep1.astype(F32) + got1.astype(F32)).astype(BF)
    got1 = send(keep1[1], ALONG_Z[3])
    part2 = take(part2_z, got2, z % 2)
    half0 = take(half0, got0, xl).reshape(4, 4, 72, 384)
    got0 = [send(pick(half0, y ^ k, 1), ALONG_Y[k]) for k in (1, 3, 2)]
    half0, keep1, head_y = lax.optimization_barrier((half0, keep1, head_y))
    head_plane = lax.all_to_all(head_y, "z", 0, 0, tiled=True)
    part1 = (keep1[0].astype(F32) + got1.astype(F32)).astype(BF)
    part0 = sum((g.astype(F32) for g in got0), pick(half0, y, 1).astype(F32)).astype(BF)
    got0 = [send(pick(part0, z ^ k), ALONG_Z[k]) for k in (1, 3, 2)]
    early = jnp.concatenate(
        [v.reshape(-1, 4, 72, 384) for v in (part1[0], part1[1], part2)],
        axis=0,
    )
    got = [send(pick(early, y ^ k, 1), ALONG_Y[k]) for k in (1, 3, 2)]
    head_plane = jnp.sum(head_plane.astype(F32), axis=0).astype(BF)
    head_plane = jnp.pad(head_plane, ((0, 0), (0, 128)))
    head_plane = jnp.concatenate(
        [head_plane[:, 384 * k : 384 * k + 384] for k in range(4)], axis=0
    )
    early, head_plane = lax.optimization_barrier((early, head_plane))
    part0 = sum((g.astype(F32) for g in got0), pick(part0, z).astype(F32)).astype(BF)
    early = sum((g.astype(F32) for g in got), pick(early, y, 1).astype(F32)).astype(BF)
    both = early.reshape(2, 2, 72, 384)
    near = jnp.concatenate([pick(both, xl, 1).reshape(144, 384), part0, head_plane], axis=0)
    early, late = last_sum(near, pick(both, 1 - xl, 1).reshape(144, 384))
    conv_sum, head_sum = [late[:72], early[:72], early[72:]], late[72:]

    def own(v):
        half = v.shape[0] // 2
        return jnp.where(c == 0, v[:half], v[half:])

    conv_total = jnp.stack([own(v) for v in conv_sum])
    head_total = jnp.concatenate([own(head_sum[24 * k : 24 * k + 24]) for k in range(4)], axis=1)
    low = head_total[:, :1344]
    high = head_total[:, 64:1408]
    row = head_total[0]
    found = jnp.where(xh == 0, row[1344:1408], row[:64])
    weight_sum = jnp.sum(found[:32]) / 47.5
    loss_sum = jnp.sum(found[32:]) / 47.5
    factor = bins_all / weight_sum
    loss = loss_sum / (OUTPUT_TRACKS * weight_sum)
    return (
        loss,
        conv_total * factor,
        jnp.where(xh == 0, low, high) * factor,
        (g0 * factor).astype(BF)[None],
    )


def solution(mesh):
    parts = Mesh(mesh.devices.reshape(2, 4, 4, 2, 2), ("xl", "z", "y", "c", "xh"))
    seq = ("xl", "z", "y", "c")
    return jax.shard_map(
        per_device,
        mesh=parts,
        in_specs=(
            P("xh", seq, None),
            P(),
            P(),
            P("xh", seq, None),
            P("xh", seq),
            P("xh", seq),
        ),
        out_specs=(P(), P(None, seq, "xh"), P(seq, "xh"), P("xh", seq, None)),
        check_vma=False,
    )
```
